512 devices in a mesh: seq: 128 (over x, z, core), head: 4 (over y).
Axes of the slice: x: 4, y: 4, z: 16, core: 2. Of those that a mesh axis runs over, the one named last changes fastest.
Arguments:
- queries: bfloat16 [16384, 2048], P('seq', 'head'), may hold values from -8 to 8
- keys: bfloat16 [16384, 2048], P('seq', 'head'), may hold values from -6 to 6
- values: bfloat16 [16384, 2048], P('seq', 'head'), may hold values from -18 to 18
- out_grad: bfloat16 [16384, 2048], P('seq', 'head'), may hold values from -6 to 6
- level_choice: int32 [128, 4], P('seq'), may hold values from 1 to 2
- frame_lengths: int32 [64], replicated, may hold values from 1 to 512, 16384 in all
Outputs:
- attended: bfloat16 [16384, 2048], P('seq', 'head')
- query_grad: bfloat16 [16384, 2048], P('seq', 'head')
- key_grad: bfloat16 [16384, 2048], P('seq', 'head')
- value_grad: bfloat16 [16384, 2048], P('seq', 'head')
The draws below stay inside these ranges and needn't reach their ends.
Inputs may be any that keep to these rules, and one draw needn't show every extreme that they name: `frame_lengths`: the lengths sum to 16384.
All inputs are finite; a program needn't handle non-finite values.
Results may differ from the reference program's by a relative error of at most 0.025.
Values may be sent and summed in bfloat16 or wider, within the bound.
A program may use at most 64 MiB of HBM per device.

```python
import math
import jax
import jax.numpy as jnp
import numpy as np
from jax import lax

HEADS = 16
HEAD_DIM = 128
TOK_DEV = 128
POOL1 = 4
POOL2 = 16
REACH1 = 3
REACH2 = 11
BLOCKS = 128
TOKENS = 16384
FRAMES = 64
FRAME_MOST = 512


def draw_queries(key, part):
    key = jax.random.fold_in(key, 1)
    return jnp.clip(2.0 * jax.random.normal(key, (TOKENS, HEADS * HEAD_DIM)), -8.0, 8.0).astype(jnp.bfloat16)


def draw_keys(key, part):
    key = jax.random.fold_in(key, 2)
    return jnp.clip(jax.random.normal(key, (TOKENS, HEADS * HEAD_DIM)), -6.0, 6.0).astype(jnp.bfloat16)


def draw_values(key, part):
    key = jax.random.fold_in(key, 3)
    ramp = jnp.arange(HEADS * HEAD_DIM, dtype=jnp.float32) / (HEADS * HEAD_DIM - 1)
    scale = jnp.exp(ramp * math.log(3.0))
    return jnp.clip(jax.random.normal(key, (TOKENS, HEADS * HEAD_DIM)) * scale[None, :], -18.0, 18.0).astype(jnp.bfloat16)


def touch_ends(values, stream_key, low, high):
    shape = values.shape
    spot = [jax.random.randint(jax.random.fold_in(stream_key, axis), (), 0, shape[axis]) for axis in range(len(shape))]
    values = values.at[tuple(spot)].set(low)
    longest = shape.index(max(shape))
    spot[longest] = (spot[longest] + 1) % shape[longest]
    return values.at[tuple(spot)].set(high)


def levels(key, extent, pieces, smallest, high):
    gain, own = 1.0, jax.random.fold_in(key, 6)
    for position, blocks in pieces:
        draws = jnp.exp(jax.random.uniform(jax.random.fold_in(own, position), (blocks,), jnp.float32, smallest / len(pieces), high / len(pieces)))
        gain = gain * jnp.repeat(draws, extent[position] // blocks).reshape([-1 if axis == position else 1 for axis in range(len(extent))])
    return gain


def split_up(amount, total, bound, slope):
    loads = [(1 << 20) // math.isqrt(rank ** slope) + 1 for rank in range(2, amount + 1)]
    surplus, holding = total - bound - (amount - 1), [1] * (amount - 1)
    while surplus > 0:
        movable = [i for i in range(amount - 1) if holding[i] < bound]
        pool, left = sum([loads[i] for i in movable]), surplus
        for i in movable:
            more = min(bound - holding[i], max(1, left * loads[i] // pool), surplus)
            holding[i] = holding[i] + more
            surplus = surplus - more
    return np.array([bound] + holding)


def uneven(own_key, count, total, reach, lean):
    if count == 2:
        one = jax.random.randint(own_key, (), max(1, total - reach), min(reach, total - 1) + 1)
        return jnp.stack([one, total - one])
    sizes = jnp.asarray(split_up(count, total, reach, lean), jnp.int32)
    pairs = (count - 1) // 2
    donor, sink = sizes[1:1 + 2 * pairs:2], sizes[2:2 + 2 * pairs:2]
    margin = jnp.minimum(donor - 1, reach - sink)
    shifted = jax.random.randint(jax.random.fold_in(own_key, 1), (pairs,), 0, 1 << 20) % (margin + 1)
    sizes = sizes.at[1:1 + 2 * pairs:2].set(donor - shifted).at[2:2 + 2 * pairs:2].set(sink + shifted)
    return sizes[jax.random.permutation(jax.random.fold_in(own_key, 2), count)]


def scatter_about(rng, dims, spread, reach, pieces=(), kind=jnp.bfloat16):
    factor_of = levels(rng, dims, pieces, -0.22, 0.18) if pieces else 1.0
    result = jax.random.normal(rng, dims, jnp.float32) * spread * factor_of
    return jnp.minimum(jnp.maximum(result, -reach), reach).astype(kind)


def setup_inputs(seed: int = 0) -> dict:
    streams_of = jax.random.split(jax.random.key(seed), 7)
    queries = draw_queries(jax.random.fold_in(streams_of[6], 71), 0)
    keys = draw_keys(jax.random.fold_in(streams_of[6], 71), 0)
    values = draw_values(jax.random.fold_in(streams_of[6], 71), 0)
    out_grad = scatter_about(streams_of[3], (TOKENS, HEADS * HEAD_DIM), 1.0, 6.0, ((0, 128), (1, 4)))
    level_choice = touch_ends(jax.random.randint(streams_of[4], (BLOCKS, 2 * (REACH1 - 1)), 1, 3), jax.random.fold_in(streams_of[4], 1), 1, 2).astype(jnp.int32)
    frame_lengths = uneven(streams_of[5], FRAMES, TOKENS, FRAME_MOST, 2).astype(jnp.int32)
    return {"queries": queries, "keys": keys, "values": values, "out_grad": out_grad, "level_choice": level_choice, "frame_lengths": frame_lengths}


MATCHED_FRAME_ADD = 1.0
NORM_EPSILON = 1e-06

def pool_rows(pair, factor):
    count = pair.shape[1] // factor
    grouped = pair.astype(jnp.float32).reshape(pair.shape[0], count, factor, pair.shape[2])
    return lax.optimization_barrier(jnp.mean(grouped, axis=2)).astype(jnp.bfloat16)

def spread_rows(total, factor):
    shape = (total.shape[0], total.shape[1], factor, total.shape[2])
    return jnp.broadcast_to(total[:, :, None, :] / factor, shape).reshape(total.shape[0], -1, total.shape[2])

def frames_at(positions, frame_lengths):
    ends = jnp.cumsum(frame_lengths, dtype=jnp.int32)
    return lax.optimization_barrier(jnp.sum((positions[:, None] >= ends[None, :]).astype(jnp.int32), axis=1, dtype=jnp.int32))

def frame_bias(query_frame_index, key_frame_index, valid):
    matched_frame = (query_frame_index[:, None] == key_frame_index[None, :]).astype(jnp.float32) * MATCHED_FRAME_ADD
    return jnp.where(valid, matched_frame, -jnp.inf)

def by_heads(array, heads):
    return array.reshape(array.shape[0], heads, -1).transpose(1, 0, 2)

def from_heads(array):
    return array.transpose(1, 0, 2).reshape(array.shape[1], -1)

def scores_of(query, key_rows, bias):
    return jnp.dot(query, key_rows.T, preferred_element_type=jnp.float32) * (1.0 / math.sqrt(query.shape[1])) + bias

def head_forward_pass(query, key_rows, value_rows, bias):
    scores = scores_of(query, key_rows, bias)
    highest = lax.optimization_barrier(jnp.max(scores, axis=1, keepdims=True))
    logsum = highest + jnp.log(lax.optimization_barrier(jnp.sum(jnp.exp(scores - highest), axis=1, keepdims=True)))
    rounded = jnp.exp(scores - logsum).astype(jnp.bfloat16)
    return (jnp.dot(rounded, value_rows, preferred_element_type=jnp.float32), logsum[:, 0])

def head_backward(query, mixed_grad, key_rows, value_rows, bias, logsum, delta):
    scale = 1.0 / math.sqrt(query.shape[1])
    weights = jnp.exp(scores_of(query, key_rows, bias) - logsum[:, None])
    rounded = weights.astype(jnp.bfloat16)
    slopes = (weights * (jnp.dot(mixed_grad, value_rows.T, preferred_element_type=jnp.float32) - delta[:, None])).astype(jnp.bfloat16)
    query_grad = (jnp.dot(slopes, key_rows, preferred_element_type=jnp.float32) * scale).astype(jnp.bfloat16)
    key_grad = jnp.dot(slopes.T, query, preferred_element_type=jnp.float32) * scale
    value_grad = jnp.dot(rounded.T, mixed_grad, preferred_element_type=jnp.float32)
    return (query_grad, key_grad, value_grad)

def reference(queries, keys, values, out_grad, level_choice, frame_lengths):
    rows = TOK_DEV
    width = HEADS * HEAD_DIM
    first_rows = rows // POOL1
    second_rows = rows // POOL2
    offsets_one = [offset for offset in range(-REACH1, REACH1 + 1) if abs(offset) >= 2]
    offsets_two = [offset for offset in range(-REACH2, REACH2 + 1) if abs(offset) >= 2]
    count_one = len(offsets_one)
    count_two = len(offsets_two)
    wide_one = 2 * REACH1 + 1
    wide_two = 2 * REACH2 + 1
    picks_one = np.array([offset + REACH1 for offset in offsets_one])
    picks_two = np.array([offset + REACH2 for offset in offsets_two])
    columns = np.array([offsets_one.index(offset) if abs(offset) <= REACH1 else 0 for offset in offsets_two])
    beyond = np.array([abs(offset) > REACH1 for offset in offsets_two])
    frames = frames_at(jnp.arange(TOKENS, dtype=jnp.int32), frame_lengths)
    frames_padded = jnp.pad(frames, (rows, rows), constant_values=-1)
    pair = jnp.stack([keys, values])
    first = pool_rows(pair, POOL1)
    second = pool_rows(pair, POOL2)
    padded_pairs = jnp.pad(pair, ((0, 0), (rows, rows), (0, 0)))
    first_padded = jnp.pad(first, ((0, 0), (REACH1 * first_rows, REACH1 * first_rows), (0, 0)))
    second_padded = jnp.pad(second, ((0, 0), (REACH2 * second_rows, REACH2 * second_rows), (0, 0)))

    def one_block(carry, block):
        near_sum, first_sum, second_sum = carry
        start = block * rows
        query = lax.dynamic_slice_in_dim(queries, start, rows, 0)
        incoming = lax.dynamic_slice_in_dim(out_grad, start, rows, 0)
        near = lax.dynamic_slice_in_dim(padded_pairs, start, 3 * rows, 1)
        window_one = lax.dynamic_slice_in_dim(first_padded, block * first_rows, wide_one * first_rows, 1)
        window_two = lax.dynamic_slice_in_dim(second_padded, block * second_rows, wide_two * second_rows, 1)
        far_one = window_one.reshape(2, wide_one, first_rows, width)[:, picks_one].reshape(2, -1, width)
        far_two = window_two.reshape(2, wide_two, second_rows, width)[:, picks_two].reshape(2, -1, width)
        own_frame = lax.dynamic_slice_in_dim(frames, start, rows, 0)
        key_frames = lax.dynamic_slice_in_dim(frames_padded, start, 3 * rows, 0)
        table = lax.dynamic_index_in_dim(level_choice, block, 0, keepdims=False)
        blocks_one = block + jnp.array(offsets_one, dtype=jnp.int32)
        usable_one = (blocks_one >= 0) & (blocks_one < BLOCKS) & (table == 1)
        blocks_two = block + jnp.array(offsets_two, dtype=jnp.int32)
        usable_two = (blocks_two >= 0) & (blocks_two < BLOCKS) & (beyond | (table[columns] == 2))
        far_row = jnp.concatenate([jnp.repeat(jnp.where(usable_one, math.log(POOL1), -jnp.inf).astype(jnp.float32), first_rows), jnp.repeat(jnp.where(usable_two, math.log(POOL2), -jnp.inf).astype(jnp.float32), second_rows)])
        bias = jnp.concatenate([frame_bias(own_frame, key_frames[rows:2 * rows], True), jnp.broadcast_to(far_row[None, :], (rows, far_row.shape[0])), frame_bias(own_frame, key_frames[:rows], block > 0), frame_bias(own_frame, key_frames[2 * rows:], block < BLOCKS - 1)], axis=1)
        gathered = jnp.concatenate([near[:, rows:2 * rows], far_one, far_two, near[:, :rows], near[:, 2 * rows:]], axis=1)
        total = gathered.shape[1]
        tail = total - 2 * rows
        query_heads = by_heads(query, HEADS)
        key_heads = by_heads(gathered[0], HEADS)
        value_heads = by_heads(gathered[1], HEADS)

        def forward_head(items):
            return head_forward_pass(items[0], items[1], items[2], bias)
        mixed_heads, logsum = lax.map(forward_head, (query_heads, key_heads, value_heads))
        mixed = from_heads(mixed_heads)
        energy = lax.optimization_barrier(jnp.sum(mixed * mixed, axis=1))
        inverse = lax.rsqrt(energy / (HEADS * HEAD_DIM) + NORM_EPSILON)[:, None]
        normed = mixed * inverse
        attended = normed.astype(jnp.bfloat16)
        agreement = lax.optimization_barrier(jnp.sum(incoming.astype(jnp.float32) * normed, axis=1))
        mixed_grad = (inverse * (incoming.astype(jnp.float32) - normed * (agreement[:, None] / (HEADS * HEAD_DIM)))).astype(jnp.bfloat16)
        delta = lax.optimization_barrier(jnp.sum((mixed_grad.astype(jnp.float32) * mixed).reshape(rows, HEADS, HEAD_DIM), axis=2)).T

        def backward_head(items):
            return head_backward(items[0], items[1], items[2], items[3], bias, items[4], items[5])
        query_grad_heads, key_set, value_set = lax.map(backward_head, (query_heads, by_heads(mixed_grad, HEADS), key_heads, value_heads, logsum, delta))
        set_grads = jnp.stack([from_heads(key_set), from_heads(value_set)])
        near_grads = jnp.concatenate([set_grads[:, tail:tail + rows], set_grads[:, :rows], set_grads[:, tail + rows:]], axis=1)
        near_sum = lax.dynamic_update_slice_in_dim(near_sum, lax.dynamic_slice_in_dim(near_sum, start, 3 * rows, 1) + near_grads, start, 1)
        split_one = rows + count_one * first_rows
        grads_one = set_grads[:, rows:split_one].reshape(2, count_one, first_rows, width)
        grads_two = set_grads[:, split_one:tail].reshape(2, count_two, second_rows, width)
        full_one = jnp.zeros((2, wide_one, first_rows, width), jnp.float32).at[:, picks_one].set(grads_one).reshape(2, -1, width)
        full_two = jnp.zeros((2, wide_two, second_rows, width), jnp.float32).at[:, picks_two].set(grads_two).reshape(2, -1, width)
        start_one = block * first_rows
        start_two = block * second_rows
        first_sum = lax.dynamic_update_slice_in_dim(first_sum, lax.dynamic_slice_in_dim(first_sum, start_one, wide_one * first_rows, 1) + full_one, start_one, 1)
        second_sum = lax.dynamic_update_slice_in_dim(second_sum, lax.dynamic_slice_in_dim(second_sum, start_two, wide_two * second_rows, 1) + full_two, start_two, 1)
        return ((near_sum, first_sum, second_sum), (attended, from_heads(query_grad_heads)))
    initial = (jnp.zeros(padded_pairs.shape, jnp.float32), jnp.zeros(first_padded.shape, jnp.float32), jnp.zeros(second_padded.shape, jnp.float32))
    sums, output_rows = lax.scan(one_block, initial, jnp.arange(BLOCKS, dtype=jnp.int32))
    near_sum, first_sum, second_sum = sums
    attended, query_grad = output_rows
    lead_one = REACH1 * first_rows
    lead_two = REACH2 * second_rows
    token_grad = near_sum[:, rows:rows + TOKENS] + spread_rows(first_sum[:, lead_one:lead_one + TOKENS // POOL1], POOL1) + spread_rows(second_sum[:, lead_two:lead_two + TOKENS // POOL2], POOL2)
    token_grad = token_grad.astype(jnp.bfloat16)
    return (attended.reshape(TOKENS, width), query_grad.reshape(TOKENS, width), token_grad[0], token_grad[1])
```

```python
import math

import jax
import jax.numpy as jnp
from jax import lax
from jax.experimental import pallas as pl
from jax.experimental.pallas import tpu as pltpu
from jax.sharding import PartitionSpec as P

HEADS = 16
HEAD_DIM = 128
POOL1 = 4
POOL2 = 16
REACH1 = 3
REACH2 = 11
MATCHED_FRAME_ADD = 1.0
NORM_EPSILON = 1e-06

MESH = pl.DeviceIdType.MESH
F32 = jnp.float32
BF16 = jnp.bfloat16
LOG2E = math.log2(math.e)
MASKED = -1e30

ROWS = 128
HALF = 256
ONE = ROWS // POOL1
TWO = ROWS // POOL2
POOLED = 2 * (ONE + TWO)
NEAR = 3 * ROWS
FAR = 384

STEPS_ONE = (2, -1)


def direction(b):
    return 2 * b - 1


REL_ONE = [-2 * steps * direction(b) + b for b in (0, 1) for steps in STEPS_ONE] + [-1, 2]


def relative_two(side):
    sigma = direction(side)
    spots = [(2, 1 - side), (3, 1 - side), (3, side), (4, 1 - side), (4, side), (5, 1 - side), (5, side), (6, side)]
    return [-2 * k * sigma + b for k, b in spots]


REL_TWO = [relative_two(0), relative_two(1)]
REL_MIDDLE = REL_ONE + [REL_TWO[0][0], REL_TWO[1][0]]
REL_LAST = REL_TWO[0][1:] + REL_TWO[1][1:]
OWN, SIDE, MIDDLE, LAST = slice(0, 256), slice(256, 384), slice(384, 640), slice(640, 768)


def dot_nt(a, b):
    return lax.dot_general(a, b, (((1,), (1,)), ((), ())), preferred_element_type=F32)


def dot_tn(a, b):
    return lax.dot_general(a, b, (((0,), (0,)), ((), ())), preferred_element_type=F32)


def dot(a, b):
    return jnp.dot(a, b, preferred_element_type=F32)


def pool_matrix():
    r = lax.broadcasted_iota(jnp.int32, (ONE + TWO, ROWS), 0)
    t = lax.broadcasted_iota(jnp.int32, (ONE + TWO, ROWS), 1)
    one = jnp.where((t >> 2) == r, 1.0 / POOL1, 0.0)
    two = jnp.where((t >> 4) == r - ONE, 1.0 / POOL2, 0.0)
    return jnp.where(r < ONE, one, two).astype(BF16)


def spread_matrix():
    t = lax.broadcasted_iota(jnp.int32, (ROWS, ONE + TWO), 0)
    r = lax.broadcasted_iota(jnp.int32, (ROWS, ONE + TWO), 1)
    one = jnp.where((t >> 2) == r, 1.0 / POOL1, 0.0)
    two = jnp.where((t >> 4) == r - ONE, 1.0 / POOL2, 0.0)
    return jnp.where(r < ONE, one, two).astype(BF16)


def column_of(row):
    i = lax.broadcasted_iota(jnp.int32, (ROWS, ROWS), 0)
    j = lax.broadcasted_iota(jnp.int32, (ROWS, ROWS), 1)
    return jnp.sum(jnp.where(i == j, row, 0.0), axis=1, keepdims=True)


def row_of(column):
    i = lax.broadcasted_iota(jnp.int32, (ROWS, ROWS), 0)
    j = lax.broadcasted_iota(jnp.int32, (ROWS, ROWS), 1)
    return jnp.sum(jnp.where(i == j, column, 0.0), axis=0, keepdims=True)


def kernel(
    q_hbm, k_hbm, v_hbm, g_hbm, level_hbm, frame_hbm,
    att_hbm, dq_hbm, dk_hbm, dv_hbm,
    kv_own, q_two, g_two, kv_near, pooled, one_in, two_in, k_middle, v_middle, k_last, v_last,
    level_s, frame_v, near_bias, far_bias, weight, turned, mixed, stats,
    mixed_grad, att, dq, near_out, pool_out, two_out, sib_out, fold_out,
    pass_in, four_in, fold_in, near_back, one_back, two_back, sib_back, dk, dv,
    local_sem, send_sem, sib_recv, near_recv, one_recv, two_recv, stat_recv, pass_recv, fold_recv,
    back_near_recv, back_one_recv, back_two_recv, out_recv,
):
    blocks = lax.axis_size("seq")
    chips = blocks // 2
    heads = lax.axis_size("head")
    me = lax.axis_index("seq")
    lane = lax.axis_index("head")
    chip = me // 2
    core = me % 2
    other = 1 - core
    d = direction(core)

    def at(steps, c):
        return {"seq": ((chip + steps + chips) % chips) * 2 + c}

    sibling = {"seq": chip * 2 + other}

    def half(h):
        return pl.ds(pl.multiple_of(h * HALF, HALF), HALF)

    def remote(src, dst, send, recv, device):
        return pltpu.make_async_remote_copy(
            src_ref=src, dst_ref=dst, send_sem=send, recv_sem=recv, device_id=device, device_id_type=MESH
        )

    def inside(*steps, sided=()):
        away = [s for s in steps] + [s * d for s in sided]
        known = True
        for s in away:
            known = known & (chip + s >= 0) & (chip + s < chips)
        return (steps, sided), known

    def only(when, act):
        if when is None:
            act()
        else:
            pl.when(when[1])(act)

    sent = 0
    started = []

    def send(src, dst, recv, device, when=None):
        nonlocal sent
        copy = remote(src, dst, send_sem.at[sent], recv, device)
        sent += 1
        only(when, copy.start)
        started.append((copy, when))

    def flush():
        groups = {}
        for copy, when in started:
            groups.setdefault(when and when[0], (when, []))[1].append(copy)
        started.clear()
        for when, copies in groups.values():

            def wait_all(copies=copies):
                for copy in copies:
                    copy.wait_send()

            only(when, wait_all)

    def arrived(ref, sem, when=None):
        only(when, remote(ref, ref, sem, sem, sibling).wait_recv)

    @pl.when((chip < 6) | (chip >= chips - 6))
    def _():
        for ref in (one_in, two_in, pass_in, four_in, fold_in, near_back, one_back, two_back):
            ref[...] = jnp.zeros(ref.shape, ref.dtype)
        for s in (0, 3):
            kv_near[s] = jnp.zeros(kv_near.shape[1:], BF16)

    mine = pl.ds(pl.multiple_of(core * ROWS, ROWS), ROWS)
    theirs = pl.ds(pl.multiple_of(other * ROWS, ROWS), ROWS)
    k_rows, v_rows = pl.ds(0, ROWS), pl.ds(ROWS, ROWS)
    locals_in = [
        pltpu.make_async_copy(k_hbm, kv_own.at[k_rows], local_sem.at[0]),
        pltpu.make_async_copy(v_hbm, kv_own.at[v_rows], local_sem.at[1]),
        pltpu.make_async_copy(level_hbm, level_s, local_sem.at[2]),
        pltpu.make_async_copy(frame_hbm, frame_v, local_sem.at[3]),
        pltpu.make_async_copy(k_hbm.at[:, half(core)], kv_near.at[1 + core, k_rows], local_sem.at[4]),
        pltpu.make_async_copy(v_hbm.at[:, half(core)], kv_near.at[1 + core, v_rows], local_sem.at[5]),
        pltpu.make_async_copy(q_hbm.at[:, half(core)], q_two.at[mine], local_sem.at[6]),
        pltpu.make_async_copy(g_hbm.at[:, half(core)], g_two.at[mine], local_sem.at[7]),
    ]
    for copy in locals_in[:2]:
        copy.start()

    barrier = pltpu.get_barrier_semaphore()
    partners = [sibling]
    for k in range(1, heads):
        for c in (0, 1):
            partners.append({"seq": chip * 2 + c, "head": (lane + k) % heads})
    expected = len(partners)

    def greet(devices):
        for device in devices:
            pl.semaphore_signal(barrier, inc=1, device_id=device, device_id_type=MESH)

    for steps in (2, -2, 1, -1):
        when = inside(steps)
        only(when, lambda: greet([at(steps, 0), at(steps, 1)]))
        expected = expected + jnp.where(when[1], 2, 0)
    greet(partners)
    for copy in locals_in[2:]:
        copy.start()

    locals_in[0].wait()
    locals_in[1].wait()
    pool = pool_matrix()
    k_pool = dot(pool, kv_own[:ROWS])
    v_pool = dot(pool, kv_own[ROWS:])
    pooled[0 : 2 * ONE, :] = jnp.concatenate([k_pool[:ONE], v_pool[:ONE]], axis=0).astype(BF16)
    pooled[2 * ONE :, :] = jnp.concatenate([k_pool[ONE:], v_pool[ONE:]], axis=0).astype(BF16)

    pl.semaphore_wait(barrier, expected)

    def send_two(steps, side, spot):
        for h in (0, 1):
            send(
                pooled.at[pl.ds(2 * ONE, 2 * TWO), half(h)], two_in.at[side, spot],
                two_recv.at[side, spot], at(steps * d, h), inside(sided=(steps,)),
            )

    send_two(2, core, 1)
    send_two(-2, other, 0)
    for h in (0, 1):
        send(
            pooled.at[:, half(h)], one_in.at[core * 2 + 1],
            one_recv.at[core * 2 + 1], at(-d, h), inside(sided=(-1,)),
        )
    send(kv_own.at[:, half(other)], kv_near.at[1 + core], sib_recv.at[0], sibling)
    send(q_hbm.at[:, half(other)], q_two.at[mine], sib_recv.at[2], sibling)
    for h in (0, 1):
        send(kv_own.at[:, half(h)], kv_near.at[3 - 3 * core], near_recv.at[core], at(d, h), inside(sided=(1,)))
    send(g_hbm.at[:, half(other)], g_two.at[mine], sib_recv.at[3], sibling)

    locals_in[2].wait()
    locals_in[3].wait()
    table = [level_s[0, i] for i in range(4)]
    spot = lax.broadcasted_iota(jnp.int32, (8, FAR), 1)
    row = jnp.full((8, FAR), MASKED, F32)

    def level_at(offset):
        choice = jnp.where(offset == -3, table[0], table[1])
        choice = jnp.where(offset == 2, table[2], choice)
        return jnp.where(offset == 3, table[3], choice)

    def slot_bias(rel, wanted, most, bias):
        offset = rel - core
        distance = jnp.abs(offset)
        block = 2 * chip + rel
        inside = (distance >= 2) & (distance <= most) & (block >= 0) & (block < blocks)
        chosen = (distance > REACH1) | (level_at(offset) == wanted)
        return jnp.where(inside & chosen, bias * LOG2E, MASKED)

    for s, rel in enumerate(REL_ONE):
        value = slot_bias(rel, 1, REACH1, math.log(POOL1))
        row = jnp.where((spot >= s * ONE) & (spot < (s + 1) * ONE), value, row)
    for s, rel in enumerate(REL_MIDDLE + REL_LAST):
        low = len(REL_ONE) * ONE + s * TWO
        value = slot_bias(rel, 2, REACH2, math.log(POOL2))
        row = jnp.where((spot >= low) & (spot < low + TWO), value, row)
    far_bias[core] = row
    send(far_bias.at[core], far_bias.at[core], sib_recv.at[4], sibling)

    lengths = frame_v[...].astype(F32)
    count = lengths.shape[1]
    i = lax.broadcasted_iota(jnp.int32, (count, count), 0)
    j = lax.broadcasted_iota(jnp.int32, (count, count), 1)
    ends_column = jnp.sum(jnp.where(j <= i, lengths, 0.0), axis=1, keepdims=True)
    ends_row = jnp.sum(jnp.where(i == j, ends_column, 0.0), axis=0, keepdims=True)
    start = (2 * chip - 1) * ROWS
    key_place = start + lax.broadcasted_iota(jnp.int32, (1, 4 * ROWS), 1)
    key_frame = jnp.sum(jnp.where(key_place.astype(F32) >= ends_column, 1.0, 0.0), axis=0, keepdims=True)
    key_inside = (key_place >= 0) & (key_place < blocks * ROWS)
    for b in (0, 1):
        place = start + (b + 1) * ROWS + lax.broadcasted_iota(jnp.int32, (ROWS, 1), 0)
        frame = jnp.sum(jnp.where(place.astype(F32) >= ends_row, 1.0, 0.0), axis=1, keepdims=True)
        matched = jnp.where(frame == key_frame, MATCHED_FRAME_ADD * LOG2E, 0.0)
        matched = jnp.where(key_inside, matched, MASKED)
        rows = slice(b * ROWS, (b + 1) * ROWS)
        near_bias[rows, OWN] = matched[:, ROWS : 3 * ROWS]
        near_bias[rows, SIDE] = matched[:, 3 * b * ROWS : (3 * b + 1) * ROWS]

    scale = LOG2E / math.sqrt(HEAD_DIM)
    columns = [slice(h * HEAD_DIM, (h + 1) * HEAD_DIM) for h in (0, 1)]
    first, second = slice(0, ROWS), slice(ROWS, 2 * ROWS)
    highs, totals, accs = [[], []], [None, None], [None, None]

    def far_of(part):
        low, high = part.start - MIDDLE.start, part.stop - MIDDLE.start
        shape = (ROWS, high - low)
        return jnp.concatenate([jnp.broadcast_to(far_bias[b, 0:1, low:high], shape) for b in (0, 1)], axis=0)

    def attend(h, part, scores, product):
        top = jnp.max(scores, axis=1, keepdims=True)
        if highs[h]:
            top = jnp.maximum(highs[h][-1], top)
        e = jnp.exp2(scores - top)
        weight[h, :, part] = e
        total = jnp.sum(e, axis=1, keepdims=True)
        acc = product(e.astype(BF16))
        if highs[h]:
            alpha = jnp.exp2(highs[h][-1] - top)
            total = totals[h] * alpha + total
            acc = accs[h] * alpha + acc
        highs[h].append(top)
        totals[h], accs[h] = total, acc

    rows_of = (first, second)

    def own_of(kind, h):
        return kv_near[1:3, rows_of[kind], columns[h]].reshape(2 * ROWS, HEAD_DIM)

    for side in (0, 1):
        sigma = direction(side)
        pair, two = pl.ds(0, 2), -2 * sigma
        for s in (0, 1):
            arrived(two_in.at[side, s], two_recv.at[side, s], inside(two))
        send(
            two_in.at[side, pair], two_in.at[side, pl.ds(4, 2)],
            two_recv.at[side, 4], at(2 * sigma, core), inside(two, 2 * sigma),
        )
        send(
            two_in.at[side, pair], two_in.at[side, pl.ds(2, 2)],
            two_recv.at[side, 2], at(sigma, core), inside(two, sigma),
        )

    locals_in[4].wait()
    locals_in[6].wait()
    locals_in[5].wait()
    arrived(kv_near.at[1 + other], sib_recv.at[0])
    arrived(q_two.at[theirs], sib_recv.at[2])
    for h in (0, 1):
        scores = dot_nt(q_two[:, columns[h]], own_of(0, h)) * scale + near_bias[:, OWN]
        attend(h, OWN, scores, lambda e: dot(e, own_of(1, h)))

    for side in (0, 1):
        sigma = direction(side)
        pair, four = pl.ds(4, 2), -4 * sigma
        arrived(two_in.at[side, pair], two_recv.at[side, 4], inside(four))
        send(
            two_in.at[side, pair], two_in.at[side, pl.ds(6, 2)],
            two_recv.at[side, 6], at(sigma, core), inside(four, sigma),
        )
        send(two_in.at[side, 5], two_in.at[side, 8], two_recv.at[side, 8], at(2 * sigma, core), inside(four, 2 * sigma))

    arrived(kv_near.at[3], near_recv.at[0], inside(1))
    arrived(kv_near.at[0], near_recv.at[1], inside(-1))
    near_pools = [(dot(pool, kv_near[s, first]), dot(pool, kv_near[s, second])) for s in (0, 3)]
    ones_only = pl.ds(0, 2 * ONE)
    for i, side in ((0, 1), (1, 0)):
        sigma = direction(side)
        fold_out[i] = jnp.concatenate([p[:ONE] for p in near_pools[i]], axis=0).astype(BF16)
        send(
            fold_out.at[i], one_in.at[side * 2, ones_only],
            one_recv.at[side * 2], at(sigma, core), inside(-sigma, sigma),
        )
    for h in (0, 1):
        query = q_two[:, columns[h]]
        scores = jnp.concatenate(
            [dot_nt(query[first], kv_near[0, first, columns[h]]), dot_nt(query[second], kv_near[3, first, columns[h]])], axis=0
        )
        attend(
            h, SIDE, scores * scale + near_bias[:, SIDE],
            lambda e: jnp.concatenate(
                [dot(e[first], kv_near[0, second, columns[h]]), dot(e[second], kv_near[3, second, columns[h]])], axis=0
            ),
        )

    for side in (0, 1):
        sigma = direction(side)
        arrived(one_in.at[side * 2, ones_only], one_recv.at[side * 2], inside(-2 * sigma))
        arrived(one_in.at[side * 2 + 1], one_recv.at[side * 2 + 1], inside(sigma))
    arrived(far_bias.at[other], sib_recv.at[4])
    nearest = [two_in[0, 1], one_in[1, 2 * ONE :], two_in[1, 1], one_in[3, 2 * ONE :]]
    nearest = [x.astype(F32) for x in nearest]
    for kind, middle in ((0, k_middle), (1, v_middle)):
        ones = slice(kind * ONE, (kind + 1) * ONE)
        rows = slice(kind * TWO, (kind + 1) * TWO)
        for s in range(4):
            middle[s * ONE : (s + 1) * ONE] = one_in[s, ones]
        for i in (0, 1):
            middle[(4 + i) * ONE : (5 + i) * ONE] = fold_out[i, ones]
        parts = [x[rows] for x in nearest] + [p[kind][ONE:] for p in near_pools]
        parts += [two_in[side, 0].astype(F32)[rows] for side in (0, 1)]
        middle[6 * ONE :] = jnp.concatenate(parts, axis=0).astype(BF16)
    for h in (0, 1):
        scores = dot_nt(q_two[:, columns[h]], k_middle[:, columns[h]]) * scale + far_of(MIDDLE)
        attend(h, MIDDLE, scores, lambda e: dot(e, v_middle[:, columns[h]]))

    for side in (0, 1):
        sigma = direction(side)
        for s, steps in ((2, 3), (6, 5)):
            arrived(two_in.at[side, pl.ds(s, 2)], two_recv.at[side, s], inside(-steps * sigma))
        arrived(two_in.at[side, 8], two_recv.at[side, 8], inside(-6 * sigma))
    twos = [two_in[side, 2:].astype(F32) for side in (0, 1)]
    for kind, last in ((0, k_last), (1, v_last)):
        rows = slice(kind * TWO, (kind + 1) * TWO)
        parts = [t[:, rows].reshape(7 * TWO, HALF) for t in twos] + [jnp.zeros((2 * TWO, HALF), F32)]
        last[...] = jnp.concatenate(parts, axis=0).astype(BF16)
    for h in (0, 1):
        scores = dot_nt(q_two[:, columns[h]], k_last[:, columns[h]]) * scale + far_of(LAST)
        attend(h, LAST, scores, lambda e: dot(e, v_last[:, columns[h]]))
    inverse_totals = [1.0 / totals[h] for h in (0, 1)]
    for h in (0, 1):
        mixed[:, columns[h]] = accs[h] * inverse_totals[h]

    locals_in[7].wait()
    arrived(g_two.at[theirs], sib_recv.at[3])
    mates = 2 * heads
    place = lane * 2 + core
    value = mixed[...]
    energy = jnp.sum(value * value, axis=1, keepdims=True)
    product = jnp.sum(value * g_two[...].astype(F32), axis=1, keepdims=True)
    stats[place] = jnp.concatenate(
        [row_of(energy[:ROWS]), row_of(energy[ROWS:]), row_of(product[:ROWS]), row_of(product[ROWS:]), jnp.zeros((4, ROWS), F32)],
        axis=0,
    )
    for k in range(1, mates):
        to = (place + k) % mates
        send(stats.at[place], stats.at[place], stat_recv.at[place], {"seq": chip * 2 + to % 2, "head": to // 2})
    for h in (0, 1):
        for index, part in enumerate((OWN, SIDE, MIDDLE, LAST)):
            weights = weight[h, :, part] * (jnp.exp2(highs[h][index] - highs[h][-1]) * inverse_totals[h])
            weight[h, :, part] = weights
            turned[h, part, :] = weights.T.astype(BF16)
    for k in range(1, mates):
        source = (place + k) % mates
        arrived(stats.at[source], stat_recv.at[source])
    summed = stats[0]
    for k in range(1, mates):
        summed = summed + stats[k]
    width = HEADS * HEAD_DIM
    deltas = [[], []]
    for b, rows in ((0, first), (1, second)):
        inverse = lax.rsqrt(column_of(summed[b : b + 1]) / width + NORM_EPSILON)
        agreement = column_of(summed[2 + b : 3 + b]) * inverse
        normed = mixed[rows] * inverse
        att[rows] = normed.astype(BF16)
        grad = (inverse * (g_two[rows].astype(F32) - normed * (agreement / width))).astype(BF16)
        mixed_grad[rows] = grad
        both = grad.astype(F32) * mixed[rows]
        for h in (0, 1):
            deltas[h].append(jnp.sum(both[:, columns[h]], axis=1, keepdims=True))
    deltas = [jnp.concatenate(deltas[h], axis=0) for h in (0, 1)]

    unscale = 1.0 / math.sqrt(HEAD_DIM)
    query_grads = [None, None]

    def slopes_of(h, part, products):
        weights = weight[h, :, part]
        return (weights * (products - deltas[h])).astype(BF16)

    def plain_backward(part, k_ref, v_ref):
        k_parts, v_parts = [], []
        for h in (0, 1):
            grad = mixed_grad[:, columns[h]]
            slopes = slopes_of(h, part, dot_nt(grad, v_ref(h)))
            change = dot(slopes, k_ref(h))
            query_grads[h] = change if query_grads[h] is None else query_grads[h] + change
            k_parts.append(dot_tn(slopes, q_two[:, columns[h]]) * unscale)
            v_parts.append(dot(turned[h, part, :], grad))
        return jnp.concatenate(k_parts, axis=1), jnp.concatenate(v_parts, axis=1)

    def two_rows(pair, low):
        return jnp.concatenate([g[low : low + TWO] for g in pair], axis=0)

    last = plain_backward(LAST, lambda h: k_last[:, columns[h]], lambda h: v_last[:, columns[h]])
    for side in (0, 1):
        sigma = direction(side)
        for s in (1, 2, 5, 6, 7):
            two_out[side, s] = two_rows(last, (side * 7 + s - 1) * TWO).astype(BF16)
        send(
            two_out.at[side, pl.ds(5, 2)], pass_in.at[side, pl.ds(0, 2)],
            pass_recv.at[side, 0], at(-sigma, core), inside(-5 * sigma),
        )
        send(two_out.at[side, 7], pass_in.at[side, 4], pass_recv.at[side, 2], at(-2 * sigma, core), inside(-6 * sigma))
        send(
            two_out.at[side, pl.ds(1, 2)], pass_in.at[side, pl.ds(2, 2)],
            pass_recv.at[side, 1], at(-sigma, core), inside(-3 * sigma),
        )
    out_att = pltpu.make_async_copy(att.at[mine], att_hbm.at[:, half(core)], local_sem.at[8])
    out_att.start()
    send(att.at[theirs], att_hbm.at[:, half(core)], out_recv.at[0], sibling)

    middle = plain_backward(MIDDLE, lambda h: k_middle[:, columns[h]], lambda h: v_middle[:, columns[h]])
    for s in range(4):
        for kind in (0, 1):
            pool_out[s, kind * ONE : (kind + 1) * ONE] = middle[kind][s * ONE : (s + 1) * ONE].astype(BF16)
    for b in (0, 1):
        s = 2 * b + 1
        pool_out[s, 2 * ONE :] = two_rows(middle, 6 * ONE + s * TWO).astype(BF16)
        send(pool_out.at[s], one_back.at[core], back_one_recv.at[core], at(direction(b), b), inside(direction(b)))
    for side in (0, 1):
        sigma = direction(side)
        send(
            pool_out.at[2 * side, ones_only], fold_in.at[side],
            fold_recv.at[side], at(-sigma, core), inside(-2 * sigma),
        )

    spread = spread_matrix()
    k_sides, v_sides = [[], []], [[], []]
    for h in (0, 1):
        grad = mixed_grad[:, columns[h]]
        query = q_two[:, columns[h]]
        products = jnp.concatenate(
            [dot_nt(grad[first], kv_near[0, second, columns[h]]), dot_nt(grad[second], kv_near[3, second, columns[h]])], axis=0
        )
        slopes = slopes_of(h, SIDE, products)
        query_grads[h] = query_grads[h] + jnp.concatenate(
            [dot(slopes[first], kv_near[0, first, columns[h]]), dot(slopes[second], kv_near[3, first, columns[h]])], axis=0
        )
        for b, rows in ((0, second), (1, first)):
            k_sides[b].append(dot_tn(slopes[rows], query[rows]) * unscale)
            v_sides[b].append(dot(turned[h, SIDE, rows], grad[rows]))
    for side in (0, 1):
        sigma = direction(side)
        four = -4 * sigma
        arrived(pass_in.at[side, pl.ds(0, 2)], pass_recv.at[side, 0], inside(sigma, four))
        arrived(pass_in.at[side, 4], pass_recv.at[side, 2], inside(2 * sigma, four))
        passed = [pass_in[side, s].astype(F32) for s in (0, 1, 4)]
        two_out[side, 3] = (two_rows(last, (side * 7 + 2) * TWO) + passed[0]).astype(BF16)
        two_out[side, 4] = (two_rows(last, (side * 7 + 3) * TWO) + passed[1] + passed[2]).astype(BF16)
        send(two_out.at[side, pl.ds(3, 2)], four_in.at[side], pass_recv.at[side, 3], at(-2 * sigma, core), inside(four))

    for b in (0, 1):
        p = 5 - b
        sigma = direction(b)
        arrived(fold_in.at[b], fold_recv.at[b], inside(sigma, -sigma))
        folded = fold_in[b].astype(F32)
        for kind, sides in ((0, k_sides), (1, v_sides)):
            pools = middle[kind]
            small = jnp.concatenate(
                [pools[p * ONE : (p + 1) * ONE] + folded[kind * ONE : (kind + 1) * ONE], pools[6 * ONE + p * TWO : 6 * ONE + (p + 1) * TWO]], axis=0
            )
            near_out[b, kind * ROWS : (kind + 1) * ROWS] = (
                jnp.concatenate(sides[b], axis=1) + dot(spread, small.astype(BF16))
            ).astype(BF16)
        send(near_out.at[b], near_back.at[core], back_near_recv.at[core], at(-direction(b), b), inside(-direction(b)))

    own = plain_backward(OWN, lambda h: own_of(0, h), lambda h: own_of(1, h))
    for kind in (0, 1):
        sib_out[kind * ROWS : (kind + 1) * ROWS] = jnp.where(core == 0, own[kind][second], own[kind][first]).astype(BF16)
    send(sib_out, sib_back, out_recv.at[1], sibling)
    for h in (0, 1):
        dq[:, columns[h]] = (query_grads[h] * unscale).astype(BF16)
    out_dq = pltpu.make_async_copy(dq.at[mine], dq_hbm.at[:, half(core)], local_sem.at[9])
    out_dq.start()
    send(dq.at[theirs], dq_hbm.at[:, half(core)], out_recv.at[2], sibling)

    for side in (0, 1):
        sigma = direction(side)
        two = -2 * sigma
        arrived(pass_in.at[side, pl.ds(2, 2)], pass_recv.at[side, 1], inside(sigma, two))
        arrived(four_in.at[side], pass_recv.at[side, 3], inside(2 * sigma, two))
        passed = pass_in[side, 2:4].astype(F32) + four_in[side].astype(F32)
        two_out[side, 0] = (two_rows(middle, 6 * ONE + (6 + side) * TWO) + passed[0]).astype(BF16)
        two_out[side, 8] = (two_rows(middle, 6 * ONE + 2 * side * TWO) + passed[1]).astype(BF16)
        send(two_out.at[side, 0], two_back.at[core, 0], back_two_recv.at[core, 0], at(two, 1 - side), inside(two))
        send(two_out.at[side, 8], two_back.at[core, 1], back_two_recv.at[core, 1], at(two, side), inside(two))

    arrived(sib_back, out_recv.at[1])
    mine_grads = [jnp.where(core == 0, own[kind][first], own[kind][second]) for kind in (0, 1)]
    bases = {}
    for h in (0, 1):
        arrived(one_back.at[h], back_one_recv.at[h], inside(sided=(-1,)))
        for j, steps in enumerate((-2, 2)):
            arrived(two_back.at[h, j], back_two_recv.at[h, j], inside(sided=(steps,)))
        ones = one_back[h].astype(F32)
        twos = ones[2 * ONE :] + two_back[h, 0].astype(F32) + two_back[h, 1].astype(F32)
        for kind in (0, 1):
            rows = slice(kind * ROWS, (kind + 1) * ROWS)
            small = jnp.concatenate([ones[kind * ONE : (kind + 1) * ONE], twos[kind * TWO : (kind + 1) * TWO]], axis=0)
            grads = jnp.where(core == h, mine_grads[kind], sib_back[rows].astype(F32))
            bases[h, kind] = grads + dot(spread, small.astype(BF16))
    arrived(att_hbm.at[:, half(other)], out_recv.at[0])
    arrived(dq_hbm.at[:, half(other)], out_recv.at[2])
    flush()
    for h in (0, 1):
        arrived(near_back.at[h], back_near_recv.at[h], inside(sided=(1,)))
    outs = [out_att, out_dq]
    for kind, out, out_hbm in ((0, dk, dk_hbm), (1, dv, dv_hbm)):
        rows = slice(kind * ROWS, (kind + 1) * ROWS)
        for h in (0, 1):
            out[:, h * HALF : (h + 1) * HALF] = (bases[h, kind] + near_back[h, rows].astype(F32)).astype(BF16)
        outs.append(pltpu.make_async_copy(out, out_hbm, local_sem.at[10 + kind]))
        outs[-1].start()
    for copy in outs:
        copy.wait()


def write_out(*refs):
    *arrays, sems = refs
    copies = [pltpu.make_async_copy(arrays[i], arrays[4 + i], sems.at[i]) for i in range(4)]
    for copy in copies:
        copy.start()
    for copy in copies:
        copy.wait()


def body(queries, keys, values, out_grad, level_choice, frame_lengths):
    rows, width = queries.shape
    vmem = pltpu.VMEM
    dma = pltpu.SemaphoreType.DMA
    out = jax.ShapeDtypeStruct((rows, width), BF16)
    limit = 40 * 1024 * 1024
    arrays = (queries, keys, values, out_grad, level_choice, frame_lengths.reshape(1, -1))
    results = pl.pallas_call(
        kernel,
        out_shape=(out, out, out, out),
        in_specs=[pl.BlockSpec(memory_space=pl.ANY)] * 6,
        out_specs=(pl.BlockSpec(memory_space=pl.ANY),) * 4,
        scratch_shapes=[
            vmem((2 * ROWS, width), BF16),
            vmem((2 * ROWS, HALF), BF16),
            vmem((2 * ROWS, HALF), BF16),
            vmem((4, 2 * ROWS, HALF), BF16),
            vmem((POOLED, width), BF16),
            vmem((4, POOLED, HALF), BF16),
            vmem((2, 9, 2 * TWO, HALF), BF16),
            vmem((256, HALF), BF16),
            vmem((256, HALF), BF16),
            vmem((128, HALF), BF16),
            vmem((128, HALF), BF16),
            pltpu.SMEM((1, 4), jnp.int32),
            vmem((1, 64), jnp.int32),
            vmem((2 * ROWS, 384), F32),
            vmem((2, 8, FAR), F32),
            vmem((2, 2 * ROWS, 768), F32),
            vmem((2, 768, 2 * ROWS), BF16),
            vmem((2 * ROWS, HALF), F32),
            vmem((8, 8, ROWS), F32),
            vmem((2 * ROWS, HALF), BF16),
            vmem((2 * ROWS, HALF), BF16),
            vmem((2 * ROWS, HALF), BF16),
            vmem((2, 2 * ROWS, HALF), BF16),
            vmem((4, POOLED, HALF), BF16),
            vmem((2, 9, 2 * TWO, HALF), BF16),
            vmem((2 * ROWS, HALF), BF16),
            vmem((2, 2 * ONE, HALF), BF16),
            vmem((2, 5, 2 * TWO, HALF), BF16),
            vmem((2, 2, 2 * TWO, HALF), BF16),
            vmem((2, 2 * ONE, HALF), BF16),
            vmem((2, 2 * ROWS, HALF), BF16),
            vmem((2, POOLED, HALF), BF16),
            vmem((2, 2, 2 * TWO, HALF), BF16),
            vmem((2 * ROWS, HALF), BF16),
            vmem((ROWS, width), BF16),
            vmem((ROWS, width), BF16),
            dma((12,)),
            dma((64,)),
            dma((5,)),
            dma((2,)),
            dma((4,)),
            dma((2, 9)),
            dma((8,)),
            dma((2, 4)),
            dma((2,)),
            dma((2,)),
            dma((2,)),
            dma((2, 2)),
            dma((3,)),
        ],
        compiler_params=pltpu.CompilerParams(collective_id=0, has_side_effects=True, vmem_limit_bytes=limit),
        cost_estimate=pl.CostEstimate(flops=700_000_000, bytes_accessed=1_100_000, transcendentals=400_000),
    )(*[pltpu.with_memory_space_constraint(array, pltpu.HBM) for array in arrays])
    return pl.pallas_call(
        write_out,
        out_shape=(out, out, out, out),
        in_specs=[pl.BlockSpec(memory_space=pl.ANY)] * 4,
        out_specs=(pl.BlockSpec(memory_space=pl.ANY),) * 4,
        scratch_shapes=[dma((4,))],
        compiler_params=pltpu.CompilerParams(vmem_limit_bytes=limit),
        cost_estimate=pl.CostEstimate(flops=0, bytes_accessed=1_100_000, transcendentals=0),
    )(*results)


def solution(mesh):
    in_specs = (
        P("seq", "head"),
        P("seq", "head"),
        P("seq", "head"),
        P("seq", "head"),
        P("seq", None),
        P(),
    )
    out_specs = (P("seq", "head"), P("seq", "head"), P("seq", "head"), P("seq", "head"))
    return jax.shard_map(body, mesh=mesh, in_specs=in_specs, out_specs=out_specs, check_vma=False)
```

```python
import math

import jax
import jax.numpy as jnp
from jax import lax
from jax.experimental import pallas as pl
from jax.experimental.pallas import tpu as pltpu
from jax.sharding import PartitionSpec as P

HEADS = 16
HEAD_DIM = 128
POOL1 = 4
POOL2 = 16
REACH1 = 3
REACH2 = 11
MATCHED_FRAME_ADD = 1.0
NORM_EPSILON = 1e-06

MESH = pl.DeviceIdType.MESH
F32 = jnp.float32
BF16 = jnp.bfloat16
LOG2E = math.log2(math.e)
MASKED = -1e30

ROWS = 128
HALF = 256
ONE = ROWS // POOL1
TWO = ROWS // POOL2
POOLED = 2 * (ONE + TWO)
NEAR = 3 * ROWS
FAR = 384

STEPS_ONE = (2, -1)


def direction(b):
    return 2 * b - 1


REL_ONE = [-2 * steps * direction(b) + b for b in (0, 1) for steps in STEPS_ONE] + [-1, 2]


def relative_two(side):
    sigma = direction(side)
    spots = [(2, 1 - side), (3, 1 - side), (3, side), (4, 1 - side), (4, side), (5, 1 - side), (5, side), (6, side)]
    return [-2 * k * sigma + b for k, b in spots]


REL_TWO = [relative_two(0), relative_two(1)]
REL_MIDDLE = REL_ONE + [REL_TWO[0][0], REL_TWO[1][0]]
REL_LAST = REL_TWO[0][1:] + REL_TWO[1][1:]
OWN, SIDE, MIDDLE, LAST = slice(0, 256), slice(256, 384), slice(384, 640), slice(640, 768)


def dot_nt(a, b):
    return lax.dot_general(a, b, (((1,), (1,)), ((), ())), preferred_element_type=F32)


def dot_tn(a, b):
    return lax.dot_general(a, b, (((0,), (0,)), ((), ())), preferred_element_type=F32)


def dot(a, b):
    return jnp.dot(a, b, preferred_element_type=F32)


def pool_matrix():
    r = lax.broadcasted_iota(jnp.int32, (ONE + TWO, ROWS), 0)
    t = lax.broadcasted_iota(jnp.int32, (ONE + TWO, ROWS), 1)
    one = jnp.where((t >> 2) == r, 1.0 / POOL1, 0.0)
    two = jnp.where((t >> 4) == r - ONE, 1.0 / POOL2, 0.0)
    return jnp.where(r < ONE, one, two).astype(BF16)


def spread_matrix():
    t = lax.broadcasted_iota(jnp.int32, (ROWS, ONE + TWO), 0)
    r = lax.broadcasted_iota(jnp.int32, (ROWS, ONE + TWO), 1)
    one = jnp.where((t >> 2) == r, 1.0 / POOL1, 0.0)
    two = jnp.where((t >> 4) == r - ONE, 1.0 / POOL2, 0.0)
    return jnp.where(r < ONE, one, two).astype(BF16)


def column_of(row):
    i = lax.broadcasted_iota(jnp.int32, (ROWS, ROWS), 0)
    j = lax.broadcasted_iota(jnp.int32, (ROWS, ROWS), 1)
    return jnp.sum(jnp.where(i == j, row, 0.0), axis=1, keepdims=True)


def row_of(column):
    i = lax.broadcasted_iota(jnp.int32, (ROWS, ROWS), 0)
    j = lax.broadcasted_iota(jnp.int32, (ROWS, ROWS), 1)
    return jnp.sum(jnp.where(i == j, column, 0.0), axis=0, keepdims=True)


def kernel(
    q_hbm, k_hbm, v_hbm, g_hbm, level_hbm, frame_hbm,
    att_hbm, dq_hbm, dk_hbm, dv_hbm,
    kv_own, q_two, g_two, kv_near, pooled, one_in, two_in, k_middle, v_middle, k_last, v_last,
    level_s, frame_v, near_bias, far_bias, weight, turned, mixed, stats,
    mixed_grad, att, dq, near_out, pool_out, two_out, sib_out, fold_out,
    pass_in, four_in, fold_in, near_back, one_back, two_back, sib_back, dk, dv,
    local_sem, send_sem, sib_recv, near_recv, one_recv, two_recv, stat_recv, pass_recv, fold_recv,
    back_near_recv, back_one_recv, back_two_recv, out_recv,
):
    blocks = lax.axis_size("seq")
    chips = blocks // 2
    heads = lax.axis_size("head")
    me = lax.axis_index("seq")
    lane = lax.axis_index("head")
    chip = me // 2
    core = me % 2
    other = 1 - core
    d = direction(core)

    def at(steps, c):
        return {"seq": ((chip + steps + chips) % chips) * 2 + c}

    sibling = {"seq": chip * 2 + other}

    def half(h):
        return pl.ds(pl.multiple_of(h * HALF, HALF), HALF)

    def remote(src, dst, send, recv, device):
        return pltpu.make_async_remote_copy(
            src_ref=src, dst_ref=dst, send_sem=send, recv_sem=recv, device_id=device, device_id_type=MESH
        )

    def inside(*steps, sided=()):
        away = [s for s in steps] + [s * d for s in sided]
        known = True
        for s in away:
            known = known & (chip + s >= 0) & (chip + s < chips)
        return (steps, sided), known

    def only(when, act):
        if when is None:
            act()
        else:
            pl.when(when[1])(act)

    sent = 0
    started = []

    def send(src, dst, recv, device, when=None):
        nonlocal sent
        copy = remote(src, dst, send_sem.at[sent], recv, device)
        sent += 1
        only(when, copy.start)
        started.append((copy, when))

    def flush():
        groups = {}
        for copy, when in started:
            groups.setdefault(when and when[0], (when, []))[1].append(copy)
        started.clear()
        for when, copies in groups.values():

            def wait_all(copies=copies):
                for copy in copies:
                    copy.wait_send()

            only(when, wait_all)

    def arrived(ref, sem, when=None):
        only(when, remote(ref, ref, sem, sem, sibling).wait_recv)

    @pl.when((chip < 6) | (chip >= chips - 6))
    def _():
        for ref in (one_in, two_in, pass_in, four_in, fold_in, near_back, one_back, two_back):
            ref[...] = jnp.zeros(ref.shape, ref.dtype)
        for s in (0, 3):
            kv_near[s] = jnp.zeros(kv_near.shape[1:], BF16)

    mine = pl.ds(pl.multiple_of(core * ROWS, ROWS), ROWS)
    theirs = pl.ds(pl.multiple_of(other * ROWS, ROWS), ROWS)
    k_rows, v_rows = pl.ds(0, ROWS), pl.ds(ROWS, ROWS)
    locals_in = [
        pltpu.make_async_copy(k_hbm, kv_own.at[k_rows], local_sem.at[0]),
        pltpu.make_async_copy(v_hbm, kv_own.at[v_rows], local_sem.at[1]),
        pltpu.make_async_copy(level_hbm, level_s, local_sem.at[2]),
        pltpu.make_async_copy(frame_hbm, frame_v, local_sem.at[3]),
        pltpu.make_async_copy(k_hbm.at[:, half(core)], kv_near.at[1 + core, k_rows], local_sem.at[4]),
        pltpu.make_async_copy(v_hbm.at[:, half(core)], kv_near.at[1 + core, v_rows], local_sem.at[5]),
        pltpu.make_async_copy(q_hbm.at[:, half(core)], q_two.at[mine], local_sem.at[6]),
        pltpu.make_async_copy(g_hbm.at[:, half(core)], g_two.at[mine], local_sem.at[7]),
    ]
    for copy in locals_in[:2]:
        copy.start()

    barrier = pltpu.get_barrier_semaphore()
    partners = [sibling]
    for k in range(1, heads):
        for c in (0, 1):
            partners.append({"seq": chip * 2 + c, "head": (lane + k) % heads})
    expected = len(partners)

    def greet(devices):
        for device in devices:
            pl.semaphore_signal(barrier, inc=1, device_id=device, device_id_type=MESH)

    for steps in (2, -2, 1, -1):
        when = inside(steps)
        only(when, lambda: greet([at(steps, 0), at(steps, 1)]))
        expected = expected + jnp.where(when[1], 2, 0)
    greet(partners)
    for copy in locals_in[2:]:
        copy.start()

    locals_in[0].wait()
    locals_in[1].wait()
    pool = pool_matrix()
    k_pool = dot(pool, kv_own[:ROWS])
    v_pool = dot(pool, kv_own[ROWS:])
    pooled[0 : 2 * ONE, :] = jnp.concatenate([k_pool[:ONE], v_pool[:ONE]], axis=0).astype(BF16)
    pooled[2 * ONE :, :] = jnp.concatenate([k_pool[ONE:], v_pool[ONE:]], axis=0).astype(BF16)

    pl.semaphore_wait(barrier, expected)

    def send_two(steps, side, spot):
        for h in (0, 1):
            send(
                pooled.at[pl.ds(2 * ONE, 2 * TWO), half(h)], two_in.at[side, spot],
                two_recv.at[side, spot], at(steps * d, h), inside(sided=(steps,)),
            )

    send_two(2, core, 1)
    send_two(-2, other, 0)
    for h in (0, 1):
        send(
            pooled.at[:, half(h)], one_in.at[core * 2 + 1],
            one_recv.at[core * 2 + 1], at(-d, h), inside(sided=(-1,)),
        )
    send(kv_own.at[:, half(other)], kv_near.at[1 + core], sib_recv.at[0], sibling)
    send(q_hbm.at[:, half(other)], q_two.at[mine], sib_recv.at[2], sibling)
    for h in (0, 1):
        send(kv_own.at[:, half(h)], kv_near.at[3 - 3 * core], near_recv.at[core], at(d, h), inside(sided=(1,)))
    send(g_hbm.at[:, half(other)], g_two.at[mine], sib_recv.at[3], sibling)

    locals_in[2].wait()
    locals_in[3].wait()
    table = [level_s[0, i] for i in range(4)]
    spot = lax.broadcasted_iota(jnp.int32, (8, FAR), 1)
    row = jnp.full((8, FAR), MASKED, F32)

    def level_at(offset):
        choice = jnp.where(offset == -3, table[0], table[1])
        choice = jnp.where(offset == 2, table[2], choice)
        return jnp.where(offset == 3, table[3], choice)

    def slot_bias(rel, wanted, most, bias):
        offset = rel - core
        distance = jnp.abs(offset)
        block = 2 * chip + rel
        inside = (distance >= 2) & (distance <= most) & (block >= 0) & (block < blocks)
        chosen = (distance > REACH1) | (level_at(offset) == wanted)
        return jnp.where(inside & chosen, bias * LOG2E, MASKED)

    for s, rel in enumerate(REL_ONE):
        value = slot_bias(rel, 1, REACH1, math.log(POOL1))
        row = jnp.where((spot >= s * ONE) & (spot < (s + 1) * ONE), value, row)
    for s, rel in enumerate(REL_MIDDLE + REL_LAST):
        low = len(REL_ONE) * ONE + s * TWO
        value = slot_bias(rel, 2, REACH2, math.log(POOL2))
        row = jnp.where((spot >= low) & (spot < low + TWO), value, row)
    far_bias[core] = row
    send(far_bias.at[core], far_bias.at[core], sib_recv.at[4], sibling)

    lengths = frame_v[...].astype(F32)
    count = lengths.shape[1]
    i = lax.broadcasted_iota(jnp.int32, (count, count), 0)
    j = lax.broadcasted_iota(jnp.int32, (count, count), 1)
    ends_column = jnp.sum(jnp.where(j <= i, lengths, 0.0), axis=1, keepdims=True)
    ends_row = jnp.sum(jnp.where(i == j, ends_column, 0.0), axis=0, keepdims=True)
    start = (2 * chip - 1) * ROWS
    key_place = start + lax.broadcasted_iota(jnp.int32, (1, 4 * ROWS), 1)
    key_frame = jnp.sum(jnp.where(key_place.astype(F32) >= ends_column, 1.0, 0.0), axis=0, keepdims=True)
    key_inside = (key_place >= 0) & (key_place < blocks * ROWS)
    for b in (0, 1):
        place = start + (b + 1) * ROWS + lax.broadcasted_iota(jnp.int32, (ROWS, 1), 0)
        frame = jnp.sum(jnp.where(place.astype(F32) >= ends_row, 1.0, 0.0), axis=1, keepdims=True)
        matched = jnp.where(frame == key_frame, MATCHED_FRAME_ADD * LOG2E, 0.0)
        matched = jnp.where(key_inside, matched, MASKED)
        rows = slice(b * ROWS, (b + 1) * ROWS)
        near_bias[rows, OWN] = matched[:, ROWS : 3 * ROWS]
        near_bias[rows, SIDE] = matched[:, 3 * b * ROWS : (3 * b + 1) * ROWS]

    scale = LOG2E / math.sqrt(HEAD_DIM)
    columns = [slice(h * HEAD_DIM, (h + 1) * HEAD_DIM) for h in (0, 1)]
    first, second = slice(0, ROWS), slice(ROWS, 2 * ROWS)
    highs, totals, accs = [[], []], [None, None], [None, None]

    def far_of(part):
        low, high = part.start - MIDDLE.start, part.stop - MIDDLE.start
        shape = (ROWS, high - low)
        return jnp.concatenate([jnp.broadcast_to(far_bias[b, 0:1, low:high], shape) for b in (0, 1)], axis=0)

    def attend(h, part, scores, product):
        top = jnp.max(scores, axis=1, keepdims=True)
        if highs[h]:
            top = jnp.maximum(highs[h][-1], top)
        e = jnp.exp2(scores - top)
        weight[h, :, part] = e
        total = jnp.sum(e, axis=1, keepdims=True)
        rounded = e.astype(BF16)
        acc = product(rounded)
        if part in (OWN, SIDE):
            turned[h, part, :] = rounded.T
        if highs[h]:
            alpha = jnp.exp2(highs[h][-1] - top)
            total = totals[h] * alpha + total
            acc = accs[h] * alpha + acc
        highs[h].append(top)
        totals[h], accs[h] = total, acc

    rows_of = (first, second)

    def own_of(kind, h):
        return kv_near[1:3, rows_of[kind], columns[h]].reshape(2 * ROWS, HEAD_DIM)

    for side in (0, 1):
        sigma = direction(side)
        pair, two = pl.ds(0, 2), -2 * sigma
        for s in (0, 1):
            arrived(two_in.at[side, s], two_recv.at[side, s], inside(two))
        send(
            two_in.at[side, pair], two_in.at[side, pl.ds(4, 2)],
            two_recv.at[side, 4], at(2 * sigma, core), inside(two, 2 * sigma),
        )
        send(
            two_in.at[side, pair], two_in.at[side, pl.ds(2, 2)],
            two_recv.at[side, 2], at(sigma, core), inside(two, sigma),
        )

    locals_in[4].wait()
    locals_in[6].wait()
    locals_in[5].wait()
    arrived(kv_near.at[1 + other], sib_recv.at[0])
    arrived(q_two.at[theirs], sib_recv.at[2])
    for h in (0, 1):
        scores = dot_nt(q_two[:, columns[h]], own_of(0, h)) * scale + near_bias[:, OWN]
        attend(h, OWN, scores, lambda e: dot(e, own_of(1, h)))

    for side in (0, 1):
        sigma = direction(side)
        pair, four = pl.ds(4, 2), -4 * sigma
        arrived(two_in.at[side, pair], two_recv.at[side, 4], inside(four))
        send(
            two_in.at[side, pair], two_in.at[side, pl.ds(6, 2)],
            two_recv.at[side, 6], at(sigma, core), inside(four, sigma),
        )
        send(two_in.at[side, 5], two_in.at[side, 8], two_recv.at[side, 8], at(2 * sigma, core), inside(four, 2 * sigma))

    arrived(kv_near.at[3], near_recv.at[0], inside(1))
    arrived(kv_near.at[0], near_recv.at[1], inside(-1))
    near_pools = [(dot(pool, kv_near[s, first]), dot(pool, kv_near[s, second])) for s in (0, 3)]
    ones_only = pl.ds(0, 2 * ONE)
    for i, side in ((0, 1), (1, 0)):
        sigma = direction(side)
        fold_out[i] = jnp.concatenate([p[:ONE] for p in near_pools[i]], axis=0).astype(BF16)
        send(
            fold_out.at[i], one_in.at[side * 2, ones_only],
            one_recv.at[side * 2], at(sigma, core), inside(-sigma, sigma),
        )
    for h in (0, 1):
        query = q_two[:, columns[h]]
        scores = jnp.concatenate(
            [dot_nt(query[first], kv_near[0, first, columns[h]]), dot_nt(query[second], kv_near[3, first, columns[h]])], axis=0
        )
        attend(
            h, SIDE, scores * scale + near_bias[:, SIDE],
            lambda e: jnp.concatenate(
                [dot(e[first], kv_near[0, second, columns[h]]), dot(e[second], kv_near[3, second, columns[h]])], axis=0
            ),
        )

    for side in (0, 1):
        sigma = direction(side)
        arrived(one_in.at[side * 2, ones_only], one_recv.at[side * 2], inside(-2 * sigma))
        arrived(one_in.at[side * 2 + 1], one_recv.at[side * 2 + 1], inside(sigma))
    arrived(far_bias.at[other], sib_recv.at[4])
    nearest = [two_in[0, 1], one_in[1, 2 * ONE :], two_in[1, 1], one_in[3, 2 * ONE :]]
    nearest = [x.astype(F32) for x in nearest]
    for kind, middle in ((0, k_middle), (1, v_middle)):
        ones = slice(kind * ONE, (kind + 1) * ONE)
        rows = slice(kind * TWO, (kind + 1) * TWO)
        for s in range(4):
            middle[s * ONE : (s + 1) * ONE] = one_in[s, ones]
        for i in (0, 1):
            middle[(4 + i) * ONE : (5 + i) * ONE] = fold_out[i, ones]
        parts = [x[rows] for x in nearest] + [p[kind][ONE:] for p in near_pools]
        parts += [two_in[side, 0].astype(F32)[rows] for side in (0, 1)]
        middle[6 * ONE :] = jnp.concatenate(parts, axis=0).astype(BF16)
    for h in (0, 1):
        scores = dot_nt(q_two[:, columns[h]], k_middle[:, columns[h]]) * scale + far_of(MIDDLE)
        attend(h, MIDDLE, scores, lambda e: dot(e, v_middle[:, columns[h]]))

    for side in (0, 1):
        sigma = direction(side)
        for s, steps in ((2, 3), (6, 5)):
            arrived(two_in.at[side, pl.ds(s, 2)], two_recv.at[side, s], inside(-steps * sigma))
        arrived(two_in.at[side, 8], two_recv.at[side, 8], inside(-6 * sigma))
    twos = [two_in[side, 2:].astype(F32) for side in (0, 1)]
    for kind, last in ((0, k_last), (1, v_last)):
        rows = slice(kind * TWO, (kind + 1) * TWO)
        parts = [t[:, rows].reshape(7 * TWO, HALF) for t in twos] + [jnp.zeros((2 * TWO, HALF), F32)]
        last[...] = jnp.concatenate(parts, axis=0).astype(BF16)
    for h in (0, 1):
        scores = dot_nt(q_two[:, columns[h]], k_last[:, columns[h]]) * scale + far_of(LAST)
        attend(h, LAST, scores, lambda e: dot(e, v_last[:, columns[h]]))
    inverse_totals = [1.0 / totals[h] for h in (0, 1)]
    for h in (0, 1):
        mixed[:, columns[h]] = accs[h] * inverse_totals[h]

    locals_in[7].wait()
    arrived(g_two.at[theirs], sib_recv.at[3])
    mates = 2 * heads
    place = lane * 2 + core
    value = mixed[...]
    energy = jnp.sum(value * value, axis=1, keepdims=True)
    product = jnp.sum(value * g_two[...].astype(F32), axis=1, keepdims=True)
    stats[place] = jnp.concatenate(
        [row_of(energy[:ROWS]), row_of(energy[ROWS:]), row_of(product[:ROWS]), row_of(product[ROWS:]), jnp.zeros((4, ROWS), F32)],
        axis=0,
    )
    for k in range(1, mates):
        to = (place + k) % mates
        send(stats.at[place], stats.at[place], stat_recv.at[place], {"seq": chip * 2 + to % 2, "head": to // 2})
    factors = [[], []]
    for h in (0, 1):
        for index, part in enumerate((OWN, SIDE, MIDDLE, LAST)):
            factors[h].append(jnp.exp2(highs[h][index] - highs[h][-1]) * inverse_totals[h])
            if part in (MIDDLE, LAST):
                turned[h, part, :] = weight[h, :, part].astype(BF16).T
    for k in range(1, mates):
        source = (place + k) % mates
        arrived(stats.at[source], stat_recv.at[source])
    summed = stats[0]
    for k in range(1, mates):
        summed = summed + stats[k]
    width = HEADS * HEAD_DIM
    deltas = [[], []]
    for b, rows in ((0, first), (1, second)):
        inverse = lax.rsqrt(column_of(summed[b : b + 1]) / width + NORM_EPSILON)
        agreement = column_of(summed[2 + b : 3 + b]) * inverse
        normed = mixed[rows] * inverse
        att[rows] = normed.astype(BF16)
        grad = inverse * (g_two[rows].astype(F32) - normed * (agreement / width))
        mixed_grad[rows] = grad
        both = grad.astype(BF16).astype(F32) * mixed[rows]
        for h in (0, 1):
            deltas[h].append(jnp.sum(both[:, columns[h]], axis=1, keepdims=True))
    deltas = [jnp.concatenate(deltas[h], axis=0) for h in (0, 1)]

    unscale = 1.0 / math.sqrt(HEAD_DIM)
    query_grads = [None, None]

    def scaled(h, part):
        factor = factors[h][(OWN, SIDE, MIDDLE, LAST).index(part)]
        return (mixed_grad[:, columns[h]] * factor).astype(BF16), deltas[h] * factor

    def slopes_of(h, part, products, delta):
        return (weight[h, :, part] * (products - delta)).astype(BF16)

    def plain_backward(part, k_ref, v_ref):
        k_parts, v_parts = [], []
        for h in (0, 1):
            grad, delta = scaled(h, part)
            slopes = slopes_of(h, part, dot_nt(grad, v_ref(h)), delta)
            change = dot(slopes, k_ref(h))
            query_grads[h] = change if query_grads[h] is None else query_grads[h] + change
            k_parts.append(dot_tn(slopes, q_two[:, columns[h]]) * unscale)
            v_parts.append(dot(turned[h, part, :], grad))
        return jnp.concatenate(k_parts, axis=1), jnp.concatenate(v_parts, axis=1)

    def two_rows(pair, low):
        return jnp.concatenate([g[low : low + TWO] for g in pair], axis=0)

    last = plain_backward(LAST, lambda h: k_last[:, columns[h]], lambda h: v_last[:, columns[h]])
    for side in (0, 1):
        sigma = direction(side)
        for s in (1, 2, 5, 6, 7):
            two_out[side, s] = two_rows(last, (side * 7 + s - 1) * TWO).astype(BF16)
        send(
            two_out.at[side, pl.ds(5, 2)], pass_in.at[side, pl.ds(0, 2)],
            pass_recv.at[side, 0], at(-sigma, core), inside(-5 * sigma),
        )
        send(two_out.at[side, 7], pass_in.at[side, 4], pass_recv.at[side, 2], at(-2 * sigma, core), inside(-6 * sigma))
        send(
            two_out.at[side, pl.ds(1, 2)], pass_in.at[side, pl.ds(2, 2)],
            pass_recv.at[side, 1], at(-sigma, core), inside(-3 * sigma),
        )
    out_att = pltpu.make_async_copy(att.at[mine], att_hbm.at[:, half(core)], local_sem.at[8])
    out_att.start()
    send(att.at[theirs], att_hbm.at[:, half(core)], out_recv.at[0], sibling)

    middle = plain_backward(MIDDLE, lambda h: k_middle[:, columns[h]], lambda h: v_middle[:, columns[h]])
    for s in range(4):
        for kind in (0, 1):
            pool_out[s, kind * ONE : (kind + 1) * ONE] = middle[kind][s * ONE : (s + 1) * ONE].astype(BF16)
    for b in (0, 1):
        s = 2 * b + 1
        pool_out[s, 2 * ONE :] = two_rows(middle, 6 * ONE + s * TWO).astype(BF16)
        send(pool_out.at[s], one_back.at[core], back_one_recv.at[core], at(direction(b), b), inside(direction(b)))
    for side in (0, 1):
        sigma = direction(side)
        send(
            pool_out.at[2 * side, ones_only], fold_in.at[side],
            fold_recv.at[side], at(-sigma, core), inside(-2 * sigma),
        )

    spread = spread_matrix()
    k_sides, v_sides = [[], []], [[], []]
    for h in (0, 1):
        grad, delta = scaled(h, SIDE)
        query = q_two[:, columns[h]]
        products = jnp.concatenate(
            [dot_nt(grad[first], kv_near[0, second, columns[h]]), dot_nt(grad[second], kv_near[3, second, columns[h]])], axis=0
        )
        slopes = slopes_of(h, SIDE, products, delta)
        query_grads[h] = query_grads[h] + jnp.concatenate(
            [dot(slopes[first], kv_near[0, first, columns[h]]), dot(slopes[second], kv_near[3, first, columns[h]])], axis=0
        )
        for b, rows in ((0, second), (1, first)):
            k_sides[b].append(dot_tn(slopes[rows], query[rows]) * unscale)
            v_sides[b].append(dot(turned[h, SIDE, rows], grad[rows]))
    for side in (0, 1):
        sigma = direction(side)
        four = -4 * sigma
        arrived(pass_in.at[side, pl.ds(0, 2)], pass_recv.at[side, 0], inside(sigma, four))
        arrived(pass_in.at[side, 4], pass_recv.at[side, 2], inside(2 * sigma, four))
        passed = [pass_in[side, s].astype(F32) for s in (0, 1, 4)]
        two_out[side, 3] = (two_rows(last, (side * 7 + 2) * TWO) + passed[0]).astype(BF16)
        two_out[side, 4] = (two_rows(last, (side * 7 + 3) * TWO) + passed[1] + passed[2]).astype(BF16)
        send(two_out.at[side, pl.ds(3, 2)], four_in.at[side], pass_recv.at[side, 3], at(-2 * sigma, core), inside(four))

    for b in (0, 1):
        p = 5 - b
        sigma = direction(b)
        arrived(fold_in.at[b], fold_recv.at[b], inside(sigma, -sigma))
        folded = fold_in[b].astype(F32)
        for kind, sides in ((0, k_sides), (1, v_sides)):
            pools = middle[kind]
            small = jnp.concatenate(
                [pools[p * ONE : (p + 1) * ONE] + folded[kind * ONE : (kind + 1) * ONE], pools[6 * ONE + p * TWO : 6 * ONE + (p + 1) * TWO]], axis=0
            )
            near_out[b, kind * ROWS : (kind + 1) * ROWS] = (
                jnp.concatenate(sides[b], axis=1) + dot(spread, small.astype(BF16))
            ).astype(BF16)
        send(near_out.at[b], near_back.at[core], back_near_recv.at[core], at(-direction(b), b), inside(-direction(b)))

    own = plain_backward(OWN, lambda h: own_of(0, h), lambda h: own_of(1, h))
    for kind in (0, 1):
        sib_out[kind * ROWS : (kind + 1) * ROWS] = jnp.where(core == 0, own[kind][second], own[kind][first]).astype(BF16)
    send(sib_out, sib_back, out_recv.at[1], sibling)
    for h in (0, 1):
        dq[:, columns[h]] = (query_grads[h] * unscale).astype(BF16)
    out_dq = pltpu.make_async_copy(dq.at[mine], dq_hbm.at[:, half(core)], local_sem.at[9])
    out_dq.start()
    send(dq.at[theirs], dq_hbm.at[:, half(core)], out_recv.at[2], sibling)

    for side in (0, 1):
        sigma = direction(side)
        two = -2 * sigma
        arrived(pass_in.at[side, pl.ds(2, 2)], pass_recv.at[side, 1], inside(sigma, two))
        arrived(four_in.at[side], pass_recv.at[side, 3], inside(2 * sigma, two))
        passed = pass_in[side, 2:4].astype(F32) + four_in[side].astype(F32)
        two_out[side, 0] = (two_rows(middle, 6 * ONE + (6 + side) * TWO) + passed[0]).astype(BF16)
        two_out[side, 8] = (two_rows(middle, 6 * ONE + 2 * side * TWO) + passed[1]).astype(BF16)
        send(two_out.at[side, 0], two_back.at[core, 0], back_two_recv.at[core, 0], at(two, 1 - side), inside(two))
        send(two_out.at[side, 8], two_back.at[core, 1], back_two_recv.at[core, 1], at(two, side), inside(two))

    arrived(sib_back, out_recv.at[1])
    mine_grads = [jnp.where(core == 0, own[kind][first], own[kind][second]) for kind in (0, 1)]
    bases = {}
    for h in (0, 1):
        arrived(one_back.at[h], back_one_recv.at[h], inside(sided=(-1,)))
        for j, steps in enumerate((-2, 2)):
            arrived(two_back.at[h, j], back_two_recv.at[h, j], inside(sided=(steps,)))
        ones = one_back[h].astype(F32)
        twos = ones[2 * ONE :] + two_back[h, 0].astype(F32) + two_back[h, 1].astype(F32)
        for kind in (0, 1):
            rows = slice(kind * ROWS, (kind + 1) * ROWS)
            small = jnp.concatenate([ones[kind * ONE : (kind + 1) * ONE], twos[kind * TWO : (kind + 1) * TWO]], axis=0)
            grads = jnp.where(core == h, mine_grads[kind], sib_back[rows].astype(F32))
            bases[h, kind] = grads + dot(spread, small.astype(BF16))
    arrived(att_hbm.at[:, half(other)], out_recv.at[0])
    arrived(dq_hbm.at[:, half(other)], out_recv.at[2])
    flush()
    for h in (0, 1):
        arrived(near_back.at[h], back_near_recv.at[h], inside(sided=(1,)))
    outs = [out_att, out_dq]
    for kind, out, out_hbm in ((0, dk, dk_hbm), (1, dv, dv_hbm)):
        rows = slice(kind * ROWS, (kind + 1) * ROWS)
        for h in (0, 1):
            out[:, h * HALF : (h + 1) * HALF] = (bases[h, kind] + near_back[h, rows].astype(F32)).astype(BF16)
        outs.append(pltpu.make_async_copy(out, out_hbm, local_sem.at[10 + kind]))
        outs[-1].start()
    for copy in outs:
        copy.wait()


def write_out(*refs):
    *arrays, sems = refs
    copies = [pltpu.make_async_copy(arrays[i], arrays[4 + i], sems.at[i]) for i in range(4)]
    for copy in copies:
        copy.start()
    for copy in copies:
        copy.wait()


def body(queries, keys, values, out_grad, level_choice, frame_lengths):
    rows, width = queries.shape
    vmem = pltpu.VMEM
    dma = pltpu.SemaphoreType.DMA
    out = jax.ShapeDtypeStruct((rows, width), BF16)
    limit = 40 * 1024 * 1024
    arrays = (queries, keys, values, out_grad, level_choice, frame_lengths.reshape(1, -1))
    results = pl.pallas_call(
        kernel,
        out_shape=(out, out, out, out),
        in_specs=[pl.BlockSpec(memory_space=pl.ANY)] * 6,
        out_specs=(pl.BlockSpec(memory_space=pl.ANY),) * 4,
        scratch_shapes=[
            vmem((2 * ROWS, width), BF16),
            vmem((2 * ROWS, HALF), BF16),
            vmem((2 * ROWS, HALF), BF16),
            vmem((4, 2 * ROWS, HALF), BF16),
            vmem((POOLED, width), BF16),
            vmem((4, POOLED, HALF), BF16),
            vmem((2, 9, 2 * TWO, HALF), BF16),
            vmem((256, HALF), BF16),
            vmem((256, HALF), BF16),
            vmem((128, HALF), BF16),
            vmem((128, HALF), BF16),
            pltpu.SMEM((1, 4), jnp.int32),
            vmem((1, 64), jnp.int32),
            vmem((2 * ROWS, 384), F32),
            vmem((2, 8, FAR), F32),
            vmem((2, 2 * ROWS, 768), F32),
            vmem((2, 768, 2 * ROWS), BF16),
            vmem((2 * ROWS, HALF), F32),
            vmem((8, 8, ROWS), F32),
            vmem((2 * ROWS, HALF), F32),
            vmem((2 * ROWS, HALF), BF16),
            vmem((2 * ROWS, HALF), BF16),
            vmem((2, 2 * ROWS, HALF), BF16),
            vmem((4, POOLED, HALF), BF16),
            vmem((2, 9, 2 * TWO, HALF), BF16),
            vmem((2 * ROWS, HALF), BF16),
            vmem((2, 2 * ONE, HALF), BF16),
            vmem((2, 5, 2 * TWO, HALF), BF16),
            vmem((2, 2, 2 * TWO, HALF), BF16),
            vmem((2, 2 * ONE, HALF), BF16),
            vmem((2, 2 * ROWS, HALF), BF16),
            vmem((2, POOLED, HALF), BF16),
            vmem((2, 2, 2 * TWO, HALF), BF16),
            vmem((2 * ROWS, HALF), BF16),
            vmem((ROWS, width), BF16),
            vmem((ROWS, width), BF16),
            dma((12,)),
            dma((64,)),
            dma((5,)),
            dma((2,)),
            dma((4,)),
            dma((2, 9)),
            dma((8,)),
            dma((2, 4)),
            dma((2,)),
            dma((2,)),
            dma((2,)),
            dma((2, 2)),
            dma((3,)),
        ],
        compiler_params=pltpu.CompilerParams(collective_id=0, has_side_effects=True, vmem_limit_bytes=limit),
        cost_estimate=pl.CostEstimate(flops=700_000_000, bytes_accessed=1_100_000, transcendentals=400_000),
    )(*[pltpu.with_memory_space_constraint(array, pltpu.HBM) for array in arrays])
    return pl.pallas_call(
        write_out,
        out_shape=(out, out, out, out),
        in_specs=[pl.BlockSpec(memory_space=pl.ANY)] * 4,
        out_specs=(pl.BlockSpec(memory_space=pl.ANY),) * 4,
        scratch_shapes=[dma((4,))],
        compiler_params=pltpu.CompilerParams(vmem_limit_bytes=limit),
        cost_estimate=pl.CostEstimate(flops=0, bytes_accessed=1_100_000, transcendentals=0),
    )(*results)


def solution(mesh):
    in_specs = (
        P("seq", "head"),
        P("seq", "head"),
        P("seq", "head"),
        P("seq", "head"),
        P("seq", None),
        P(),
    )
    out_specs = (P("seq", "head"), P("seq", "head"), P("seq", "head"), P("seq", "head"))
    return jax.shard_map(body, mesh=mesh, in_specs=in_specs, out_specs=out_specs, check_vma=False)
```

```python
import math

import jax
import jax.numpy as jnp
from jax import lax
from jax.experimental import pallas as pl
from jax.experimental.pallas import tpu as pltpu
from jax.sharding import PartitionSpec as P

HEADS = 16
HEAD_DIM = 128
POOL1 = 4
POOL2 = 16
REACH1 = 3
REACH2 = 11
MATCHED_FRAME_ADD = 1.0
NORM_EPSILON = 1e-06

MESH = pl.DeviceIdType.MESH
F32 = jnp.float32
BF16 = jnp.bfloat16
LOG2E = math.log2(math.e)
MASKED = -1e30

ROWS = 128
HALF = 256
ONE = ROWS // POOL1
TWO = ROWS // POOL2
POOLED = 2 * (ONE + TWO)
NEAR = 3 * ROWS
FAR = 384

STEPS_ONE = (2, -1)


def direction(b):
    return 2 * b - 1


REL_ONE = [-2 * steps * direction(b) + b for b in (0, 1) for steps in STEPS_ONE] + [-1, 2]


def relative_two(side):
    sigma = direction(side)
    spots = [(2, 1 - side), (3, 1 - side), (3, side), (4, 1 - side), (4, side), (5, 1 - side), (5, side), (6, side)]
    return [-2 * k * sigma + b for k, b in spots]


REL_TWO = [relative_two(0), relative_two(1)]
REL_MIDDLE = REL_ONE + [REL_TWO[0][0], REL_TWO[1][0]]
REL_LAST = REL_TWO[0][1:] + REL_TWO[1][1:]
OWN, SIDE, MIDDLE, LAST = slice(0, 256), slice(256, 384), slice(384, 640), slice(640, 768)


def dot_nt(a, b):
    return lax.dot_general(a, b, (((1,), (1,)), ((), ())), preferred_element_type=F32)


def dot_tn(a, b):
    return lax.dot_general(a, b, (((0,), (0,)), ((), ())), preferred_element_type=F32)


def dot(a, b):
    return jnp.dot(a, b, preferred_element_type=F32)


def pool_matrix():
    r = lax.broadcasted_iota(jnp.int32, (ONE + TWO, ROWS), 0)
    t = lax.broadcasted_iota(jnp.int32, (ONE + TWO, ROWS), 1)
    one = jnp.where((t >> 2) == r, 1.0 / POOL1, 0.0)
    two = jnp.where((t >> 4) == r - ONE, 1.0 / POOL2, 0.0)
    return jnp.where(r < ONE, one, two).astype(BF16)


def spread_matrix():
    t = lax.broadcasted_iota(jnp.int32, (ROWS, ONE + TWO), 0)
    r = lax.broadcasted_iota(jnp.int32, (ROWS, ONE + TWO), 1)
    one = jnp.where((t >> 2) == r, 1.0 / POOL1, 0.0)
    two = jnp.where((t >> 4) == r - ONE, 1.0 / POOL2, 0.0)
    return jnp.where(r < ONE, one, two).astype(BF16)


def column_of(row):
    i = lax.broadcasted_iota(jnp.int32, (ROWS, ROWS), 0)
    j = lax.broadcasted_iota(jnp.int32, (ROWS, ROWS), 1)
    return jnp.sum(jnp.where(i == j, row, 0.0), axis=1, keepdims=True)


def row_of(column):
    i = lax.broadcasted_iota(jnp.int32, (ROWS, ROWS), 0)
    j = lax.broadcasted_iota(jnp.int32, (ROWS, ROWS), 1)
    return jnp.sum(jnp.where(i == j, column, 0.0), axis=0, keepdims=True)


def kernel(
    q_hbm, k_hbm, v_hbm, g_hbm, level_hbm, frame_hbm,
    att_hbm, dq_hbm, dk_hbm, dv_hbm,
    kv_own, q_two, g_two, kv_near, pooled, one_in, two_in, k_middle, v_middle, k_last, v_last,
    level_s, frame_v, near_bias, far_bias, weight, turned, mixed, stats,
    mixed_grad, att, dq, near_out, pool_out, two_out, sib_out, fold_out,
    pass_in, four_in, fold_in, near_back, one_back, two_back, sib_back, dk, dv,
    local_sem, send_sem, sib_recv, near_recv, one_recv, two_recv, stat_recv, pass_recv, fold_recv,
    back_near_recv, back_one_recv, back_two_recv, out_recv,
):
    blocks = lax.axis_size("seq")
    chips = blocks // 2
    heads = lax.axis_size("head")
    me = lax.axis_index("seq")
    lane = lax.axis_index("head")
    chip = me // 2
    core = me % 2
    other = 1 - core
    d = direction(core)

    def at(steps, c):
        return {"seq": ((chip + steps + chips) % chips) * 2 + c}

    sibling = {"seq": chip * 2 + other}

    def half(h):
        return pl.ds(pl.multiple_of(h * HALF, HALF), HALF)

    def remote(src, dst, send, recv, device):
        return pltpu.make_async_remote_copy(
            src_ref=src, dst_ref=dst, send_sem=send, recv_sem=recv, device_id=device, device_id_type=MESH
        )

    def inside(*steps, sided=()):
        away = [s for s in steps] + [s * d for s in sided]
        known = True
        for s in away:
            known = known & (chip + s >= 0) & (chip + s < chips)
        return (steps, sided), known

    def only(when, act):
        if when is None:
            act()
        else:
            pl.when(when[1])(act)

    sent = 0
    started = []

    def send(src, dst, recv, device, when=None):
        nonlocal sent
        copy = remote(src, dst, send_sem.at[sent], recv, device)
        sent += 1
        only(when, copy.start)
        started.append((copy, when))

    def flush():
        groups = {}
        for copy, when in started:
            groups.setdefault(when and when[0], (when, []))[1].append(copy)
        started.clear()
        for when, copies in groups.values():

            def wait_all(copies=copies):
                for copy in copies:
                    copy.wait_send()

            only(when, wait_all)

    def arrived(ref, sem, when=None):
        only(when, remote(ref, ref, sem, sem, sibling).wait_recv)

    @pl.when((chip < 6) | (chip >= chips - 6))
    def _():
        for ref in (one_in, two_in, pass_in, four_in, fold_in, near_back, one_back, two_back):
            ref[...] = jnp.zeros(ref.shape, ref.dtype)
        for s in (0, 3):
            kv_near[s] = jnp.zeros(kv_near.shape[1:], BF16)

    mine = pl.ds(pl.multiple_of(core * ROWS, ROWS), ROWS)
    theirs = pl.ds(pl.multiple_of(other * ROWS, ROWS), ROWS)
    k_rows, v_rows = pl.ds(0, ROWS), pl.ds(ROWS, ROWS)
    locals_in = [
        pltpu.make_async_copy(k_hbm, kv_own.at[k_rows], local_sem.at[0]),
        pltpu.make_async_copy(v_hbm, kv_own.at[v_rows], local_sem.at[1]),
        pltpu.make_async_copy(level_hbm, level_s, local_sem.at[2]),
        pltpu.make_async_copy(frame_hbm, frame_v, local_sem.at[3]),
        pltpu.make_async_copy(k_hbm.at[:, half(core)], kv_near.at[1 + core, k_rows], local_sem.at[4]),
        pltpu.make_async_copy(v_hbm.at[:, half(core)], kv_near.at[1 + core, v_rows], local_sem.at[5]),
        pltpu.make_async_copy(q_hbm.at[:, half(core)], q_two.at[mine], local_sem.at[6]),
        pltpu.make_async_copy(g_hbm.at[:, half(core)], g_two.at[mine], local_sem.at[7]),
    ]
    for copy in locals_in[:2]:
        copy.start()

    barrier = pltpu.get_barrier_semaphore()
    partners = [sibling]
    for k in range(1, heads):
        for c in (0, 1):
            partners.append({"seq": chip * 2 + c, "head": (lane + k) % heads})
    expected = len(partners)

    def greet(devices):
        for device in devices:
            pl.semaphore_signal(barrier, inc=1, device_id=device, device_id_type=MESH)

    for steps in (4, -4, 2, -2, 1, -1):
        when = inside(steps)
        only(when, lambda: greet([at(steps, 0), at(steps, 1)]))
        expected = expected + jnp.where(when[1], 2, 0)
    greet(partners)
    for copy in locals_in[2:]:
        copy.start()

    locals_in[0].wait()
    locals_in[1].wait()
    pool = pool_matrix()
    k_pool = dot(pool, kv_own[:ROWS])
    v_pool = dot(pool, kv_own[ROWS:])
    pooled[0 : 2 * ONE, :] = jnp.concatenate([k_pool[:ONE], v_pool[:ONE]], axis=0).astype(BF16)
    pooled[2 * ONE :, :] = jnp.concatenate([k_pool[ONE:], v_pool[ONE:]], axis=0).astype(BF16)

    pl.semaphore_wait(barrier, expected)

    def send_two(steps, side, spot):
        for h in (0, 1):
            send(
                pooled.at[pl.ds(2 * ONE, 2 * TWO), half(h)], two_in.at[side, spot],
                two_recv.at[side, spot], at(steps * d, h), inside(sided=(steps,)),
            )

    send_two(4, core, 5)
    send_two(-4, other, 4)
    send_two(2, core, 1)
    send_two(-2, other, 0)
    for h in (0, 1):
        send(
            pooled.at[:, half(h)], one_in.at[core * 2 + 1],
            one_recv.at[core * 2 + 1], at(-d, h), inside(sided=(-1,)),
        )
    send(kv_own.at[:, half(other)], kv_near.at[1 + core], sib_recv.at[0], sibling)
    send(q_hbm.at[:, half(other)], q_two.at[mine], sib_recv.at[2], sibling)
    for h in (0, 1):
        send(kv_own.at[:, half(h)], kv_near.at[3 - 3 * core], near_recv.at[core], at(d, h), inside(sided=(1,)))
    send(g_hbm.at[:, half(other)], g_two.at[mine], sib_recv.at[3], sibling)

    locals_in[2].wait()
    locals_in[3].wait()
    table = [level_s[0, i] for i in range(4)]
    spot = lax.broadcasted_iota(jnp.int32, (8, FAR), 1)
    row = jnp.full((8, FAR), MASKED, F32)

    def level_at(offset):
        choice = jnp.where(offset == -3, table[0], table[1])
        choice = jnp.where(offset == 2, table[2], choice)
        return jnp.where(offset == 3, table[3], choice)

    def slot_bias(rel, wanted, most, bias):
        offset = rel - core
        distance = jnp.abs(offset)
        block = 2 * chip + rel
        inside = (distance >= 2) & (distance <= most) & (block >= 0) & (block < blocks)
        chosen = (distance > REACH1) | (level_at(offset) == wanted)
        return jnp.where(inside & chosen, bias * LOG2E, MASKED)

    for s, rel in enumerate(REL_ONE):
        value = slot_bias(rel, 1, REACH1, math.log(POOL1))
        row = jnp.where((spot >= s * ONE) & (spot < (s + 1) * ONE), value, row)
    for s, rel in enumerate(REL_MIDDLE + REL_LAST):
        low = len(REL_ONE) * ONE + s * TWO
        value = slot_bias(rel, 2, REACH2, math.log(POOL2))
        row = jnp.where((spot >= low) & (spot < low + TWO), value, row)
    far_bias[core] = row
    send(far_bias.at[core], far_bias.at[core], sib_recv.at[4], sibling)

    lengths = frame_v[...].astype(F32)
    count = lengths.shape[1]
    i = lax.broadcasted_iota(jnp.int32, (count, count), 0)
    j = lax.broadcasted_iota(jnp.int32, (count, count), 1)
    ends_column = jnp.sum(jnp.where(j <= i, lengths, 0.0), axis=1, keepdims=True)
    ends_row = jnp.sum(jnp.where(i == j, ends_column, 0.0), axis=0, keepdims=True)
    start = (2 * chip - 1) * ROWS
    key_place = start + lax.broadcasted_iota(jnp.int32, (1, 4 * ROWS), 1)
    key_frame = jnp.sum(jnp.where(key_place.astype(F32) >= ends_column, 1.0, 0.0), axis=0, keepdims=True)
    key_inside = (key_place >= 0) & (key_place < blocks * ROWS)
    for b in (0, 1):
        place = start + (b + 1) * ROWS + lax.broadcasted_iota(jnp.int32, (ROWS, 1), 0)
        frame = jnp.sum(jnp.where(place.astype(F32) >= ends_row, 1.0, 0.0), axis=1, keepdims=True)
        matched = jnp.where(frame == key_frame, MATCHED_FRAME_ADD * LOG2E, 0.0)
        matched = jnp.where(key_inside, matched, MASKED)
        rows = slice(b * ROWS, (b + 1) * ROWS)
        near_bias[rows, OWN] = matched[:, ROWS : 3 * ROWS]
        near_bias[rows, SIDE] = matched[:, 3 * b * ROWS : (3 * b + 1) * ROWS]

    scale = LOG2E / math.sqrt(HEAD_DIM)
    columns = [slice(h * HEAD_DIM, (h + 1) * HEAD_DIM) for h in (0, 1)]
    first, second = slice(0, ROWS), slice(ROWS, 2 * ROWS)
    highs, totals, accs = [[], []], [None, None], [None, None]

    def far_of(part):
        low, high = part.start - MIDDLE.start, part.stop - MIDDLE.start
        shape = (ROWS, high - low)
        return jnp.concatenate([jnp.broadcast_to(far_bias[b, 0:1, low:high], shape) for b in (0, 1)], axis=0)

    def attend(h, part, scores, product):
        top = jnp.max(scores, axis=1, keepdims=True)
        if highs[h]:
            top = jnp.maximum(highs[h][-1], top)
        e = jnp.exp2(scores - top)
        weight[h, :, part] = e
        total = jnp.sum(e, axis=1, keepdims=True)
        rounded = e.astype(BF16)
        acc = product(rounded)
        if part in (OWN, SIDE):
            turned[h, part, :] = rounded.T
        if highs[h]:
            alpha = jnp.exp2(highs[h][-1] - top)
            total = totals[h] * alpha + total
            acc = accs[h] * alpha + acc
        highs[h].append(top)
        totals[h], accs[h] = total, acc

    rows_of = (first, second)

    def own_of(kind, h):
        return kv_near[1:3, rows_of[kind], columns[h]].reshape(2 * ROWS, HEAD_DIM)

    for side in (0, 1):
        sigma = direction(side)
        four, two = -4 * sigma, -2 * sigma
        for s in (4, 5):
            arrived(two_in.at[side, s], two_recv.at[side, s], inside(four))
        send(two_in.at[side, 5], two_in.at[side, 8], two_recv.at[side, 8], at(2 * sigma, core), inside(four, 2 * sigma))
        send(
            two_in.at[side, pl.ds(4, 2)], two_in.at[side, pl.ds(6, 2)],
            two_recv.at[side, 6], at(sigma, core), inside(four, sigma),
        )
        for s in (0, 1):
            arrived(two_in.at[side, s], two_recv.at[side, s], inside(two))
        send(
            two_in.at[side, pl.ds(0, 2)], two_in.at[side, pl.ds(2, 2)],
            two_recv.at[side, 2], at(sigma, core), inside(two, sigma),
        )

    locals_in[4].wait()
    locals_in[6].wait()
    locals_in[5].wait()
    arrived(kv_near.at[1 + other], sib_recv.at[0])
    arrived(q_two.at[theirs], sib_recv.at[2])
    for h in (0, 1):
        scores = dot_nt(q_two[:, columns[h]], own_of(0, h)) * scale + near_bias[:, OWN]
        attend(h, OWN, scores, lambda e: dot(e, own_of(1, h)))

    arrived(kv_near.at[3], near_recv.at[0], inside(1))
    arrived(kv_near.at[0], near_recv.at[1], inside(-1))
    near_pools = [(dot(pool, kv_near[s, first]), dot(pool, kv_near[s, second])) for s in (0, 3)]
    ones_only = pl.ds(0, 2 * ONE)
    for i, side in ((0, 1), (1, 0)):
        sigma = direction(side)
        fold_out[i] = jnp.concatenate([p[:ONE] for p in near_pools[i]], axis=0).astype(BF16)
        send(
            fold_out.at[i], one_in.at[side * 2, ones_only],
            one_recv.at[side * 2], at(sigma, core), inside(-sigma, sigma),
        )
    for h in (0, 1):
        query = q_two[:, columns[h]]
        scores = jnp.concatenate(
            [dot_nt(query[first], kv_near[0, first, columns[h]]), dot_nt(query[second], kv_near[3, first, columns[h]])], axis=0
        )
        attend(
            h, SIDE, scores * scale + near_bias[:, SIDE],
            lambda e: jnp.concatenate(
                [dot(e[first], kv_near[0, second, columns[h]]), dot(e[second], kv_near[3, second, columns[h]])], axis=0
            ),
        )

    for side in (0, 1):
        sigma = direction(side)
        arrived(one_in.at[side * 2, ones_only], one_recv.at[side * 2], inside(-2 * sigma))
        arrived(one_in.at[side * 2 + 1], one_recv.at[side * 2 + 1], inside(sigma))
    arrived(far_bias.at[other], sib_recv.at[4])
    nearest = [two_in[0, 1], one_in[1, 2 * ONE :], two_in[1, 1], one_in[3, 2 * ONE :]]
    nearest = [x.astype(F32) for x in nearest]
    for kind, middle in ((0, k_middle), (1, v_middle)):
        ones = slice(kind * ONE, (kind + 1) * ONE)
        rows = slice(kind * TWO, (kind + 1) * TWO)
        for s in range(4):
            middle[s * ONE : (s + 1) * ONE] = one_in[s, ones]
        for i in (0, 1):
            middle[(4 + i) * ONE : (5 + i) * ONE] = fold_out[i, ones]
        parts = [x[rows] for x in nearest] + [p[kind][ONE:] for p in near_pools]
        parts += [two_in[side, 0].astype(F32)[rows] for side in (0, 1)]
        middle[6 * ONE :] = jnp.concatenate(parts, axis=0).astype(BF16)
    for h in (0, 1):
        scores = dot_nt(q_two[:, columns[h]], k_middle[:, columns[h]]) * scale + far_of(MIDDLE)
        attend(h, MIDDLE, scores, lambda e: dot(e, v_middle[:, columns[h]]))

    for side in (0, 1):
        sigma = direction(side)
        for s, steps in ((2, 3), (6, 5)):
            arrived(two_in.at[side, pl.ds(s, 2)], two_recv.at[side, s], inside(-steps * sigma))
        arrived(two_in.at[side, 8], two_recv.at[side, 8], inside(-6 * sigma))
    twos = [two_in[side, 2:].astype(F32) for side in (0, 1)]
    for kind, last in ((0, k_last), (1, v_last)):
        rows = slice(kind * TWO, (kind + 1) * TWO)
        parts = [t[:, rows].reshape(7 * TWO, HALF) for t in twos] + [jnp.zeros((2 * TWO, HALF), F32)]
        last[...] = jnp.concatenate(parts, axis=0).astype(BF16)
    for h in (0, 1):
        scores = dot_nt(q_two[:, columns[h]], k_last[:, columns[h]]) * scale + far_of(LAST)
        attend(h, LAST, scores, lambda e: dot(e, v_last[:, columns[h]]))
    inverse_totals = [1.0 / totals[h] for h in (0, 1)]
    for h in (0, 1):
        mixed[:, columns[h]] = accs[h] * inverse_totals[h]

    locals_in[7].wait()
    arrived(g_two.at[theirs], sib_recv.at[3])
    mates = 2 * heads
    place = lane * 2 + core
    value = mixed[...]
    energy = jnp.sum(value * value, axis=1, keepdims=True)
    product = jnp.sum(value * g_two[...].astype(F32), axis=1, keepdims=True)
    stats[place] = jnp.concatenate(
        [row_of(energy[:ROWS]), row_of(energy[ROWS:]), row_of(product[:ROWS]), row_of(product[ROWS:]), jnp.zeros((4, ROWS), F32)],
        axis=0,
    )
    for k in range(1, mates):
        to = (place + k) % mates
        send(stats.at[place], stats.at[place], stat_recv.at[place], {"seq": chip * 2 + to % 2, "head": to // 2})
    factors = [[], []]
    for h in (0, 1):
        for index, part in enumerate((OWN, SIDE, MIDDLE, LAST)):
            factors[h].append(jnp.exp2(highs[h][index] - highs[h][-1]) * inverse_totals[h])
            if part in (MIDDLE, LAST):
                turned[h, part, :] = weight[h, :, part].astype(BF16).T
    for k in range(1, mates):
        source = (place + k) % mates
        arrived(stats.at[source], stat_recv.at[source])
    summed = stats[0]
    for k in range(1, mates):
        summed = summed + stats[k]
    width = HEADS * HEAD_DIM
    deltas = [[], []]
    for b, rows in ((0, first), (1, second)):
        inverse = lax.rsqrt(column_of(summed[b : b + 1]) / width + NORM_EPSILON)
        agreement = column_of(summed[2 + b : 3 + b]) * inverse
        normed = mixed[rows] * inverse
        att[rows] = normed.astype(BF16)
        grad = inverse * (g_two[rows].astype(F32) - normed * (agreement / width))
        mixed_grad[rows] = grad
        both = grad.astype(BF16).astype(F32) * mixed[rows]
        for h in (0, 1):
            deltas[h].append(jnp.sum(both[:, columns[h]], axis=1, keepdims=True))
    deltas = [jnp.concatenate(deltas[h], axis=0) for h in (0, 1)]

    unscale = 1.0 / math.sqrt(HEAD_DIM)
    query_grads = [None, None]

    def scaled(h, part):
        factor = factors[h][(OWN, SIDE, MIDDLE, LAST).index(part)]
        return (mixed_grad[:, columns[h]] * factor).astype(BF16), deltas[h] * factor

    def slopes_of(h, part, products, delta):
        return (weight[h, :, part] * (products - delta)).astype(BF16)

    def plain_backward(part, k_ref, v_ref):
        k_parts, v_parts = [], []
        for h in (0, 1):
            grad, delta = scaled(h, part)
            slopes = slopes_of(h, part, dot_nt(grad, v_ref(h)), delta)
            change = dot(slopes, k_ref(h))
            query_grads[h] = change if query_grads[h] is None else query_grads[h] + change
            k_parts.append(dot_tn(slopes, q_two[:, columns[h]]) * unscale)
            v_parts.append(dot(turned[h, part, :], grad))
        return jnp.concatenate(k_parts, axis=1), jnp.concatenate(v_parts, axis=1)

    def two_rows(pair, low):
        return jnp.concatenate([g[low : low + TWO] for g in pair], axis=0)

    last = plain_backward(LAST, lambda h: k_last[:, columns[h]], lambda h: v_last[:, columns[h]])
    for side in (0, 1):
        sigma = direction(side)
        for s in (1, 2, 5, 6, 7):
            two_out[side, s] = two_rows(last, (side * 7 + s - 1) * TWO).astype(BF16)
        send(
            two_out.at[side, pl.ds(5, 2)], pass_in.at[side, pl.ds(0, 2)],
            pass_recv.at[side, 0], at(-sigma, core), inside(-5 * sigma),
        )
        send(two_out.at[side, 7], pass_in.at[side, 4], pass_recv.at[side, 2], at(-2 * sigma, core), inside(-6 * sigma))
        send(
            two_out.at[side, pl.ds(1, 2)], pass_in.at[side, pl.ds(2, 2)],
            pass_recv.at[side, 1], at(-sigma, core), inside(-3 * sigma),
        )
    out_att = pltpu.make_async_copy(att.at[mine], att_hbm.at[:, half(core)], local_sem.at[8])
    out_att.start()
    send(att.at[theirs], att_hbm.at[:, half(core)], out_recv.at[0], sibling)

    middle = plain_backward(MIDDLE, lambda h: k_middle[:, columns[h]], lambda h: v_middle[:, columns[h]])
    for s in range(4):
        for kind in (0, 1):
            pool_out[s, kind * ONE : (kind + 1) * ONE] = middle[kind][s * ONE : (s + 1) * ONE].astype(BF16)
    for b in (0, 1):
        s = 2 * b + 1
        pool_out[s, 2 * ONE :] = two_rows(middle, 6 * ONE + s * TWO).astype(BF16)
        send(pool_out.at[s], one_back.at[core], back_one_recv.at[core], at(direction(b), b), inside(direction(b)))
    for side in (0, 1):
        sigma = direction(side)
        send(
            pool_out.at[2 * side, ones_only], fold_in.at[side],
            fold_recv.at[side], at(-sigma, core), inside(-2 * sigma),
        )

    spread = spread_matrix()
    k_sides, v_sides = [[], []], [[], []]
    for h in (0, 1):
        grad, delta = scaled(h, SIDE)
        query = q_two[:, columns[h]]
        products = jnp.concatenate(
            [dot_nt(grad[first], kv_near[0, second, columns[h]]), dot_nt(grad[second], kv_near[3, second, columns[h]])], axis=0
        )
        slopes = slopes_of(h, SIDE, products, delta)
        query_grads[h] = query_grads[h] + jnp.concatenate(
            [dot(slopes[first], kv_near[0, first, columns[h]]), dot(slopes[second], kv_near[3, first, columns[h]])], axis=0
        )
        for b, rows in ((0, second), (1, first)):
            k_sides[b].append(dot_tn(slopes[rows], query[rows]) * unscale)
            v_sides[b].append(dot(turned[h, SIDE, rows], grad[rows]))
    for side in (0, 1):
        sigma = direction(side)
        four = -4 * sigma
        arrived(pass_in.at[side, pl.ds(0, 2)], pass_recv.at[side, 0], inside(sigma, four))
        arrived(pass_in.at[side, 4], pass_recv.at[side, 2], inside(2 * sigma, four))
        passed = [pass_in[side, s].astype(F32) for s in (0, 1, 4)]
        two_out[side, 3] = (two_rows(last, (side * 7 + 2) * TWO) + passed[0]).astype(BF16)
        two_out[side, 4] = (two_rows(last, (side * 7 + 3) * TWO) + passed[1] + passed[2]).astype(BF16)
        send(two_out.at[side, pl.ds(3, 2)], four_in.at[side], pass_recv.at[side, 3], at(-2 * sigma, core), inside(four))

    for b in (0, 1):
        p = 5 - b
        sigma = direction(b)
        arrived(fold_in.at[b], fold_recv.at[b], inside(sigma, -sigma))
        folded = fold_in[b].astype(F32)
        for kind, sides in ((0, k_sides), (1, v_sides)):
            pools = middle[kind]
            small = jnp.concatenate(
                [pools[p * ONE : (p + 1) * ONE] + folded[kind * ONE : (kind + 1) * ONE], pools[6 * ONE + p * TWO : 6 * ONE + (p + 1) * TWO]], axis=0
            )
            near_out[b, kind * ROWS : (kind + 1) * ROWS] = (
                jnp.concatenate(sides[b], axis=1) + dot(spread, small.astype(BF16))
            ).astype(BF16)
        send(near_out.at[b], near_back.at[core], back_near_recv.at[core], at(-direction(b), b), inside(-direction(b)))

    own = plain_backward(OWN, lambda h: own_of(0, h), lambda h: own_of(1, h))
    for kind in (0, 1):
        sib_out[kind * ROWS : (kind + 1) * ROWS] = jnp.where(core == 0, own[kind][second], own[kind][first]).astype(BF16)
    send(sib_out, sib_back, out_recv.at[1], sibling)
    for h in (0, 1):
        dq[:, columns[h]] = (query_grads[h] * unscale).astype(BF16)
    out_dq = pltpu.make_async_copy(dq.at[mine], dq_hbm.at[:, half(core)], local_sem.at[9])
    out_dq.start()
    send(dq.at[theirs], dq_hbm.at[:, half(core)], out_recv.at[2], sibling)

    for side in (0, 1):
        sigma = direction(side)
        two = -2 * sigma
        arrived(pass_in.at[side, pl.ds(2, 2)], pass_recv.at[side, 1], inside(sigma, two))
        arrived(four_in.at[side], pass_recv.at[side, 3], inside(2 * sigma, two))
        passed = pass_in[side, 2:4].astype(F32) + four_in[side].astype(F32)
        two_out[side, 0] = (two_rows(middle, 6 * ONE + (6 + side) * TWO) + passed[0]).astype(BF16)
        two_out[side, 8] = (two_rows(middle, 6 * ONE + 2 * side * TWO) + passed[1]).astype(BF16)
        send(two_out.at[side, 0], two_back.at[core, 0], back_two_recv.at[core, 0], at(two, 1 - side), inside(two))
        send(two_out.at[side, 8], two_back.at[core, 1], back_two_recv.at[core, 1], at(two, side), inside(two))

    arrived(sib_back, out_recv.at[1])
    mine_grads = [jnp.where(core == 0, own[kind][first], own[kind][second]) for kind in (0, 1)]
    bases = {}
    for h in (0, 1):
        arrived(one_back.at[h], back_one_recv.at[h], inside(sided=(-1,)))
        for j, steps in enumerate((-2, 2)):
            arrived(two_back.at[h, j], back_two_recv.at[h, j], inside(sided=(steps,)))
        ones = one_back[h].astype(F32)
        twos = ones[2 * ONE :] + two_back[h, 0].astype(F32) + two_back[h, 1].astype(F32)
        for kind in (0, 1):
            rows = slice(kind * ROWS, (kind + 1) * ROWS)
            small = jnp.concatenate([ones[kind * ONE : (kind + 1) * ONE], twos[kind * TWO : (kind + 1) * TWO]], axis=0)
            grads = jnp.where(core == h, mine_grads[kind], sib_back[rows].astype(F32))
            bases[h, kind] = grads + dot(spread, small.astype(BF16))
    arrived(att_hbm.at[:, half(other)], out_recv.at[0])
    arrived(dq_hbm.at[:, half(other)], out_recv.at[2])
    flush()
    for h in (0, 1):
        arrived(near_back.at[h], back_near_recv.at[h], inside(sided=(1,)))
    outs = [out_att, out_dq]
    for kind, out, out_hbm in ((0, dk, dk_hbm), (1, dv, dv_hbm)):
        rows = slice(kind * ROWS, (kind + 1) * ROWS)
        for h in (0, 1):
            out[:, h * HALF : (h + 1) * HALF] = (bases[h, kind] + near_back[h, rows].astype(F32)).astype(BF16)
        outs.append(pltpu.make_async_copy(out, out_hbm, local_sem.at[10 + kind]))
        outs[-1].start()
    for copy in outs:
        copy.wait()


def write_out(*refs):
    *arrays, sems = refs
    copies = [pltpu.make_async_copy(arrays[i], arrays[4 + i], sems.at[i]) for i in range(4)]
    for copy in copies:
        copy.start()
    for copy in copies:
        copy.wait()


def body(queries, keys, values, out_grad, level_choice, frame_lengths):
    rows, width = queries.shape
    vmem = pltpu.VMEM
    dma = pltpu.SemaphoreType.DMA
    out = jax.ShapeDtypeStruct((rows, width), BF16)
    limit = 40 * 1024 * 1024
    arrays = (queries, keys, values, out_grad, level_choice, frame_lengths.reshape(1, -1))
    results = pl.pallas_call(
        kernel,
        out_shape=(out, out, out, out),
        in_specs=[pl.BlockSpec(memory_space=pl.ANY)] * 6,
        out_specs=(pl.BlockSpec(memory_space=pl.ANY),) * 4,
        scratch_shapes=[
            vmem((2 * ROWS, width), BF16),
            vmem((2 * ROWS, HALF), BF16),
            vmem((2 * ROWS, HALF), BF16),
            vmem((4, 2 * ROWS, HALF), BF16),
            vmem((POOLED, width), BF16),
            vmem((4, POOLED, HALF), BF16),
            vmem((2, 9, 2 * TWO, HALF), BF16),
            vmem((256, HALF), BF16),
            vmem((256, HALF), BF16),
            vmem((128, HALF), BF16),
            vmem((128, HALF), BF16),
            pltpu.SMEM((1, 4), jnp.int32),
            vmem((1, 64), jnp.int32),
            vmem((2 * ROWS, 384), F32),
            vmem((2, 8, FAR), F32),
            vmem((2, 2 * ROWS, 768), F32),
            vmem((2, 768, 2 * ROWS), BF16),
            vmem((2 * ROWS, HALF), F32),
            vmem((8, 8, ROWS), F32),
            vmem((2 * ROWS, HALF), F32),
            vmem((2 * ROWS, HALF), BF16),
            vmem((2 * ROWS, HALF), BF16),
            vmem((2, 2 * ROWS, HALF), BF16),
            vmem((4, POOLED, HALF), BF16),
            vmem((2, 9, 2 * TWO, HALF), BF16),
            vmem((2 * ROWS, HALF), BF16),
            vmem((2, 2 * ONE, HALF), BF16),
            vmem((2, 5, 2 * TWO, HALF), BF16),
            vmem((2, 2, 2 * TWO, HALF), BF16),
            vmem((2, 2 * ONE, HALF), BF16),
            vmem((2, 2 * ROWS, HALF), BF16),
            vmem((2, POOLED, HALF), BF16),
            vmem((2, 2, 2 * TWO, HALF), BF16),
            vmem((2 * ROWS, HALF), BF16),
            vmem((ROWS, width), BF16),
            vmem((ROWS, width), BF16),
            dma((12,)),
            dma((64,)),
            dma((5,)),
            dma((2,)),
            dma((4,)),
            dma((2, 9)),
            dma((8,)),
            dma((2, 4)),
            dma((2,)),
            dma((2,)),
            dma((2,)),
            dma((2, 2)),
            dma((3,)),
        ],
        compiler_params=pltpu.CompilerParams(collective_id=0, has_side_effects=True, vmem_limit_bytes=limit),
        cost_estimate=pl.CostEstimate(flops=700_000_000, bytes_accessed=1_100_000, transcendentals=400_000),
    )(*[pltpu.with_memory_space_constraint(array, pltpu.HBM) for array in arrays])
    return pl.pallas_call(
        write_out,
        out_shape=(out, out, out, out),
        in_specs=[pl.BlockSpec(memory_space=pl.ANY)] * 4,
        out_specs=(pl.BlockSpec(memory_space=pl.ANY),) * 4,
        scratch_shapes=[dma((4,))],
        compiler_params=pltpu.CompilerParams(vmem_limit_bytes=limit),
        cost_estimate=pl.CostEstimate(flops=0, bytes_accessed=1_100_000, transcendentals=0),
    )(*results)


def solution(mesh):
    in_specs = (
        P("seq", "head"),
        P("seq", "head"),
        P("seq", "head"),
        P("seq", "head"),
        P("seq", None),
        P(),
    )
    out_specs = (P("seq", "head"), P("seq", "head"), P("seq", "head"), P("seq", "head"))
    return jax.shard_map(body, mesh=mesh, in_specs=in_specs, out_specs=out_specs, check_vma=False)
```

```python
import math

import jax
import jax.numpy as jnp
from jax import lax
from jax.experimental import pallas as pl
from jax.experimental.pallas import tpu as pltpu
from jax.sharding import PartitionSpec as P

HEADS = 16
HEAD_DIM = 128
POOL1 = 4
POOL2 = 16
REACH1 = 3
REACH2 = 11
MATCHED_FRAME_ADD = 1.0
NORM_EPSILON = 1e-06

MESH = pl.DeviceIdType.MESH
F32 = jnp.float32
BF16 = jnp.bfloat16
LOG2E = math.log2(math.e)
MASKED = -1e30

ROWS = 128
HALF = 256
ONE = ROWS // POOL1
TWO = ROWS // POOL2
POOLED = 2 * (ONE + TWO)
NEAR = 3 * ROWS
FAR = 384

STEPS_ONE = (2, -1)


def direction(b):
    return 2 * b - 1


REL_ONE = [-2 * steps * direction(b) + b for b in (0, 1) for steps in STEPS_ONE] + [-1, 2]


def relative_two(side):
    sigma = direction(side)
    spots = [(2, 1 - side), (3, 1 - side), (3, side), (4, 1 - side), (4, side), (5, 1 - side), (5, side), (6, side)]
    return [-2 * k * sigma + b for k, b in spots]


REL_TWO = [relative_two(0), relative_two(1)]
REL_MIDDLE = REL_ONE + [REL_TWO[0][0], REL_TWO[1][0]]
REL_LAST = REL_TWO[0][1:] + REL_TWO[1][1:]
OWN, SIDE, MIDDLE, LAST = slice(0, 256), slice(256, 384), slice(384, 640), slice(640, 768)


def dot_nt(a, b):
    return lax.dot_general(a, b, (((1,), (1,)), ((), ())), preferred_element_type=F32)


def dot_tn(a, b):
    return lax.dot_general(a, b, (((0,), (0,)), ((), ())), preferred_element_type=F32)


def dot(a, b):
    return jnp.dot(a, b, preferred_element_type=F32)


def pool_matrix():
    r = lax.broadcasted_iota(jnp.int32, (ONE + TWO, ROWS), 0)
    t = lax.broadcasted_iota(jnp.int32, (ONE + TWO, ROWS), 1)
    one = jnp.where((t >> 2) == r, 1.0 / POOL1, 0.0)
    two = jnp.where((t >> 4) == r - ONE, 1.0 / POOL2, 0.0)
    return jnp.where(r < ONE, one, two).astype(BF16)


def spread_matrix():
    t = lax.broadcasted_iota(jnp.int32, (ROWS, ONE + TWO), 0)
    r = lax.broadcasted_iota(jnp.int32, (ROWS, ONE + TWO), 1)
    one = jnp.where((t >> 2) == r, 1.0 / POOL1, 0.0)
    two = jnp.where((t >> 4) == r - ONE, 1.0 / POOL2, 0.0)
    return jnp.where(r < ONE, one, two).astype(BF16)


def column_of(row):
    i = lax.broadcasted_iota(jnp.int32, (ROWS, ROWS), 0)
    j = lax.broadcasted_iota(jnp.int32, (ROWS, ROWS), 1)
    return jnp.sum(jnp.where(i == j, row, 0.0), axis=1, keepdims=True)


def row_of(column):
    i = lax.broadcasted_iota(jnp.int32, (ROWS, ROWS), 0)
    j = lax.broadcasted_iota(jnp.int32, (ROWS, ROWS), 1)
    return jnp.sum(jnp.where(i == j, column, 0.0), axis=0, keepdims=True)


def kernel(
    q_hbm, k_hbm, v_hbm, g_hbm, level_hbm, frame_hbm,
    att_hbm, dq_hbm, dk_hbm, dv_hbm,
    kv_own, q_two, g_two, kv_near, pooled, one_in, two_in, k_middle, v_middle, k_last, v_last,
    level_s, frame_v, near_bias, far_bias, weight, turned, mixed, stats,
    mixed_grad, att, dq, near_out, pool_out, two_out, sib_out,
    pass_in, four_in, near_back, one_back, two_back, sib_back, dk, dv,
    local_sem, send_sem, sib_recv, near_recv, one_recv, two_recv, stat_recv, pass_recv,
    back_near_recv, back_one_recv, back_two_recv, out_recv,
):
    blocks = lax.axis_size("seq")
    chips = blocks // 2
    heads = lax.axis_size("head")
    me = lax.axis_index("seq")
    lane = lax.axis_index("head")
    chip = me // 2
    core = me % 2
    other = 1 - core
    d = direction(core)

    def at(steps, c):
        return {"seq": ((chip + steps + chips) % chips) * 2 + c}

    sibling = {"seq": chip * 2 + other}

    def half(h):
        return pl.ds(pl.multiple_of(h * HALF, HALF), HALF)

    def remote(src, dst, send, recv, device):
        return pltpu.make_async_remote_copy(
            src_ref=src, dst_ref=dst, send_sem=send, recv_sem=recv, device_id=device, device_id_type=MESH
        )

    def inside(*steps, sided=()):
        away = [s for s in steps] + [s * d for s in sided]
        known = True
        for s in away:
            known = known & (chip + s >= 0) & (chip + s < chips)
        return (steps, sided), known

    def only(when, act):
        if when is None:
            act()
        else:
            pl.when(when[1])(act)

    sent = 0
    started = []

    def send(src, dst, recv, device, when=None):
        nonlocal sent
        copy = remote(src, dst, send_sem.at[sent], recv, device)
        sent += 1
        only(when, copy.start)
        started.append((copy, when))

    def flush():
        groups = {}
        for copy, when in started:
            groups.setdefault(when and when[0], (when, []))[1].append(copy)
        started.clear()
        for when, copies in groups.values():

            def wait_all(copies=copies):
                for copy in copies:
                    copy.wait_send()

            only(when, wait_all)

    def arrived(ref, sem, when=None):
        only(when, remote(ref, ref, sem, sem, sibling).wait_recv)

    @pl.when((chip < 6) | (chip >= chips - 6))
    def _():
        for ref in (one_in, two_in, pass_in, four_in, near_back, one_back, two_back):
            ref[...] = jnp.zeros(ref.shape, ref.dtype)
        for s in (0, 3):
            kv_near[s] = jnp.zeros(kv_near.shape[1:], BF16)

    mine = pl.ds(pl.multiple_of(core * ROWS, ROWS), ROWS)
    theirs = pl.ds(pl.multiple_of(other * ROWS, ROWS), ROWS)
    k_rows, v_rows = pl.ds(0, ROWS), pl.ds(ROWS, ROWS)
    locals_in = [
        pltpu.make_async_copy(k_hbm, kv_own.at[k_rows], local_sem.at[0]),
        pltpu.make_async_copy(v_hbm, kv_own.at[v_rows], local_sem.at[1]),
        pltpu.make_async_copy(level_hbm, level_s, local_sem.at[2]),
        pltpu.make_async_copy(frame_hbm, frame_v, local_sem.at[3]),
        pltpu.make_async_copy(k_hbm.at[:, half(core)], kv_near.at[1 + core, k_rows], local_sem.at[4]),
        pltpu.make_async_copy(v_hbm.at[:, half(core)], kv_near.at[1 + core, v_rows], local_sem.at[5]),
        pltpu.make_async_copy(q_hbm.at[:, half(core)], q_two.at[mine], local_sem.at[6]),
        pltpu.make_async_copy(g_hbm.at[:, half(core)], g_two.at[mine], local_sem.at[7]),
    ]
    for copy in locals_in[:2]:
        copy.start()

    barrier = pltpu.get_barrier_semaphore()
    partners = [sibling]
    for k in range(1, heads):
        for c in (0, 1):
            partners.append({"seq": chip * 2 + c, "head": (lane + k) % heads})
    expected = len(partners)

    def greet(devices):
        for device in devices:
            pl.semaphore_signal(barrier, inc=1, device_id=device, device_id_type=MESH)

    for steps in (4, -4, 2, -2, 1, -1):
        when = inside(steps)
        only(when, lambda: greet([at(steps, 0), at(steps, 1)]))
        expected = expected + jnp.where(when[1], 2, 0)
    greet(partners)
    for copy in locals_in[2:]:
        copy.start()

    locals_in[0].wait()
    locals_in[1].wait()
    pool = pool_matrix()
    k_pool = dot(pool, kv_own[:ROWS])
    v_pool = dot(pool, kv_own[ROWS:])
    pooled[0 : 2 * ONE, :] = jnp.concatenate([k_pool[:ONE], v_pool[:ONE]], axis=0).astype(BF16)
    pooled[2 * ONE :, :] = jnp.concatenate([k_pool[ONE:], v_pool[ONE:]], axis=0).astype(BF16)

    pl.semaphore_wait(barrier, expected)

    def send_two(steps, side, spot):
        for h in (0, 1):
            send(
                pooled.at[pl.ds(2 * ONE, 2 * TWO), half(h)], two_in.at[side, spot],
                two_recv.at[side, spot], at(steps * d, h), inside(sided=(steps,)),
            )

    send_two(4, core, 5)
    send_two(-4, other, 4)
    send_two(2, core, 1)
    send_two(-2, other, 0)
    send(kv_own.at[:, half(other)], kv_near.at[1 + core], sib_recv.at[0], sibling)
    send(q_hbm.at[:, half(other)], q_two.at[mine], sib_recv.at[2], sibling)
    for h in (0, 1):
        send(kv_own.at[:, half(h)], kv_near.at[3 - 3 * core], near_recv.at[core], at(d, h), inside(sided=(1,)))
    for h in (0, 1):
        send(
            pooled.at[:, half(h)], one_in.at[core * 2 + 1],
            one_recv.at[core * 2 + 1], at(-d, h), inside(sided=(-1,)),
        )
    ones_only = pl.ds(0, 2 * ONE)
    for h in (0, 1):
        send(
            pooled.at[ones_only, half(h)], one_in.at[core * 2, ones_only],
            one_recv.at[core * 2], at(2 * d, h), inside(sided=(2,)),
        )

    locals_in[2].wait()
    locals_in[3].wait()
    table = [level_s[0, i] for i in range(4)]
    spot = lax.broadcasted_iota(jnp.int32, (8, FAR), 1)
    row = jnp.full((8, FAR), MASKED, F32)

    def level_at(offset):
        choice = jnp.where(offset == -3, table[0], table[1])
        choice = jnp.where(offset == 2, table[2], choice)
        return jnp.where(offset == 3, table[3], choice)

    def slot_bias(rel, wanted, most, bias):
        offset = rel - core
        distance = jnp.abs(offset)
        block = 2 * chip + rel
        inside = (distance >= 2) & (distance <= most) & (block >= 0) & (block < blocks)
        chosen = (distance > REACH1) | (level_at(offset) == wanted)
        return jnp.where(inside & chosen, bias * LOG2E, MASKED)

    for s, rel in enumerate(REL_ONE):
        value = slot_bias(rel, 1, REACH1, math.log(POOL1))
        row = jnp.where((spot >= s * ONE) & (spot < (s + 1) * ONE), value, row)
    for s, rel in enumerate(REL_MIDDLE + REL_LAST):
        low = len(REL_ONE) * ONE + s * TWO
        value = slot_bias(rel, 2, REACH2, math.log(POOL2))
        row = jnp.where((spot >= low) & (spot < low + TWO), value, row)
    far_bias[core] = row
    send(far_bias.at[core], far_bias.at[core], sib_recv.at[4], sibling)

    lengths = frame_v[...].astype(F32)
    count = lengths.shape[1]
    i = lax.broadcasted_iota(jnp.int32, (count, count), 0)
    j = lax.broadcasted_iota(jnp.int32, (count, count), 1)
    ends_column = jnp.sum(jnp.where(j <= i, lengths, 0.0), axis=1, keepdims=True)
    ends_row = jnp.sum(jnp.where(i == j, ends_column, 0.0), axis=0, keepdims=True)
    start = (2 * chip - 1) * ROWS
    key_place = start + lax.broadcasted_iota(jnp.int32, (1, 4 * ROWS), 1)
    key_frame = jnp.sum(jnp.where(key_place.astype(F32) >= ends_column, 1.0, 0.0), axis=0, keepdims=True)
    key_inside = (key_place >= 0) & (key_place < blocks * ROWS)
    for b in (0, 1):
        place = start + (b + 1) * ROWS + lax.broadcasted_iota(jnp.int32, (ROWS, 1), 0)
        frame = jnp.sum(jnp.where(place.astype(F32) >= ends_row, 1.0, 0.0), axis=1, keepdims=True)
        matched = jnp.where(frame == key_frame, MATCHED_FRAME_ADD * LOG2E, 0.0)
        matched = jnp.where(key_inside, matched, MASKED)
        rows = slice(b * ROWS, (b + 1) * ROWS)
        near_bias[rows, OWN] = matched[:, ROWS : 3 * ROWS]
        near_bias[rows, SIDE] = matched[:, 3 * b * ROWS : (3 * b + 1) * ROWS]

    scale = LOG2E / math.sqrt(HEAD_DIM)
    columns = [slice(h * HEAD_DIM, (h + 1) * HEAD_DIM) for h in (0, 1)]
    first, second = slice(0, ROWS), slice(ROWS, 2 * ROWS)
    highs, totals, accs = [[], []], [None, None], [None, None]

    def far_of(part):
        low, high = part.start - MIDDLE.start, part.stop - MIDDLE.start
        shape = (ROWS, high - low)
        return jnp.concatenate([jnp.broadcast_to(far_bias[b, 0:1, low:high], shape) for b in (0, 1)], axis=0)

    def attend(h, part, scores, product):
        top = jnp.max(scores, axis=1, keepdims=True)
        if highs[h]:
            top = jnp.maximum(highs[h][-1], top)
        e = jnp.exp2(scores - top)
        weight[h, :, part] = e
        total = jnp.sum(e, axis=1, keepdims=True)
        rounded = e.astype(BF16)
        acc = product(rounded)
        if part in (OWN, SIDE):
            turned[h, part, :] = rounded.T
        if highs[h]:
            alpha = jnp.exp2(highs[h][-1] - top)
            total = totals[h] * alpha + total
            acc = accs[h] * alpha + acc
        highs[h].append(top)
        totals[h], accs[h] = total, acc

    rows_of = (first, second)

    def own_of(kind, h):
        return kv_near[1:3, rows_of[kind], columns[h]].reshape(2 * ROWS, HEAD_DIM)

    for side in (0, 1):
        sigma = direction(side)
        four, two = -4 * sigma, -2 * sigma
        for s in (4, 5):
            arrived(two_in.at[side, s], two_recv.at[side, s], inside(four))
        send(two_in.at[side, 5], two_in.at[side, 8], two_recv.at[side, 8], at(2 * sigma, core), inside(four, 2 * sigma))
        send(
            two_in.at[side, pl.ds(4, 2)], two_in.at[side, pl.ds(6, 2)],
            two_recv.at[side, 6], at(sigma, core), inside(four, sigma),
        )
        for s in (0, 1):
            arrived(two_in.at[side, s], two_recv.at[side, s], inside(two))
        send(
            two_in.at[side, pl.ds(0, 2)], two_in.at[side, pl.ds(2, 2)],
            two_recv.at[side, 2], at(sigma, core), inside(two, sigma),
        )

    send(g_hbm.at[:, half(other)], g_two.at[mine], sib_recv.at[3], sibling)

    locals_in[4].wait()
    locals_in[6].wait()
    locals_in[5].wait()
    arrived(kv_near.at[1 + other], sib_recv.at[0])
    arrived(q_two.at[theirs], sib_recv.at[2])
    for h in (0, 1):
        scores = dot_nt(q_two[:, columns[h]], own_of(0, h)) * scale + near_bias[:, OWN]
        attend(h, OWN, scores, lambda e: dot(e, own_of(1, h)))

    arrived(kv_near.at[3], near_recv.at[0], inside(1))
    arrived(kv_near.at[0], near_recv.at[1], inside(-1))
    for h in (0, 1):
        query = q_two[:, columns[h]]
        scores = jnp.concatenate(
            [dot_nt(query[first], kv_near[0, first, columns[h]]), dot_nt(query[second], kv_near[3, first, columns[h]])], axis=0
        )
        attend(
            h, SIDE, scores * scale + near_bias[:, SIDE],
            lambda e: jnp.concatenate(
                [dot(e[first], kv_near[0, second, columns[h]]), dot(e[second], kv_near[3, second, columns[h]])], axis=0
            ),
        )

    near_pools = [(dot(pool, kv_near[s, first]), dot(pool, kv_near[s, second])) for s in (0, 3)]
    for side in (0, 1):
        sigma = direction(side)
        arrived(one_in.at[side * 2, ones_only], one_recv.at[side * 2], inside(-2 * sigma))
        arrived(one_in.at[side * 2 + 1], one_recv.at[side * 2 + 1], inside(sigma))
    arrived(far_bias.at[other], sib_recv.at[4])
    nearest = [two_in[0, 1], one_in[1, 2 * ONE :], two_in[1, 1], one_in[3, 2 * ONE :]]
    nearest = [x.astype(F32) for x in nearest]
    for kind, middle in ((0, k_middle), (1, v_middle)):
        ones = slice(kind * ONE, (kind + 1) * ONE)
        rows = slice(kind * TWO, (kind + 1) * TWO)
        for s in range(4):
            middle[s * ONE : (s + 1) * ONE] = one_in[s, ones]
        middle[4 * ONE : 6 * ONE] = jnp.concatenate([p[kind][:ONE] for p in near_pools], axis=0).astype(BF16)
        parts = [x[rows] for x in nearest] + [p[kind][ONE:] for p in near_pools]
        parts += [two_in[side, 0].astype(F32)[rows] for side in (0, 1)]
        middle[6 * ONE :] = jnp.concatenate(parts, axis=0).astype(BF16)
    for h in (0, 1):
        scores = dot_nt(q_two[:, columns[h]], k_middle[:, columns[h]]) * scale + far_of(MIDDLE)
        attend(h, MIDDLE, scores, lambda e: dot(e, v_middle[:, columns[h]]))

    for side in (0, 1):
        sigma = direction(side)
        for s, steps in ((2, 3), (6, 5)):
            arrived(two_in.at[side, pl.ds(s, 2)], two_recv.at[side, s], inside(-steps * sigma))
        arrived(two_in.at[side, 8], two_recv.at[side, 8], inside(-6 * sigma))
    twos = [two_in[side, 2:].astype(F32) for side in (0, 1)]
    for kind, last in ((0, k_last), (1, v_last)):
        rows = slice(kind * TWO, (kind + 1) * TWO)
        parts = [t[:, rows].reshape(7 * TWO, HALF) for t in twos] + [jnp.zeros((2 * TWO, HALF), F32)]
        last[...] = jnp.concatenate(parts, axis=0).astype(BF16)
    for h in (0, 1):
        scores = dot_nt(q_two[:, columns[h]], k_last[:, columns[h]]) * scale + far_of(LAST)
        attend(h, LAST, scores, lambda e: dot(e, v_last[:, columns[h]]))
    inverse_totals = [1.0 / totals[h] for h in (0, 1)]
    for h in (0, 1):
        mixed[:, columns[h]] = accs[h] * inverse_totals[h]

    locals_in[7].wait()
    arrived(g_two.at[theirs], sib_recv.at[3])
    mates = 2 * heads
    place = lane * 2 + core
    value = mixed[...]
    energy = jnp.sum(value * value, axis=1, keepdims=True)
    product = jnp.sum(value * g_two[...].astype(F32), axis=1, keepdims=True)
    stats[place] = jnp.concatenate(
        [row_of(energy[:ROWS]), row_of(energy[ROWS:]), row_of(product[:ROWS]), row_of(product[ROWS:]), jnp.zeros((4, ROWS), F32)],
        axis=0,
    )
    for k in range(1, mates):
        to = (place + k) % mates
        send(stats.at[place], stats.at[place], stat_recv.at[place], {"seq": chip * 2 + to % 2, "head": to // 2})
    factors = [[], []]
    for h in (0, 1):
        for index, part in enumerate((OWN, SIDE, MIDDLE, LAST)):
            factors[h].append(jnp.exp2(highs[h][index] - highs[h][-1]) * inverse_totals[h])
            if part in (MIDDLE, LAST):
                turned[h, part, :] = weight[h, :, part].astype(BF16).T
    for k in range(1, mates):
        source = (place + k) % mates
        arrived(stats.at[source], stat_recv.at[source])
    summed = stats[0]
    for k in range(1, mates):
        summed = summed + stats[k]
    width = HEADS * HEAD_DIM
    deltas = [[], []]
    for b, rows in ((0, first), (1, second)):
        inverse = lax.rsqrt(column_of(summed[b : b + 1]) / width + NORM_EPSILON)
        agreement = column_of(summed[2 + b : 3 + b]) * inverse
        normed = mixed[rows] * inverse
        att[rows] = normed.astype(BF16)
        grad = inverse * (g_two[rows].astype(F32) - normed * (agreement / width))
        mixed_grad[rows] = grad
        both = grad.astype(BF16).astype(F32) * mixed[rows]
        for h in (0, 1):
            deltas[h].append(jnp.sum(both[:, columns[h]], axis=1, keepdims=True))
    deltas = [jnp.concatenate(deltas[h], axis=0) for h in (0, 1)]

    out_att = pltpu.make_async_copy(att.at[mine], att_hbm.at[:, half(core)], local_sem.at[8])
    out_att.start()
    send(att.at[theirs], att_hbm.at[:, half(core)], out_recv.at[0], sibling)

    unscale = 1.0 / math.sqrt(HEAD_DIM)
    query_grads = [None, None]

    def scaled(h, part):
        factor = factors[h][(OWN, SIDE, MIDDLE, LAST).index(part)]
        return (mixed_grad[:, columns[h]] * factor).astype(BF16), deltas[h] * factor

    def slopes_of(h, part, products, delta):
        return (weight[h, :, part] * (products - delta)).astype(BF16)

    def plain_backward(part, k_ref, v_ref):
        k_parts, v_parts = [], []
        for h in (0, 1):
            grad, delta = scaled(h, part)
            slopes = slopes_of(h, part, dot_nt(grad, v_ref(h)), delta)
            change = dot(slopes, k_ref(h))
            query_grads[h] = change if query_grads[h] is None else query_grads[h] + change
            k_parts.append(dot_tn(slopes, q_two[:, columns[h]]) * unscale)
            v_parts.append(dot(turned[h, part, :], grad))
        return jnp.concatenate(k_parts, axis=1), jnp.concatenate(v_parts, axis=1)

    def two_rows(pair, low):
        return jnp.concatenate([g[low : low + TWO] for g in pair], axis=0)

    last = plain_backward(LAST, lambda h: k_last[:, columns[h]], lambda h: v_last[:, columns[h]])
    for side in (0, 1):
        sigma = direction(side)
        for s in (1, 2, 5, 6, 7):
            two_out[side, s] = two_rows(last, (side * 7 + s - 1) * TWO).astype(BF16)
        send(
            two_out.at[side, pl.ds(5, 2)], pass_in.at[side, pl.ds(0, 2)],
            pass_recv.at[side, 0], at(-sigma, core), inside(-5 * sigma),
        )
        send(two_out.at[side, 7], pass_in.at[side, 4], pass_recv.at[side, 2], at(-2 * sigma, core), inside(-6 * sigma))
        send(
            two_out.at[side, pl.ds(1, 2)], pass_in.at[side, pl.ds(2, 2)],
            pass_recv.at[side, 1], at(-sigma, core), inside(-3 * sigma),
        )

    middle = plain_backward(MIDDLE, lambda h: k_middle[:, columns[h]], lambda h: v_middle[:, columns[h]])
    for s in range(4):
        for kind in (0, 1):
            pool_out[s, kind * ONE : (kind + 1) * ONE] = middle[kind][s * ONE : (s + 1) * ONE].astype(BF16)
    for b in (0, 1):
        s = 2 * b + 1
        pool_out[s, 2 * ONE :] = two_rows(middle, 6 * ONE + s * TWO).astype(BF16)
        send(pool_out.at[s], one_back.at[core, 1], back_one_recv.at[core, 1], at(direction(b), b), inside(direction(b)))
    for side in (0, 1):
        sigma = direction(side)
        send(
            pool_out.at[2 * side, ones_only], one_back.at[core, 0, ones_only],
            back_one_recv.at[core, 0], at(-2 * sigma, side), inside(-2 * sigma),
        )

    spread = spread_matrix()
    k_sides, v_sides = [[], []], [[], []]
    for h in (0, 1):
        grad, delta = scaled(h, SIDE)
        query = q_two[:, columns[h]]
        products = jnp.concatenate(
            [dot_nt(grad[first], kv_near[0, second, columns[h]]), dot_nt(grad[second], kv_near[3, second, columns[h]])], axis=0
        )
        slopes = slopes_of(h, SIDE, products, delta)
        query_grads[h] = query_grads[h] + jnp.concatenate(
            [dot(slopes[first], kv_near[0, first, columns[h]]), dot(slopes[second], kv_near[3, first, columns[h]])], axis=0
        )
        for b, rows in ((0, second), (1, first)):
            k_sides[b].append(dot_tn(slopes[rows], query[rows]) * unscale)
            v_sides[b].append(dot(turned[h, SIDE, rows], grad[rows]))
    for side in (0, 1):
        sigma = direction(side)
        four = -4 * sigma
        arrived(pass_in.at[side, pl.ds(0, 2)], pass_recv.at[side, 0], inside(sigma, four))
        arrived(pass_in.at[side, 4], pass_recv.at[side, 2], inside(2 * sigma, four))
        passed = [pass_in[side, s].astype(F32) for s in (0, 1, 4)]
        two_out[side, 3] = (two_rows(last, (side * 7 + 2) * TWO) + passed[0]).astype(BF16)
        two_out[side, 4] = (two_rows(last, (side * 7 + 3) * TWO) + passed[1] + passed[2]).astype(BF16)
        send(two_out.at[side, pl.ds(3, 2)], four_in.at[side], pass_recv.at[side, 3], at(-2 * sigma, core), inside(four))

    for b in (0, 1):
        p = 5 - b
        for kind, sides in ((0, k_sides), (1, v_sides)):
            pools = middle[kind]
            small = jnp.concatenate(
                [pools[p * ONE : (p + 1) * ONE], pools[6 * ONE + p * TWO : 6 * ONE + (p + 1) * TWO]], axis=0
            )
            near_out[b, kind * ROWS : (kind + 1) * ROWS] = (
                jnp.concatenate(sides[b], axis=1) + dot(spread, small.astype(BF16))
            ).astype(BF16)
        send(near_out.at[b], near_back.at[core], back_near_recv.at[core], at(-direction(b), b), inside(-direction(b)))

    own = plain_backward(OWN, lambda h: own_of(0, h), lambda h: own_of(1, h))
    for side in (0, 1):
        sigma = direction(side)
        two = -2 * sigma
        arrived(pass_in.at[side, pl.ds(2, 2)], pass_recv.at[side, 1], inside(sigma, two))
        arrived(four_in.at[side], pass_recv.at[side, 3], inside(2 * sigma, two))
        passed = pass_in[side, 2:4].astype(F32) + four_in[side].astype(F32)
        two_out[side, 0] = (two_rows(middle, 6 * ONE + (6 + side) * TWO) + passed[0]).astype(BF16)
        two_out[side, 8] = (two_rows(middle, 6 * ONE + 2 * side * TWO) + passed[1]).astype(BF16)
        send(two_out.at[side, 0], two_back.at[core, 0], back_two_recv.at[core, 0], at(two, 1 - side), inside(two))
        send(two_out.at[side, 8], two_back.at[core, 1], back_two_recv.at[core, 1], at(two, side), inside(two))

    for kind in (0, 1):
        sib_out[kind * ROWS : (kind + 1) * ROWS] = jnp.where(core == 0, own[kind][second], own[kind][first]).astype(BF16)
    send(sib_out, sib_back, out_recv.at[1], sibling)
    for h in (0, 1):
        dq[:, columns[h]] = (query_grads[h] * unscale).astype(BF16)
    out_dq = pltpu.make_async_copy(dq.at[mine], dq_hbm.at[:, half(core)], local_sem.at[9])
    out_dq.start()
    send(dq.at[theirs], dq_hbm.at[:, half(core)], out_recv.at[2], sibling)

    arrived(sib_back, out_recv.at[1])
    mine_grads = [jnp.where(core == 0, own[kind][first], own[kind][second]) for kind in (0, 1)]
    bases = {}
    for h in (0, 1):
        arrived(one_back.at[h, 0, ones_only], back_one_recv.at[h, 0], inside(sided=(2,)))
        arrived(one_back.at[h, 1], back_one_recv.at[h, 1], inside(sided=(-1,)))
        for j, steps in enumerate((-2, 2)):
            arrived(two_back.at[h, j], back_two_recv.at[h, j], inside(sided=(steps,)))
        ones = one_back[h, 1].astype(F32)
        twos = ones[2 * ONE :] + two_back[h, 0].astype(F32) + two_back[h, 1].astype(F32)
        ones = ones[: 2 * ONE] + one_back[h, 0, : 2 * ONE].astype(F32)
        for kind in (0, 1):
            rows = slice(kind * ROWS, (kind + 1) * ROWS)
            small = jnp.concatenate([ones[kind * ONE : (kind + 1) * ONE], twos[kind * TWO : (kind + 1) * TWO]], axis=0)
            grads = jnp.where(core == h, mine_grads[kind], sib_back[rows].astype(F32))
            bases[h, kind] = grads + dot(spread, small.astype(BF16))
    arrived(att_hbm.at[:, half(other)], out_recv.at[0])
    arrived(dq_hbm.at[:, half(other)], out_recv.at[2])
    flush()
    for h in (0, 1):
        arrived(near_back.at[h], back_near_recv.at[h], inside(sided=(1,)))
    outs = [out_att, out_dq]
    for kind, out, out_hbm in ((0, dk, dk_hbm), (1, dv, dv_hbm)):
        rows = slice(kind * ROWS, (kind + 1) * ROWS)
        for h in (0, 1):
            out[:, h * HALF : (h + 1) * HALF] = (bases[h, kind] + near_back[h, rows].astype(F32)).astype(BF16)
        outs.append(pltpu.make_async_copy(out, out_hbm, local_sem.at[10 + kind]))
        outs[-1].start()
    for copy in outs:
        copy.wait()


def write_out(*refs):
    *arrays, sems = refs
    copies = [pltpu.make_async_copy(arrays[i], arrays[4 + i], sems.at[i]) for i in range(4)]
    for copy in copies:
        copy.start()
    for copy in copies:
        copy.wait()


def body(queries, keys, values, out_grad, level_choice, frame_lengths):
    rows, width = queries.shape
    vmem = pltpu.VMEM
    dma = pltpu.SemaphoreType.DMA
    out = jax.ShapeDtypeStruct((rows, width), BF16)
    limit = 40 * 1024 * 1024
    arrays = (queries, keys, values, out_grad, level_choice, frame_lengths.reshape(1, -1))
    results = pl.pallas_call(
        kernel,
        out_shape=(out, out, out, out),
        in_specs=[pl.BlockSpec(memory_space=pl.ANY)] * 6,
        out_specs=(pl.BlockSpec(memory_space=pl.ANY),) * 4,
        scratch_shapes=[
            vmem((2 * ROWS, width), BF16),
            vmem((2 * ROWS, HALF), BF16),
            vmem((2 * ROWS, HALF), BF16),
            vmem((4, 2 * ROWS, HALF), BF16),
            vmem((POOLED, width), BF16),
            vmem((4, POOLED, HALF), BF16),
            vmem((2, 9, 2 * TWO, HALF), BF16),
            vmem((256, HALF), BF16),
            vmem((256, HALF), BF16),
            vmem((128, HALF), BF16),
            vmem((128, HALF), BF16),
            pltpu.SMEM((1, 4), jnp.int32),
            vmem((1, 64), jnp.int32),
            vmem((2 * ROWS, 384), F32),
            vmem((2, 8, FAR), F32),
            vmem((2, 2 * ROWS, 768), F32),
            vmem((2, 768, 2 * ROWS), BF16),
            vmem((2 * ROWS, HALF), F32),
            vmem((8, 8, ROWS), F32),
            vmem((2 * ROWS, HALF), F32),
            vmem((2 * ROWS, HALF), BF16),
            vmem((2 * ROWS, HALF), BF16),
            vmem((2, 2 * ROWS, HALF), BF16),
            vmem((4, POOLED, HALF), BF16),
            vmem((2, 9, 2 * TWO, HALF), BF16),
            vmem((2 * ROWS, HALF), BF16),
            vmem((2, 5, 2 * TWO, HALF), BF16),
            vmem((2, 2, 2 * TWO, HALF), BF16),
            vmem((2, 2 * ROWS, HALF), BF16),
            vmem((2, 2, POOLED, HALF), BF16),
            vmem((2, 2, 2 * TWO, HALF), BF16),
            vmem((2 * ROWS, HALF), BF16),
            vmem((ROWS, width), BF16),
            vmem((ROWS, width), BF16),
            dma((12,)),
            dma((64,)),
            dma((5,)),
            dma((2,)),
            dma((4,)),
            dma((2, 9)),
            dma((8,)),
            dma((2, 4)),
            dma((2,)),
            dma((2, 2)),
            dma((2, 2)),
            dma((3,)),
        ],
        compiler_params=pltpu.CompilerParams(collective_id=0, has_side_effects=True, vmem_limit_bytes=limit),
        cost_estimate=pl.CostEstimate(flops=700_000_000, bytes_accessed=1_100_000, transcendentals=400_000),
    )(*[pltpu.with_memory_space_constraint(array, pltpu.HBM) for array in arrays])
    return pl.pallas_call(
        write_out,
        out_shape=(out, out, out, out),
        in_specs=[pl.BlockSpec(memory_space=pl.ANY)] * 4,
        out_specs=(pl.BlockSpec(memory_space=pl.ANY),) * 4,
        scratch_shapes=[dma((4,))],
        compiler_params=pltpu.CompilerParams(vmem_limit_bytes=limit),
        cost_estimate=pl.CostEstimate(flops=0, bytes_accessed=1_100_000, transcendentals=0),
    )(*results)


def solution(mesh):
    in_specs = (
        P("seq", "head"),
        P("seq", "head"),
        P("seq", "head"),
        P("seq", "head"),
        P("seq", None),
        P(),
    )
    out_specs = (P("seq", "head"), P("seq", "head"), P("seq", "head"), P("seq", "head"))
    return jax.shard_map(body, mesh=mesh, in_specs=in_specs, out_specs=out_specs, check_vma=False)
```

```python
import math

import jax
import jax.numpy as jnp
from jax import lax
from jax.experimental import pallas as pl
from jax.experimental.pallas import tpu as pltpu
from jax.sharding import PartitionSpec as P

HEADS = 16
HEAD_DIM = 128
POOL1 = 4
POOL2 = 16
REACH1 = 3
REACH2 = 11
MATCHED_FRAME_ADD = 1.0
NORM_EPSILON = 1e-06

MESH = pl.DeviceIdType.MESH
F32 = jnp.float32
BF16 = jnp.bfloat16
LOG2E = math.log2(math.e)
MASKED = -1e30

ROWS = 128
HALF = 256
ONE = ROWS // POOL1
TWO = ROWS // POOL2
POOLED = 2 * (ONE + TWO)
NEAR = 3 * ROWS
FAR = 384

STEPS_ONE = (2, -1)


def direction(b):
    return 2 * b - 1


REL_ONE = [-2 * steps * direction(b) + b for b in (0, 1) for steps in STEPS_ONE] + [-1, 2]


def relative_two(side):
    sigma = direction(side)
    spots = [(2, 1 - side), (3, 1 - side), (3, side), (4, 1 - side), (4, side), (5, 1 - side), (5, side), (6, side)]
    return [-2 * k * sigma + b for k, b in spots]


REL_TWO = [relative_two(0), relative_two(1)]
REL_MIDDLE = REL_ONE + [REL_TWO[0][0], REL_TWO[1][0]]
REL_LAST = REL_TWO[0][1:] + REL_TWO[1][1:]
OWN, SIDE, MIDDLE, LAST = slice(0, 256), slice(256, 384), slice(384, 640), slice(640, 768)


def dot_nt(a, b):
    return lax.dot_general(a, b, (((1,), (1,)), ((), ())), preferred_element_type=F32)


def dot_tn(a, b):
    return lax.dot_general(a, b, (((0,), (0,)), ((), ())), preferred_element_type=F32)


def dot(a, b):
    return jnp.dot(a, b, preferred_element_type=F32)


def pool_matrix():
    r = lax.broadcasted_iota(jnp.int32, (ONE + TWO, ROWS), 0)
    t = lax.broadcasted_iota(jnp.int32, (ONE + TWO, ROWS), 1)
    one = jnp.where((t >> 2) == r, 1.0 / POOL1, 0.0)
    two = jnp.where((t >> 4) == r - ONE, 1.0 / POOL2, 0.0)
    return jnp.where(r < ONE, one, two).astype(BF16)


def spread_matrix():
    t = lax.broadcasted_iota(jnp.int32, (ROWS, ONE + TWO), 0)
    r = lax.broadcasted_iota(jnp.int32, (ROWS, ONE + TWO), 1)
    one = jnp.where((t >> 2) == r, 1.0 / POOL1, 0.0)
    two = jnp.where((t >> 4) == r - ONE, 1.0 / POOL2, 0.0)
    return jnp.where(r < ONE, one, two).astype(BF16)


def column_of(row):
    i = lax.broadcasted_iota(jnp.int32, (ROWS, ROWS), 0)
    j = lax.broadcasted_iota(jnp.int32, (ROWS, ROWS), 1)
    return jnp.sum(jnp.where(i == j, row, 0.0), axis=1, keepdims=True)


def row_of(column):
    i = lax.broadcasted_iota(jnp.int32, (ROWS, ROWS), 0)
    j = lax.broadcasted_iota(jnp.int32, (ROWS, ROWS), 1)
    return jnp.sum(jnp.where(i == j, column, 0.0), axis=0, keepdims=True)


def kernel(
    q_hbm, k_hbm, v_hbm, g_hbm, level_hbm, frame_hbm,
    att_hbm, dq_hbm, dk_hbm, dv_hbm,
    kv_own, q_two, g_two, kv_near, pooled, one_in, two_in, k_middle, v_middle, k_last, v_last,
    level_s, frame_v, near_bias, far_bias, weight, turned, mixed, stats,
    mixed_grad, att, dq, near_out, pool_out, two_out, sib_out,
    pass_in, four_in, near_back, one_back, two_back, sib_back, dk, dv,
    local_sem, send_sem, sib_recv, near_recv, one_recv, two_recv, stat_recv, pass_recv,
    back_near_recv, back_one_recv, back_two_recv, out_recv,
):
    blocks = lax.axis_size("seq")
    chips = blocks // 2
    heads = lax.axis_size("head")
    me = lax.axis_index("seq")
    lane = lax.axis_index("head")
    chip = me // 2
    core = me % 2
    other = 1 - core
    d = direction(core)

    def at(steps, c):
        return {"seq": ((chip + steps + chips) % chips) * 2 + c}

    sibling = {"seq": chip * 2 + other}

    def half(h):
        return pl.ds(pl.multiple_of(h * HALF, HALF), HALF)

    def remote(src, dst, send, recv, device):
        return pltpu.make_async_remote_copy(
            src_ref=src, dst_ref=dst, send_sem=send, recv_sem=recv, device_id=device, device_id_type=MESH
        )

    def inside(*steps, sided=()):
        away = [s for s in steps] + [s * d for s in sided]
        known = True
        for s in away:
            known = known & (chip + s >= 0) & (chip + s < chips)
        return (steps, sided), known

    def only(when, act):
        if when is None:
            act()
        else:
            pl.when(when[1])(act)

    sent = 0
    started = []

    def send(src, dst, recv, device, when=None):
        nonlocal sent
        copy = remote(src, dst, send_sem.at[sent], recv, device)
        sent += 1
        only(when, copy.start)
        started.append((copy, when))

    def flush(keep=0):
        groups = {}
        done = len(started) - keep
        for copy, when in started[:done]:
            groups.setdefault(when and when[0], (when, []))[1].append(copy)
        del started[:done]
        for when, copies in groups.values():

            def wait_all(copies=copies):
                for copy in copies:
                    copy.wait_send()

            only(when, wait_all)

    def arrived(ref, sem, when=None):
        only(when, remote(ref, ref, sem, sem, sibling).wait_recv)

    @pl.when((chip < 6) | (chip >= chips - 6))
    def _():
        for ref in (one_in, two_in, pass_in, four_in, near_back, one_back, two_back):
            ref[...] = jnp.zeros(ref.shape, ref.dtype)
        for s in (0, 3):
            kv_near[s] = jnp.zeros(kv_near.shape[1:], BF16)

    mine = pl.ds(pl.multiple_of(core * ROWS, ROWS), ROWS)
    theirs = pl.ds(pl.multiple_of(other * ROWS, ROWS), ROWS)
    k_rows, v_rows = pl.ds(0, ROWS), pl.ds(ROWS, ROWS)
    locals_in = [
        pltpu.make_async_copy(k_hbm, kv_own.at[k_rows], local_sem.at[0]),
        pltpu.make_async_copy(v_hbm, kv_own.at[v_rows], local_sem.at[1]),
        pltpu.make_async_copy(level_hbm, level_s, local_sem.at[2]),
        pltpu.make_async_copy(frame_hbm, frame_v, local_sem.at[3]),
        pltpu.make_async_copy(k_hbm.at[:, half(core)], kv_near.at[1 + core, k_rows], local_sem.at[4]),
        pltpu.make_async_copy(v_hbm.at[:, half(core)], kv_near.at[1 + core, v_rows], local_sem.at[5]),
        pltpu.make_async_copy(q_hbm.at[:, half(core)], q_two.at[mine], local_sem.at[6]),
        pltpu.make_async_copy(g_hbm.at[:, half(core)], g_two.at[mine], local_sem.at[7]),
    ]
    for copy in locals_in[:2]:
        copy.start()

    barrier = pltpu.get_barrier_semaphore()
    partners = [sibling]
    for k in range(1, heads):
        for c in (0, 1):
            partners.append({"seq": chip * 2 + c, "head": (lane + k) % heads})
    expected = len(partners)

    def greet(devices):
        for device in devices:
            pl.semaphore_signal(barrier, inc=1, device_id=device, device_id_type=MESH)

    for steps in (4, -4, 2, -2, 1, -1):
        when = inside(steps)
        only(when, lambda: greet([at(steps, 0), at(steps, 1)]))
        expected = expected + jnp.where(when[1], 2, 0)
    greet(partners)
    for copy in locals_in[2:]:
        copy.start()

    locals_in[0].wait()
    locals_in[1].wait()
    pool = pool_matrix()
    k_pool = dot(pool, kv_own[:ROWS])
    v_pool = dot(pool, kv_own[ROWS:])
    pooled[0 : 2 * ONE, :] = jnp.concatenate([k_pool[:ONE], v_pool[:ONE]], axis=0).astype(BF16)
    pooled[2 * ONE :, :] = jnp.concatenate([k_pool[ONE:], v_pool[ONE:]], axis=0).astype(BF16)

    pl.semaphore_wait(barrier, expected)

    def send_two(steps, side, spot):
        for h in (0, 1):
            send(
                pooled.at[pl.ds(2 * ONE, 2 * TWO), half(h)], two_in.at[side, spot],
                two_recv.at[side, spot], at(steps * d, h), inside(sided=(steps,)),
            )

    send_two(4, core, 5)
    send_two(-4, other, 4)
    send_two(2, core, 1)
    send_two(-2, other, 0)
    send(kv_own.at[:, half(other)], kv_near.at[1 + core], sib_recv.at[0], sibling)
    send(q_hbm.at[:, half(other)], q_two.at[mine], sib_recv.at[2], sibling)
    for h in (0, 1):
        send(kv_own.at[:, half(h)], kv_near.at[3 - 3 * core], near_recv.at[core], at(d, h), inside(sided=(1,)))
    for h in (0, 1):
        send(
            pooled.at[:, half(h)], one_in.at[core * 2 + 1],
            one_recv.at[core * 2 + 1], at(-d, h), inside(sided=(-1,)),
        )
    ones_only = pl.ds(0, 2 * ONE)
    for h in (0, 1):
        send(
            pooled.at[ones_only, half(h)], one_in.at[core * 2, ones_only],
            one_recv.at[core * 2], at(2 * d, h), inside(sided=(2,)),
        )

    locals_in[2].wait()
    locals_in[3].wait()
    table = [level_s[0, i] for i in range(4)]
    spot = lax.broadcasted_iota(jnp.int32, (8, FAR), 1)
    row = jnp.full((8, FAR), MASKED, F32)

    def level_at(offset):
        choice = jnp.where(offset == -3, table[0], table[1])
        choice = jnp.where(offset == 2, table[2], choice)
        return jnp.where(offset == 3, table[3], choice)

    def slot_bias(rel, wanted, most, bias):
        offset = rel - core
        distance = jnp.abs(offset)
        block = 2 * chip + rel
        inside = (distance >= 2) & (distance <= most) & (block >= 0) & (block < blocks)
        chosen = (distance > REACH1) | (level_at(offset) == wanted)
        return jnp.where(inside & chosen, bias * LOG2E, MASKED)

    for s, rel in enumerate(REL_ONE):
        value = slot_bias(rel, 1, REACH1, math.log(POOL1))
        row = jnp.where((spot >= s * ONE) & (spot < (s + 1) * ONE), value, row)
    for s, rel in enumerate(REL_MIDDLE + REL_LAST):
        low = len(REL_ONE) * ONE + s * TWO
        value = slot_bias(rel, 2, REACH2, math.log(POOL2))
        row = jnp.where((spot >= low) & (spot < low + TWO), value, row)
    far_bias[core] = row
    send(far_bias.at[core], far_bias.at[core], sib_recv.at[4], sibling)

    lengths = frame_v[...].astype(F32)
    count = lengths.shape[1]
    i = lax.broadcasted_iota(jnp.int32, (count, count), 0)
    j = lax.broadcasted_iota(jnp.int32, (count, count), 1)
    ends_column = jnp.sum(jnp.where(j <= i, lengths, 0.0), axis=1, keepdims=True)
    ends_row = jnp.sum(jnp.where(i == j, ends_column, 0.0), axis=0, keepdims=True)
    start = (2 * chip - 1) * ROWS
    key_place = start + lax.broadcasted_iota(jnp.int32, (1, 4 * ROWS), 1)
    key_frame = jnp.sum(jnp.where(key_place.astype(F32) >= ends_column, 1.0, 0.0), axis=0, keepdims=True)
    key_inside = (key_place >= 0) & (key_place < blocks * ROWS)
    for b in (0, 1):
        place = start + (b + 1) * ROWS + lax.broadcasted_iota(jnp.int32, (ROWS, 1), 0)
        frame = jnp.sum(jnp.where(place.astype(F32) >= ends_row, 1.0, 0.0), axis=1, keepdims=True)
        matched = jnp.where(frame == key_frame, MATCHED_FRAME_ADD * LOG2E, 0.0)
        matched = jnp.where(key_inside, matched, MASKED)
        rows = slice(b * ROWS, (b + 1) * ROWS)
        near_bias[rows, OWN] = matched[:, ROWS : 3 * ROWS]
        near_bias[rows, SIDE] = matched[:, 3 * b * ROWS : (3 * b + 1) * ROWS]

    scale = LOG2E / math.sqrt(HEAD_DIM)
    columns = [slice(h * HEAD_DIM, (h + 1) * HEAD_DIM) for h in (0, 1)]
    first, second = slice(0, ROWS), slice(ROWS, 2 * ROWS)
    highs, totals, accs = [[], []], [None, None], [None, None]

    def far_of(part):
        low, high = part.start - MIDDLE.start, part.stop - MIDDLE.start
        shape = (ROWS, high - low)
        return jnp.concatenate([jnp.broadcast_to(far_bias[b, 0:1, low:high], shape) for b in (0, 1)], axis=0)

    def attend(h, part, scores, product):
        top = jnp.max(scores, axis=1, keepdims=True)
        if highs[h]:
            top = jnp.maximum(highs[h][-1], top)
        e = jnp.exp2(scores - top)
        weight[h, :, part] = e
        total = jnp.sum(e, axis=1, keepdims=True)
        rounded = e.astype(BF16)
        acc = product(rounded)
        if part in (OWN, SIDE):
            turned[h, part, :] = rounded.T
        if highs[h]:
            alpha = jnp.exp2(highs[h][-1] - top)
            total = totals[h] * alpha + total
            acc = accs[h] * alpha + acc
        highs[h].append(top)
        totals[h], accs[h] = total, acc

    rows_of = (first, second)

    def own_of(kind, h):
        return kv_near[1:3, rows_of[kind], columns[h]].reshape(2 * ROWS, HEAD_DIM)

    for side in (0, 1):
        sigma = direction(side)
        four, two = -4 * sigma, -2 * sigma
        for s in (4, 5):
            arrived(two_in.at[side, s], two_recv.at[side, s], inside(four))
        send(two_in.at[side, 5], two_in.at[side, 8], two_recv.at[side, 8], at(2 * sigma, core), inside(four, 2 * sigma))
        send(
            two_in.at[side, pl.ds(4, 2)], two_in.at[side, pl.ds(6, 2)],
            two_recv.at[side, 6], at(sigma, core), inside(four, sigma),
        )
        for s in (0, 1):
            arrived(two_in.at[side, s], two_recv.at[side, s], inside(two))
        send(
            two_in.at[side, pl.ds(0, 2)], two_in.at[side, pl.ds(2, 2)],
            two_recv.at[side, 2], at(sigma, core), inside(two, sigma),
        )

    send(g_hbm.at[:, half(other)], g_two.at[mine], sib_recv.at[3], sibling)

    locals_in[4].wait()
    locals_in[6].wait()
    locals_in[5].wait()
    arrived(kv_near.at[1 + other], sib_recv.at[0])
    arrived(q_two.at[theirs], sib_recv.at[2])
    for h in (0, 1):
        scores = dot_nt(q_two[:, columns[h]], own_of(0, h)) * scale + near_bias[:, OWN]
        attend(h, OWN, scores, lambda e: dot(e, own_of(1, h)))

    arrived(kv_near.at[3], near_recv.at[0], inside(1))
    arrived(kv_near.at[0], near_recv.at[1], inside(-1))
    for h in (0, 1):
        query = q_two[:, columns[h]]
        scores = jnp.concatenate(
            [dot_nt(query[first], kv_near[0, first, columns[h]]), dot_nt(query[second], kv_near[3, first, columns[h]])], axis=0
        )
        attend(
            h, SIDE, scores * scale + near_bias[:, SIDE],
            lambda e: jnp.concatenate(
                [dot(e[first], kv_near[0, second, columns[h]]), dot(e[second], kv_near[3, second, columns[h]])], axis=0
            ),
        )

    near_pools = [(dot(pool, kv_near[s, first]), dot(pool, kv_near[s, second])) for s in (0, 3)]
    for side in (0, 1):
        sigma = direction(side)
        arrived(one_in.at[side * 2, ones_only], one_recv.at[side * 2], inside(-2 * sigma))
        arrived(one_in.at[side * 2 + 1], one_recv.at[side * 2 + 1], inside(sigma))
    arrived(far_bias.at[other], sib_recv.at[4])
    nearest = [two_in[0, 1], one_in[1, 2 * ONE :], two_in[1, 1], one_in[3, 2 * ONE :]]
    nearest = [x.astype(F32) for x in nearest]
    for kind, middle in ((0, k_middle), (1, v_middle)):
        ones = slice(kind * ONE, (kind + 1) * ONE)
        rows = slice(kind * TWO, (kind + 1) * TWO)
        for s in range(4):
            middle[s * ONE : (s + 1) * ONE] = one_in[s, ones]
        middle[4 * ONE : 6 * ONE] = jnp.concatenate([p[kind][:ONE] for p in near_pools], axis=0).astype(BF16)
        parts = [x[rows] for x in nearest] + [p[kind][ONE:] for p in near_pools]
        parts += [two_in[side, 0].astype(F32)[rows] for side in (0, 1)]
        middle[6 * ONE :] = jnp.concatenate(parts, axis=0).astype(BF16)
    for h in (0, 1):
        scores = dot_nt(q_two[:, columns[h]], k_middle[:, columns[h]]) * scale + far_of(MIDDLE)
        attend(h, MIDDLE, scores, lambda e: dot(e, v_middle[:, columns[h]]))

    for side in (0, 1):
        sigma = direction(side)
        for s, steps in ((2, 3), (6, 5)):
            arrived(two_in.at[side, pl.ds(s, 2)], two_recv.at[side, s], inside(-steps * sigma))
        arrived(two_in.at[side, 8], two_recv.at[side, 8], inside(-6 * sigma))
    twos = [two_in[side, 2:].astype(F32) for side in (0, 1)]
    for kind, last in ((0, k_last), (1, v_last)):
        rows = slice(kind * TWO, (kind + 1) * TWO)
        parts = [t[:, rows].reshape(7 * TWO, HALF) for t in twos] + [jnp.zeros((2 * TWO, HALF), F32)]
        last[...] = jnp.concatenate(parts, axis=0).astype(BF16)
    for h in (0, 1):
        scores = dot_nt(q_two[:, columns[h]], k_last[:, columns[h]]) * scale + far_of(LAST)
        attend(h, LAST, scores, lambda e: dot(e, v_last[:, columns[h]]))
    inverse_totals = [1.0 / totals[h] for h in (0, 1)]
    for h in (0, 1):
        mixed[:, columns[h]] = accs[h] * inverse_totals[h]

    locals_in[7].wait()
    arrived(g_two.at[theirs], sib_recv.at[3])
    mates = 2 * heads
    place = lane * 2 + core
    value = mixed[...]
    energy = jnp.sum(value * value, axis=1, keepdims=True)
    product = jnp.sum(value * g_two[...].astype(F32), axis=1, keepdims=True)
    stats[place] = jnp.concatenate(
        [row_of(energy[:ROWS]), row_of(energy[ROWS:]), row_of(product[:ROWS]), row_of(product[ROWS:]), jnp.zeros((4, ROWS), F32)],
        axis=0,
    )
    for k in range(1, mates):
        to = (place + k) % mates
        send(stats.at[place], stats.at[place], stat_recv.at[place], {"seq": chip * 2 + to % 2, "head": to // 2})
    factors = [[], []]
    for h in (0, 1):
        for index, part in enumerate((OWN, SIDE, MIDDLE, LAST)):
            factors[h].append(jnp.exp2(highs[h][index] - highs[h][-1]) * inverse_totals[h])
            if part in (MIDDLE, LAST):
                turned[h, part, :] = weight[h, :, part].astype(BF16).T
    flush(keep=mates - 1)
    for k in range(1, mates):
        source = (place + k) % mates
        arrived(stats.at[source], stat_recv.at[source])
    summed = stats[0]
    for k in range(1, mates):
        summed = summed + stats[k]
    width = HEADS * HEAD_DIM
    deltas = [[], []]
    for b, rows in ((0, first), (1, second)):
        inverse = lax.rsqrt(column_of(summed[b : b + 1]) / width + NORM_EPSILON)
        agreement = column_of(summed[2 + b : 3 + b]) * inverse
        normed = mixed[rows] * inverse
        att[rows] = normed.astype(BF16)
        grad = inverse * (g_two[rows].astype(F32) - normed * (agreement / width))
        mixed_grad[rows] = grad
        both = grad.astype(BF16).astype(F32) * mixed[rows]
        for h in (0, 1):
            deltas[h].append(jnp.sum(both[:, columns[h]], axis=1, keepdims=True))
    deltas = [jnp.concatenate(deltas[h], axis=0) for h in (0, 1)]

    out_att = pltpu.make_async_copy(att.at[mine], att_hbm.at[:, half(core)], local_sem.at[8])
    out_att.start()
    send(att.at[theirs], att_hbm.at[:, half(core)], out_recv.at[0], sibling)

    unscale = 1.0 / math.sqrt(HEAD_DIM)
    query_grads = [None, None]

    def scaled(h, part):
        factor = factors[h][(OWN, SIDE, MIDDLE, LAST).index(part)]
        return (mixed_grad[:, columns[h]] * factor).astype(BF16), deltas[h] * factor

    def slopes_of(h, part, products, delta):
        return (weight[h, :, part] * (products - delta)).astype(BF16)

    def plain_backward(part, k_ref, v_ref):
        k_parts, v_parts = [], []
        for h in (0, 1):
            grad, delta = scaled(h, part)
            slopes = slopes_of(h, part, dot_nt(grad, v_ref(h)), delta)
            change = dot(slopes, k_ref(h))
            query_grads[h] = change if query_grads[h] is None else query_grads[h] + change
            k_parts.append(dot_tn(slopes, q_two[:, columns[h]]) * unscale)
            v_parts.append(dot(turned[h, part, :], grad))
        return jnp.concatenate(k_parts, axis=1), jnp.concatenate(v_parts, axis=1)

    def two_rows(pair, low):
        return jnp.concatenate([g[low : low + TWO] for g in pair], axis=0)

    last = plain_backward(LAST, lambda h: k_last[:, columns[h]], lambda h: v_last[:, columns[h]])
    for side in (0, 1):
        sigma = direction(side)
        for s in (1, 2, 5, 6, 7):
            two_out[side, s] = two_rows(last, (side * 7 + s - 1) * TWO).astype(BF16)
        send(
            two_out.at[side, pl.ds(5, 2)], pass_in.at[side, pl.ds(0, 2)],
            pass_recv.at[side, 0], at(-sigma, core), inside(-5 * sigma),
        )
        send(two_out.at[side, 7], pass_in.at[side, 4], pass_recv.at[side, 2], at(-2 * sigma, core), inside(-6 * sigma))
        send(
            two_out.at[side, pl.ds(1, 2)], pass_in.at[side, pl.ds(2, 2)],
            pass_recv.at[side, 1], at(-sigma, core), inside(-3 * sigma),
        )

    middle = plain_backward(MIDDLE, lambda h: k_middle[:, columns[h]], lambda h: v_middle[:, columns[h]])
    for s in range(4):
        for kind in (0, 1):
            pool_out[s, kind * ONE : (kind + 1) * ONE] = middle[kind][s * ONE : (s + 1) * ONE].astype(BF16)
    for b in (0, 1):
        s = 2 * b + 1
        pool_out[s, 2 * ONE :] = two_rows(middle, 6 * ONE + s * TWO).astype(BF16)
        send(pool_out.at[s], one_back.at[core, 1], back_one_recv.at[core, 1], at(direction(b), b), inside(direction(b)))
    for side in (0, 1):
        sigma = direction(side)
        send(
            pool_out.at[2 * side, ones_only], one_back.at[core, 0, ones_only],
            back_one_recv.at[core, 0], at(-2 * sigma, side), inside(-2 * sigma),
        )

    spread = spread_matrix()
    k_sides, v_sides = [[], []], [[], []]
    for h in (0, 1):
        grad, delta = scaled(h, SIDE)
        query = q_two[:, columns[h]]
        products = jnp.concatenate(
            [dot_nt(grad[first], kv_near[0, second, columns[h]]), dot_nt(grad[second], kv_near[3, second, columns[h]])], axis=0
        )
        slopes = slopes_of(h, SIDE, products, delta)
        query_grads[h] = query_grads[h] + jnp.concatenate(
            [dot(slopes[first], kv_near[0, first, columns[h]]), dot(slopes[second], kv_near[3, first, columns[h]])], axis=0
        )
        for b, rows in ((0, second), (1, first)):
            k_sides[b].append(dot_tn(slopes[rows], query[rows]) * unscale)
            v_sides[b].append(dot(turned[h, SIDE, rows], grad[rows]))
    for side in (0, 1):
        sigma = direction(side)
        four = -4 * sigma
        arrived(pass_in.at[side, pl.ds(0, 2)], pass_recv.at[side, 0], inside(sigma, four))
        arrived(pass_in.at[side, 4], pass_recv.at[side, 2], inside(2 * sigma, four))
        passed = [pass_in[side, s].astype(F32) for s in (0, 1, 4)]
        two_out[side, 3] = (two_rows(last, (side * 7 + 2) * TWO) + passed[0]).astype(BF16)
        two_out[side, 4] = (two_rows(last, (side * 7 + 3) * TWO) + passed[1] + passed[2]).astype(BF16)
        send(two_out.at[side, pl.ds(3, 2)], four_in.at[side], pass_recv.at[side, 3], at(-2 * sigma, core), inside(four))

    for b in (0, 1):
        p = 5 - b
        for kind, sides in ((0, k_sides), (1, v_sides)):
            pools = middle[kind]
            small = jnp.concatenate(
                [pools[p * ONE : (p + 1) * ONE], pools[6 * ONE + p * TWO : 6 * ONE + (p + 1) * TWO]], axis=0
            )
            near_out[b, kind * ROWS : (kind + 1) * ROWS] = (
                jnp.concatenate(sides[b], axis=1) + dot(spread, small.astype(BF16))
            ).astype(BF16)
        send(near_out.at[b], near_back.at[core], back_near_recv.at[core], at(-direction(b), b), inside(-direction(b)))

    own = plain_backward(OWN, lambda h: own_of(0, h), lambda h: own_of(1, h))
    flush(keep=2)
    for side in (0, 1):
        sigma = direction(side)
        two = -2 * sigma
        arrived(pass_in.at[side, pl.ds(2, 2)], pass_recv.at[side, 1], inside(sigma, two))
        arrived(four_in.at[side], pass_recv.at[side, 3], inside(2 * sigma, two))
        passed = pass_in[side, 2:4].astype(F32) + four_in[side].astype(F32)
        two_out[side, 0] = (two_rows(middle, 6 * ONE + (6 + side) * TWO) + passed[0]).astype(BF16)
        two_out[side, 8] = (two_rows(middle, 6 * ONE + 2 * side * TWO) + passed[1]).astype(BF16)
        send(two_out.at[side, 0], two_back.at[core, 0], back_two_recv.at[core, 0], at(two, 1 - side), inside(two))
        send(two_out.at[side, 8], two_back.at[core, 1], back_two_recv.at[core, 1], at(two, side), inside(two))

    for kind in (0, 1):
        sib_out[kind * ROWS : (kind + 1) * ROWS] = jnp.where(core == 0, own[kind][second], own[kind][first]).astype(BF16)
    send(sib_out, sib_back, out_recv.at[1], sibling)
    for h in (0, 1):
        dq[:, columns[h]] = (query_grads[h] * unscale).astype(BF16)
    out_dq = pltpu.make_async_copy(dq.at[mine], dq_hbm.at[:, half(core)], local_sem.at[9])
    out_dq.start()
    send(dq.at[theirs], dq_hbm.at[:, half(core)], out_recv.at[2], sibling)

    outs = [out_att, out_dq]

    def finish(h, sem, rest):
        arrived(one_back.at[h, 0, ones_only], back_one_recv.at[h, 0], inside(sided=(2,)))
        arrived(one_back.at[h, 1], back_one_recv.at[h, 1], inside(sided=(-1,)))
        arrived(near_back.at[h], back_near_recv.at[h], inside(sided=(1,)))
        for j, steps in enumerate((-2, 2)):
            arrived(two_back.at[h, j], back_two_recv.at[h, j], inside(sided=(steps,)))
        ones = one_back[h, 1].astype(F32)
        twos = ones[2 * ONE :] + two_back[h, 0].astype(F32) + two_back[h, 1].astype(F32)
        ones = ones[: 2 * ONE] + one_back[h, 0, : 2 * ONE].astype(F32)
        sums = []
        for kind, rows in ((0, first), (1, second)):
            small = jnp.concatenate([ones[kind * ONE : (kind + 1) * ONE], twos[kind * TWO : (kind + 1) * TWO]], axis=0)
            sums.append(near_back[h, rows].astype(F32) + dot(spread, small.astype(BF16)))
        rest = rest()
        for kind, out, out_hbm in ((0, dk, dk_hbm), (1, dv, dv_hbm)):
            out[:, half(h)] = (sums[kind] + rest[kind]).astype(BF16)
            outs.append(pltpu.make_async_copy(out.at[:, half(h)], out_hbm.at[:, half(h)], local_sem.at[sem + kind]))
            outs[-1].start()

    def from_sibling():
        arrived(sib_back, out_recv.at[1])
        return [sib_back[rows].astype(F32) for rows in (first, second)]

    finish(core, 10, lambda: [jnp.where(core == 0, own[kind][first], own[kind][second]) for kind in (0, 1)])
    finish(other, 12, from_sibling)
    arrived(att_hbm.at[:, half(other)], out_recv.at[0])
    arrived(dq_hbm.at[:, half(other)], out_recv.at[2])
    flush()
    for copy in outs:
        copy.wait()


def write_out(*refs):
    *arrays, sems = refs
    copies = [pltpu.make_async_copy(arrays[i], arrays[4 + i], sems.at[i]) for i in range(4)]
    for copy in copies:
        copy.start()
    for copy in copies:
        copy.wait()


def body(queries, keys, values, out_grad, level_choice, frame_lengths):
    rows, width = queries.shape
    vmem = pltpu.VMEM
    dma = pltpu.SemaphoreType.DMA
    out = jax.ShapeDtypeStruct((rows, width), BF16)
    limit = 40 * 1024 * 1024
    arrays = (queries, keys, values, out_grad, level_choice, frame_lengths.reshape(1, -1))
    results = pl.pallas_call(
        kernel,
        out_shape=(out, out, out, out),
        in_specs=[pl.BlockSpec(memory_space=pl.ANY)] * 6,
        out_specs=(pl.BlockSpec(memory_space=pl.ANY),) * 4,
        scratch_shapes=[
            vmem((2 * ROWS, width), BF16),
            vmem((2 * ROWS, HALF), BF16),
            vmem((2 * ROWS, HALF), BF16),
            vmem((4, 2 * ROWS, HALF), BF16),
            vmem((POOLED, width), BF16),
            vmem((4, POOLED, HALF), BF16),
            vmem((2, 9, 2 * TWO, HALF), BF16),
            vmem((256, HALF), BF16),
            vmem((256, HALF), BF16),
            vmem((128, HALF), BF16),
            vmem((128, HALF), BF16),
            pltpu.SMEM((1, 4), jnp.int32),
            vmem((1, 64), jnp.int32),
            vmem((2 * ROWS, 384), F32),
            vmem((2, 8, FAR), F32),
            vmem((2, 2 * ROWS, 768), F32),
            vmem((2, 768, 2 * ROWS), BF16),
            vmem((2 * ROWS, HALF), F32),
            vmem((8, 8, ROWS), F32),
            vmem((2 * ROWS, HALF), F32),
            vmem((2 * ROWS, HALF), BF16),
            vmem((2 * ROWS, HALF), BF16),
            vmem((2, 2 * ROWS, HALF), BF16),
            vmem((4, POOLED, HALF), BF16),
            vmem((2, 9, 2 * TWO, HALF), BF16),
            vmem((2 * ROWS, HALF), BF16),
            vmem((2, 5, 2 * TWO, HALF), BF16),
            vmem((2, 2, 2 * TWO, HALF), BF16),
            vmem((2, 2 * ROWS, HALF), BF16),
            vmem((2, 2, POOLED, HALF), BF16),
            vmem((2, 2, 2 * TWO, HALF), BF16),
            vmem((2 * ROWS, HALF), BF16),
            vmem((ROWS, width), BF16),
            vmem((ROWS, width), BF16),
            dma((14,)),
            dma((64,)),
            dma((5,)),
            dma((2,)),
            dma((4,)),
            dma((2, 9)),
            dma((8,)),
            dma((2, 4)),
            dma((2,)),
            dma((2, 2)),
            dma((2, 2)),
            dma((3,)),
        ],
        compiler_params=pltpu.CompilerParams(collective_id=0, has_side_effects=True, vmem_limit_bytes=limit),
        cost_estimate=pl.CostEstimate(flops=700_000_000, bytes_accessed=1_100_000, transcendentals=400_000),
    )(*[pltpu.with_memory_space_constraint(array, pltpu.HBM) for array in arrays])
    return pl.pallas_call(
        write_out,
        out_shape=(out, out, out, out),
        in_specs=[pl.BlockSpec(memory_space=pl.ANY)] * 4,
        out_specs=(pl.BlockSpec(memory_space=pl.ANY),) * 4,
        scratch_shapes=[dma((4,))],
        compiler_params=pltpu.CompilerParams(vmem_limit_bytes=limit),
        cost_estimate=pl.CostEstimate(flops=0, bytes_accessed=1_100_000, transcendentals=0),
    )(*results)


def solution(mesh):
    in_specs = (
        P("seq", "head"),
        P("seq", "head"),
        P("seq", "head"),
        P("seq", "head"),
        P("seq", None),
        P(),
    )
    out_specs = (P("seq", "head"), P("seq", "head"), P("seq", "head"), P("seq", "head"))
    return jax.shard_map(body, mesh=mesh, in_specs=in_specs, out_specs=out_specs, check_vma=False)
```

```python
import math

import jax
import jax.numpy as jnp
from jax import lax
from jax.experimental import pallas as pl
from jax.experimental.pallas import tpu as pltpu
from jax.sharding import PartitionSpec as P

HEADS = 16
HEAD_DIM = 128
POOL1 = 4
POOL2 = 16
REACH1 = 3
REACH2 = 11
MATCHED_FRAME_ADD = 1.0
NORM_EPSILON = 1e-06

MESH = pl.DeviceIdType.MESH
F32 = jnp.float32
BF16 = jnp.bfloat16
LOG2E = math.log2(math.e)
MASKED = -1e30

ROWS = 128
HALF = 256
ONE = ROWS // POOL1
TWO = ROWS // POOL2
POOLED = 2 * (ONE + TWO)
NEAR = 3 * ROWS
FAR = 384

STEPS_ONE = (2, -1)


def direction(b):
    return 2 * b - 1


REL_ONE = [-2 * steps * direction(b) + b for b in (0, 1) for steps in STEPS_ONE] + [-1, 2]


def relative_two(side):
    sigma = direction(side)
    spots = [(2, 1 - side), (3, 1 - side), (3, side), (4, 1 - side), (4, side), (5, 1 - side), (5, side), (6, side)]
    return [-2 * k * sigma + b for k, b in spots]


REL_TWO = [relative_two(0), relative_two(1)]
REL_MIDDLE = REL_ONE + [REL_TWO[0][0], REL_TWO[1][0]]
REL_LAST = REL_TWO[0][1:] + REL_TWO[1][1:]
OWN, SIDE, MIDDLE, LAST = slice(0, 256), slice(256, 384), slice(384, 640), slice(640, 768)


def dot_nt(a, b):
    return lax.dot_general(a, b, (((1,), (1,)), ((), ())), preferred_element_type=F32)


def dot_tn(a, b):
    return lax.dot_general(a, b, (((0,), (0,)), ((), ())), preferred_element_type=F32)


def dot(a, b):
    return jnp.dot(a, b, preferred_element_type=F32)


def pool_matrix():
    r = lax.broadcasted_iota(jnp.int32, (ONE + TWO, ROWS), 0)
    t = lax.broadcasted_iota(jnp.int32, (ONE + TWO, ROWS), 1)
    one = jnp.where((t >> 2) == r, 1.0 / POOL1, 0.0)
    two = jnp.where((t >> 4) == r - ONE, 1.0 / POOL2, 0.0)
    return jnp.where(r < ONE, one, two).astype(BF16)


def spread_matrix():
    t = lax.broadcasted_iota(jnp.int32, (ROWS, ONE + TWO), 0)
    r = lax.broadcasted_iota(jnp.int32, (ROWS, ONE + TWO), 1)
    one = jnp.where((t >> 2) == r, 1.0 / POOL1, 0.0)
    two = jnp.where((t >> 4) == r - ONE, 1.0 / POOL2, 0.0)
    return jnp.where(r < ONE, one, two).astype(BF16)


def column_of(row):
    i = lax.broadcasted_iota(jnp.int32, (ROWS, ROWS), 0)
    j = lax.broadcasted_iota(jnp.int32, (ROWS, ROWS), 1)
    return jnp.sum(jnp.where(i == j, row, 0.0), axis=1, keepdims=True)


def row_of(column):
    i = lax.broadcasted_iota(jnp.int32, (ROWS, ROWS), 0)
    j = lax.broadcasted_iota(jnp.int32, (ROWS, ROWS), 1)
    return jnp.sum(jnp.where(i == j, column, 0.0), axis=0, keepdims=True)


def kernel(
    q_hbm, k_hbm, v_hbm, g_hbm, level_hbm, frame_hbm,
    att_hbm, dq_hbm, dk_hbm, dv_hbm,
    kv_own, q_two, g_two, kv_near, pooled, one_in, two_in, k_middle, v_middle, k_last, v_last,
    level_s, frame_v, near_bias, far_bias, weight, turned, mixed, stats,
    mixed_grad, att, dq, near_out, pool_out, two_out, sib_out,
    pass_in, four_in, near_back, one_back, two_back, sib_back, dk, dv,
    local_sem, send_sem, sib_recv, near_recv, one_recv, two_recv, stat_recv, pass_recv,
    back_near_recv, back_one_recv, back_two_recv, out_recv,
):
    blocks = lax.axis_size("seq")
    chips = blocks // 2
    heads = lax.axis_size("head")
    me = lax.axis_index("seq")
    lane = lax.axis_index("head")
    chip = me // 2
    core = me % 2
    other = 1 - core
    d = direction(core)

    def at(steps, c):
        return {"seq": ((chip + steps + chips) % chips) * 2 + c}

    sibling = {"seq": chip * 2 + other}

    def half(h):
        return pl.ds(pl.multiple_of(h * HALF, HALF), HALF)

    def remote(src, dst, send, recv, device):
        return pltpu.make_async_remote_copy(
            src_ref=src, dst_ref=dst, send_sem=send, recv_sem=recv, device_id=device, device_id_type=MESH
        )

    def inside(*steps, sided=()):
        away = [s for s in steps] + [s * d for s in sided]
        known = True
        for s in away:
            known = known & (chip + s >= 0) & (chip + s < chips)
        return (steps, sided), known

    def only(when, act):
        if when is None:
            act()
        else:
            pl.when(when[1])(act)

    sent = 0
    started = []

    def send(src, dst, recv, device, when=None):
        nonlocal sent
        copy = remote(src, dst, send_sem.at[sent], recv, device)
        sent += 1
        only(when, copy.start)
        started.append((copy, when))

    def send_all(copies, when):
        nonlocal sent
        made = []
        for src, dst, recv, device in copies:
            made.append(remote(src, dst, send_sem.at[sent], recv, device))
            sent += 1

        def start_all():
            for copy in made:
                copy.start()

        only(when, start_all)
        started.extend((copy, when) for copy in made)

    def flush(keep=0):
        groups = {}
        done = len(started) - keep
        for copy, when in started[:done]:
            groups.setdefault(when and when[0], (when, []))[1].append(copy)
        del started[:done]
        for when, copies in groups.values():

            def wait_all(copies=copies):
                for copy in copies:
                    copy.wait_send()

            only(when, wait_all)

    def arrived(ref, sem, when=None):
        only(when, remote(ref, ref, sem, sem, sibling).wait_recv)

    def all_arrived(pairs, when):
        def wait_all():
            for ref, sem in pairs:
                arrived(ref, sem)

        only(when, wait_all)

    @pl.when((chip < 6) | (chip >= chips - 6))
    def _():
        for ref in (one_in, two_in, pass_in, four_in, near_back, one_back, two_back):
            ref[...] = jnp.zeros(ref.shape, ref.dtype)
        for s in (0, 3):
            kv_near[s] = jnp.zeros(kv_near.shape[1:], BF16)

    mine = pl.ds(pl.multiple_of(core * ROWS, ROWS), ROWS)
    theirs = pl.ds(pl.multiple_of(other * ROWS, ROWS), ROWS)
    k_rows, v_rows = pl.ds(0, ROWS), pl.ds(ROWS, ROWS)
    locals_in = [
        pltpu.make_async_copy(k_hbm, kv_own.at[k_rows], local_sem.at[0]),
        pltpu.make_async_copy(v_hbm, kv_own.at[v_rows], local_sem.at[1]),
        pltpu.make_async_copy(level_hbm, level_s, local_sem.at[2]),
        pltpu.make_async_copy(frame_hbm, frame_v, local_sem.at[3]),
        pltpu.make_async_copy(k_hbm.at[:, half(core)], kv_near.at[1 + core, k_rows], local_sem.at[4]),
        pltpu.make_async_copy(v_hbm.at[:, half(core)], kv_near.at[1 + core, v_rows], local_sem.at[5]),
        pltpu.make_async_copy(q_hbm.at[:, half(core)], q_two.at[mine], local_sem.at[6]),
        pltpu.make_async_copy(g_hbm.at[:, half(core)], g_two.at[mine], local_sem.at[7]),
    ]
    for copy in locals_in[:2]:
        copy.start()

    barrier = pltpu.get_barrier_semaphore()
    partners = [sibling]
    for k in range(1, heads):
        for c in (0, 1):
            partners.append({"seq": chip * 2 + c, "head": (lane + k) % heads})
    expected = len(partners)

    def greet(devices):
        for device in devices:
            pl.semaphore_signal(barrier, inc=1, device_id=device, device_id_type=MESH)

    for steps in (4, -4, 2, -2, 1, -1):
        when = inside(steps)
        only(when, lambda: greet([at(steps, 0), at(steps, 1)]))
        expected = expected + jnp.where(when[1], 2, 0)
    greet(partners)
    for copy in locals_in[2:]:
        copy.start()

    locals_in[0].wait()
    locals_in[1].wait()
    pool = pool_matrix()
    k_pool = dot(pool, kv_own[:ROWS])
    v_pool = dot(pool, kv_own[ROWS:])
    pooled[0 : 2 * ONE, :] = jnp.concatenate([k_pool[:ONE], v_pool[:ONE]], axis=0).astype(BF16)
    pooled[2 * ONE :, :] = jnp.concatenate([k_pool[ONE:], v_pool[ONE:]], axis=0).astype(BF16)

    pl.semaphore_wait(barrier, expected)

    two_rows_out = pl.ds(2 * ONE, 2 * TWO)

    def send_two(steps, side, spot):
        send_all(
            [
                (pooled.at[two_rows_out, half(h)], two_in.at[side, spot], two_recv.at[side, spot], at(steps * d, h))
                for h in (0, 1)
            ],
            inside(sided=(steps,)),
        )

    send_two(4, core, 5)
    send_two(-4, other, 4)
    send_two(2, core, 1)
    send_two(-2, other, 0)
    send(kv_own.at[:, half(other)], kv_near.at[1 + core], sib_recv.at[0], sibling)
    send(q_hbm.at[:, half(other)], q_two.at[mine], sib_recv.at[2], sibling)
    ones_only = pl.ds(0, 2 * ONE)
    send_all(
        [(kv_own.at[:, half(h)], kv_near.at[3 - 3 * core], near_recv.at[core], at(d, h)) for h in (0, 1)],
        inside(sided=(1,)),
    )
    spot_one = core * 2
    send_all(
        [(pooled.at[:, half(h)], one_in.at[spot_one + 1], one_recv.at[spot_one + 1], at(-d, h)) for h in (0, 1)],
        inside(sided=(-1,)),
    )
    send_all(
        [
            (pooled.at[ones_only, half(h)], one_in.at[spot_one, ones_only], one_recv.at[spot_one], at(2 * d, h))
            for h in (0, 1)
        ],
        inside(sided=(2,)),
    )

    locals_in[2].wait()
    locals_in[3].wait()
    table = [level_s[0, i] for i in range(4)]
    spot = lax.broadcasted_iota(jnp.int32, (8, FAR), 1)
    row = jnp.full((8, FAR), MASKED, F32)

    def level_at(offset):
        choice = jnp.where(offset == -3, table[0], table[1])
        choice = jnp.where(offset == 2, table[2], choice)
        return jnp.where(offset == 3, table[3], choice)

    def slot_bias(rel, wanted, most, bias):
        offset = rel - core
        distance = jnp.abs(offset)
        block = 2 * chip + rel
        inside = (distance >= 2) & (distance <= most) & (block >= 0) & (block < blocks)
        chosen = (distance > REACH1) | (level_at(offset) == wanted)
        return jnp.where(inside & chosen, bias * LOG2E, MASKED)

    for s, rel in enumerate(REL_ONE):
        value = slot_bias(rel, 1, REACH1, math.log(POOL1))
        row = jnp.where((spot >= s * ONE) & (spot < (s + 1) * ONE), value, row)
    for s, rel in enumerate(REL_MIDDLE + REL_LAST):
        low = len(REL_ONE) * ONE + s * TWO
        value = slot_bias(rel, 2, REACH2, math.log(POOL2))
        row = jnp.where((spot >= low) & (spot < low + TWO), value, row)
    far_bias[core] = row
    send(far_bias.at[core], far_bias.at[core], sib_recv.at[4], sibling)

    lengths = frame_v[...].astype(F32)
    count = lengths.shape[1]
    i = lax.broadcasted_iota(jnp.int32, (count, count), 0)
    j = lax.broadcasted_iota(jnp.int32, (count, count), 1)
    ends_column = jnp.sum(jnp.where(j <= i, lengths, 0.0), axis=1, keepdims=True)
    ends_row = jnp.sum(jnp.where(i == j, ends_column, 0.0), axis=0, keepdims=True)
    start = (2 * chip - 1) * ROWS
    key_place = start + lax.broadcasted_iota(jnp.int32, (1, 4 * ROWS), 1)
    key_frame = jnp.sum(jnp.where(key_place.astype(F32) >= ends_column, 1.0, 0.0), axis=0, keepdims=True)
    key_inside = (key_place >= 0) & (key_place < blocks * ROWS)
    for b in (0, 1):
        place = start + (b + 1) * ROWS + lax.broadcasted_iota(jnp.int32, (ROWS, 1), 0)
        frame = jnp.sum(jnp.where(place.astype(F32) >= ends_row, 1.0, 0.0), axis=1, keepdims=True)
        matched = jnp.where(frame == key_frame, MATCHED_FRAME_ADD * LOG2E, 0.0)
        matched = jnp.where(key_inside, matched, MASKED)
        rows = slice(b * ROWS, (b + 1) * ROWS)
        near_bias[rows, OWN] = matched[:, ROWS : 3 * ROWS]
        near_bias[rows, SIDE] = matched[:, 3 * b * ROWS : (3 * b + 1) * ROWS]

    scale = LOG2E / math.sqrt(HEAD_DIM)
    columns = [slice(h * HEAD_DIM, (h + 1) * HEAD_DIM) for h in (0, 1)]
    first, second = slice(0, ROWS), slice(ROWS, 2 * ROWS)
    highs, totals, accs = [[], []], [None, None], [None, None]

    def far_of(part):
        low, high = part.start - MIDDLE.start, part.stop - MIDDLE.start
        shape = (ROWS, high - low)
        return jnp.concatenate([jnp.broadcast_to(far_bias[b, 0:1, low:high], shape) for b in (0, 1)], axis=0)

    def attend(h, part, scores, product):
        top = jnp.max(scores, axis=1, keepdims=True)
        if highs[h]:
            top = jnp.maximum(highs[h][-1], top)
        e = jnp.exp2(scores - top)
        weight[h, :, part] = e
        total = jnp.sum(e, axis=1, keepdims=True)
        rounded = e.astype(BF16)
        acc = product(rounded)
        if part in (OWN, SIDE):
            turned[h, part, :] = rounded.T
        if highs[h]:
            alpha = jnp.exp2(highs[h][-1] - top)
            total = totals[h] * alpha + total
            acc = accs[h] * alpha + acc
        highs[h].append(top)
        totals[h], accs[h] = total, acc

    rows_of = (first, second)

    def own_of(kind, h):
        return kv_near[1:3, rows_of[kind], columns[h]].reshape(2 * ROWS, HEAD_DIM)

    for side in (0, 1):
        sigma = direction(side)
        four, two = -4 * sigma, -2 * sigma
        all_arrived([(two_in.at[side, s], two_recv.at[side, s]) for s in (4, 5)], inside(four))
        send(two_in.at[side, 5], two_in.at[side, 8], two_recv.at[side, 8], at(2 * sigma, core), inside(four, 2 * sigma))
        send(
            two_in.at[side, pl.ds(4, 2)], two_in.at[side, pl.ds(6, 2)],
            two_recv.at[side, 6], at(sigma, core), inside(four, sigma),
        )
        all_arrived([(two_in.at[side, s], two_recv.at[side, s]) for s in (0, 1)], inside(two))
        send(
            two_in.at[side, pl.ds(0, 2)], two_in.at[side, pl.ds(2, 2)],
            two_recv.at[side, 2], at(sigma, core), inside(two, sigma),
        )

    send(g_hbm.at[:, half(other)], g_two.at[mine], sib_recv.at[3], sibling)

    locals_in[4].wait()
    locals_in[6].wait()
    locals_in[5].wait()
    arrived(kv_near.at[1 + other], sib_recv.at[0])
    arrived(q_two.at[theirs], sib_recv.at[2])
    for h in (0, 1):
        scores = dot_nt(q_two[:, columns[h]], own_of(0, h)) * scale + near_bias[:, OWN]
        attend(h, OWN, scores, lambda e: dot(e, own_of(1, h)))

    arrived(kv_near.at[3], near_recv.at[0], inside(1))
    arrived(kv_near.at[0], near_recv.at[1], inside(-1))
    for h in (0, 1):
        query = q_two[:, columns[h]]
        scores = jnp.concatenate(
            [dot_nt(query[first], kv_near[0, first, columns[h]]), dot_nt(query[second], kv_near[3, first, columns[h]])], axis=0
        )
        attend(
            h, SIDE, scores * scale + near_bias[:, SIDE],
            lambda e: jnp.concatenate(
                [dot(e[first], kv_near[0, second, columns[h]]), dot(e[second], kv_near[3, second, columns[h]])], axis=0
            ),
        )

    near_pools = [(dot(pool, kv_near[s, first]), dot(pool, kv_near[s, second])) for s in (0, 3)]
    for side in (0, 1):
        sigma = direction(side)
        arrived(one_in.at[side * 2, ones_only], one_recv.at[side * 2], inside(-2 * sigma))
        arrived(one_in.at[side * 2 + 1], one_recv.at[side * 2 + 1], inside(sigma))
    arrived(far_bias.at[other], sib_recv.at[4])
    nearest = [two_in[0, 1], one_in[1, 2 * ONE :], two_in[1, 1], one_in[3, 2 * ONE :]]
    nearest = [x.astype(F32) for x in nearest]
    for kind, middle in ((0, k_middle), (1, v_middle)):
        ones = slice(kind * ONE, (kind + 1) * ONE)
        rows = slice(kind * TWO, (kind + 1) * TWO)
        for s in range(4):
            middle[s * ONE : (s + 1) * ONE] = one_in[s, ones]
        middle[4 * ONE : 6 * ONE] = jnp.concatenate([p[kind][:ONE] for p in near_pools], axis=0).astype(BF16)
        parts = [x[rows] for x in nearest] + [p[kind][ONE:] for p in near_pools]
        parts += [two_in[side, 0].astype(F32)[rows] for side in (0, 1)]
        middle[6 * ONE :] = jnp.concatenate(parts, axis=0).astype(BF16)
    for h in (0, 1):
        scores = dot_nt(q_two[:, columns[h]], k_middle[:, columns[h]]) * scale + far_of(MIDDLE)
        attend(h, MIDDLE, scores, lambda e: dot(e, v_middle[:, columns[h]]))

    for side in (0, 1):
        sigma = direction(side)
        for s, steps in ((2, 3), (6, 5)):
            arrived(two_in.at[side, pl.ds(s, 2)], two_recv.at[side, s], inside(-steps * sigma))
        arrived(two_in.at[side, 8], two_recv.at[side, 8], inside(-6 * sigma))
    twos = [two_in[side, 2:].astype(F32) for side in (0, 1)]
    for kind, last in ((0, k_last), (1, v_last)):
        rows = slice(kind * TWO, (kind + 1) * TWO)
        parts = [t[:, rows].reshape(7 * TWO, HALF) for t in twos] + [jnp.zeros((2 * TWO, HALF), F32)]
        last[...] = jnp.concatenate(parts, axis=0).astype(BF16)
    for h in (0, 1):
        scores = dot_nt(q_two[:, columns[h]], k_last[:, columns[h]]) * scale + far_of(LAST)
        attend(h, LAST, scores, lambda e: dot(e, v_last[:, columns[h]]))
    inverse_totals = [1.0 / totals[h] for h in (0, 1)]
    for h in (0, 1):
        mixed[:, columns[h]] = accs[h] * inverse_totals[h]

    locals_in[7].wait()
    arrived(g_two.at[theirs], sib_recv.at[3])
    mates = 2 * heads
    place = lane * 2 + core
    value = mixed[...]
    energy = jnp.sum(value * value, axis=1, keepdims=True)
    product = jnp.sum(value * g_two[...].astype(F32), axis=1, keepdims=True)
    stats[place] = jnp.concatenate(
        [row_of(energy[:ROWS]), row_of(energy[ROWS:]), row_of(product[:ROWS]), row_of(product[ROWS:]), jnp.zeros((4, ROWS), F32)],
        axis=0,
    )
    for k in range(1, mates):
        to = (place + k) % mates
        send(stats.at[place], stats.at[place], stat_recv.at[place], {"seq": chip * 2 + to % 2, "head": to // 2})
    factors = [[], []]
    for h in (0, 1):
        for index, part in enumerate((OWN, SIDE, MIDDLE, LAST)):
            factors[h].append(jnp.exp2(highs[h][index] - highs[h][-1]) * inverse_totals[h])
            if part in (MIDDLE, LAST):
                turned[h, part, :] = weight[h, :, part].astype(BF16).T
    flush(keep=mates - 1)
    for k in range(1, mates):
        source = (place + k) % mates
        arrived(stats.at[source], stat_recv.at[source])
    summed = stats[0]
    for k in range(1, mates):
        summed = summed + stats[k]
    width = HEADS * HEAD_DIM
    deltas = [[], []]
    for b, rows in ((0, first), (1, second)):
        inverse = lax.rsqrt(column_of(summed[b : b + 1]) / width + NORM_EPSILON)
        agreement = column_of(summed[2 + b : 3 + b]) * inverse
        normed = mixed[rows] * inverse
        att[rows] = normed.astype(BF16)
        grad = inverse * (g_two[rows].astype(F32) - normed * (agreement / width))
        mixed_grad[rows] = grad
        both = grad.astype(BF16).astype(F32) * mixed[rows]
        for h in (0, 1):
            deltas[h].append(jnp.sum(both[:, columns[h]], axis=1, keepdims=True))
    deltas = [jnp.concatenate(deltas[h], axis=0) for h in (0, 1)]

    out_att = pltpu.make_async_copy(att.at[mine], att_hbm.at[:, half(core)], local_sem.at[8])
    out_att.start()
    send(att.at[theirs], att_hbm.at[:, half(core)], out_recv.at[0], sibling)

    unscale = 1.0 / math.sqrt(HEAD_DIM)
    query_grads = [None, None]

    def scaled(h, part):
        factor = factors[h][(OWN, SIDE, MIDDLE, LAST).index(part)]
        return (mixed_grad[:, columns[h]] * factor).astype(BF16), deltas[h] * factor

    def slopes_of(h, part, products, delta):
        return (weight[h, :, part] * (products - delta)).astype(BF16)

    def plain_backward(part, k_ref, v_ref):
        k_parts, v_parts = [], []
        for h in (0, 1):
            grad, delta = scaled(h, part)
            slopes = slopes_of(h, part, dot_nt(grad, v_ref(h)), delta)
            change = dot(slopes, k_ref(h))
            query_grads[h] = change if query_grads[h] is None else query_grads[h] + change
            k_parts.append(dot_tn(slopes, q_two[:, columns[h]]) * unscale)
            v_parts.append(dot(turned[h, part, :], grad))
        return jnp.concatenate(k_parts, axis=1), jnp.concatenate(v_parts, axis=1)

    def two_rows(pair, low):
        return jnp.concatenate([g[low : low + TWO] for g in pair], axis=0)

    last = plain_backward(LAST, lambda h: k_last[:, columns[h]], lambda h: v_last[:, columns[h]])
    for side in (0, 1):
        sigma = direction(side)
        for s in (1, 2, 5, 6, 7):
            two_out[side, s] = two_rows(last, (side * 7 + s - 1) * TWO).astype(BF16)
        send(
            two_out.at[side, pl.ds(5, 2)], pass_in.at[side, pl.ds(0, 2)],
            pass_recv.at[side, 0], at(-sigma, core), inside(-5 * sigma),
        )
        send(two_out.at[side, 7], pass_in.at[side, 4], pass_recv.at[side, 2], at(-2 * sigma, core), inside(-6 * sigma))
        send(
            two_out.at[side, pl.ds(1, 2)], pass_in.at[side, pl.ds(2, 2)],
            pass_recv.at[side, 1], at(-sigma, core), inside(-3 * sigma),
        )

    middle = plain_backward(MIDDLE, lambda h: k_middle[:, columns[h]], lambda h: v_middle[:, columns[h]])
    for s in range(4):
        for kind in (0, 1):
            pool_out[s, kind * ONE : (kind + 1) * ONE] = middle[kind][s * ONE : (s + 1) * ONE].astype(BF16)
    for b in (0, 1):
        s = 2 * b + 1
        pool_out[s, 2 * ONE :] = two_rows(middle, 6 * ONE + s * TWO).astype(BF16)
        send(pool_out.at[s], one_back.at[core, 1], back_one_recv.at[core, 1], at(direction(b), b), inside(direction(b)))
    for side in (0, 1):
        sigma = direction(side)
        send(
            pool_out.at[2 * side, ones_only], one_back.at[core, 0, ones_only],
            back_one_recv.at[core, 0], at(-2 * sigma, side), inside(-2 * sigma),
        )

    spread = spread_matrix()
    k_sides, v_sides = [[], []], [[], []]
    for h in (0, 1):
        grad, delta = scaled(h, SIDE)
        query = q_two[:, columns[h]]
        products = jnp.concatenate(
            [dot_nt(grad[first], kv_near[0, second, columns[h]]), dot_nt(grad[second], kv_near[3, second, columns[h]])], axis=0
        )
        slopes = slopes_of(h, SIDE, products, delta)
        query_grads[h] = query_grads[h] + jnp.concatenate(
            [dot(slopes[first], kv_near[0, first, columns[h]]), dot(slopes[second], kv_near[3, first, columns[h]])], axis=0
        )
        for b, rows in ((0, second), (1, first)):
            k_sides[b].append(dot_tn(slopes[rows], query[rows]) * unscale)
            v_sides[b].append(dot(turned[h, SIDE, rows], grad[rows]))
    for side in (0, 1):
        sigma = direction(side)
        four = -4 * sigma
        arrived(pass_in.at[side, pl.ds(0, 2)], pass_recv.at[side, 0], inside(sigma, four))
        arrived(pass_in.at[side, 4], pass_recv.at[side, 2], inside(2 * sigma, four))
        passed = [pass_in[side, s].astype(F32) for s in (0, 1, 4)]
        two_out[side, 3] = (two_rows(last, (side * 7 + 2) * TWO) + passed[0]).astype(BF16)
        two_out[side, 4] = (two_rows(last, (side * 7 + 3) * TWO) + passed[1] + passed[2]).astype(BF16)
        send(two_out.at[side, pl.ds(3, 2)], four_in.at[side], pass_recv.at[side, 3], at(-2 * sigma, core), inside(four))

    for b in (0, 1):
        p = 5 - b
        for kind, sides in ((0, k_sides), (1, v_sides)):
            pools = middle[kind]
            small = jnp.concatenate(
                [pools[p * ONE : (p + 1) * ONE], pools[6 * ONE + p * TWO : 6 * ONE + (p + 1) * TWO]], axis=0
            )
            near_out[b, kind * ROWS : (kind + 1) * ROWS] = (
                jnp.concatenate(sides[b], axis=1) + dot(spread, small.astype(BF16))
            ).astype(BF16)
        send(near_out.at[b], near_back.at[core], back_near_recv.at[core], at(-direction(b), b), inside(-direction(b)))

    own = plain_backward(OWN, lambda h: own_of(0, h), lambda h: own_of(1, h))
    flush(keep=2)
    for side in (0, 1):
        sigma = direction(side)
        two = -2 * sigma
        arrived(pass_in.at[side, pl.ds(2, 2)], pass_recv.at[side, 1], inside(sigma, two))
        arrived(four_in.at[side], pass_recv.at[side, 3], inside(2 * sigma, two))
        passed = pass_in[side, 2:4].astype(F32) + four_in[side].astype(F32)
        two_out[side, 0] = (two_rows(middle, 6 * ONE + (6 + side) * TWO) + passed[0]).astype(BF16)
        two_out[side, 8] = (two_rows(middle, 6 * ONE + 2 * side * TWO) + passed[1]).astype(BF16)
        send(two_out.at[side, 0], two_back.at[core, 0], back_two_recv.at[core, 0], at(two, 1 - side), inside(two))
        send(two_out.at[side, 8], two_back.at[core, 1], back_two_recv.at[core, 1], at(two, side), inside(two))

    for kind in (0, 1):
        sib_out[kind * ROWS : (kind + 1) * ROWS] = jnp.where(core == 0, own[kind][second], own[kind][first]).astype(BF16)
    send(sib_out, sib_back, out_recv.at[1], sibling)
    for h in (0, 1):
        dq[:, columns[h]] = (query_grads[h] * unscale).astype(BF16)
    out_dq = pltpu.make_async_copy(dq.at[mine], dq_hbm.at[:, half(core)], local_sem.at[9])
    out_dq.start()
    send(dq.at[theirs], dq_hbm.at[:, half(core)], out_recv.at[2], sibling)

    outs = [out_att, out_dq]

    def finish(h, sem, rest):
        arrived(one_back.at[h, 0, ones_only], back_one_recv.at[h, 0], inside(sided=(2,)))
        arrived(one_back.at[h, 1], back_one_recv.at[h, 1], inside(sided=(-1,)))
        arrived(near_back.at[h], back_near_recv.at[h], inside(sided=(1,)))
        for j, steps in enumerate((-2, 2)):
            arrived(two_back.at[h, j], back_two_recv.at[h, j], inside(sided=(steps,)))
        ones = one_back[h, 1].astype(F32)
        twos = ones[2 * ONE :] + two_back[h, 0].astype(F32) + two_back[h, 1].astype(F32)
        ones = ones[: 2 * ONE] + one_back[h, 0, : 2 * ONE].astype(F32)
        sums = []
        for kind, rows in ((0, first), (1, second)):
            small = jnp.concatenate([ones[kind * ONE : (kind + 1) * ONE], twos[kind * TWO : (kind + 1) * TWO]], axis=0)
            sums.append(near_back[h, rows].astype(F32) + dot(spread, small.astype(BF16)))
        rest = rest()
        for kind, out, out_hbm in ((0, dk, dk_hbm), (1, dv, dv_hbm)):
            out[:, half(h)] = (sums[kind] + rest[kind]).astype(BF16)
            outs.append(pltpu.make_async_copy(out.at[:, half(h)], out_hbm.at[:, half(h)], local_sem.at[sem + kind]))
            outs[-1].start()

    def from_sibling():
        arrived(sib_back, out_recv.at[1])
        return [sib_back[rows].astype(F32) for rows in (first, second)]

    finish(core, 10, lambda: [jnp.where(core == 0, own[kind][first], own[kind][second]) for kind in (0, 1)])
    finish(other, 12, from_sibling)
    arrived(att_hbm.at[:, half(other)], out_recv.at[0])
    arrived(dq_hbm.at[:, half(other)], out_recv.at[2])
    flush()
    for copy in outs:
        copy.wait()


def write_out(*refs):
    *arrays, sems = refs
    rows = arrays[0].shape[0] // 2
    copies = []
    for i in range(4):
        for j in (0, 1):
            part = pl.ds(j * rows, rows)
            copies.append(pltpu.make_async_copy(arrays[i].at[part], arrays[4 + i].at[part], sems.at[2 * i + j]))
    for copy in copies:
        copy.start()
    for copy in copies:
        copy.wait()


def body(queries, keys, values, out_grad, level_choice, frame_lengths):
    rows, width = queries.shape
    vmem = pltpu.VMEM
    dma = pltpu.SemaphoreType.DMA
    out = jax.ShapeDtypeStruct((rows, width), BF16)
    limit = 40 * 1024 * 1024
    arrays = (queries, keys, values, out_grad, level_choice, frame_lengths.reshape(1, -1))
    results = pl.pallas_call(
        kernel,
        out_shape=(out, out, out, out),
        in_specs=[pl.BlockSpec(memory_space=pl.ANY)] * 6,
        out_specs=(pl.BlockSpec(memory_space=pl.ANY),) * 4,
        scratch_shapes=[
            vmem((2 * ROWS, width), BF16),
            vmem((2 * ROWS, HALF), BF16),
            vmem((2 * ROWS, HALF), BF16),
            vmem((4, 2 * ROWS, HALF), BF16),
            vmem((POOLED, width), BF16),
            vmem((4, POOLED, HALF), BF16),
            vmem((2, 9, 2 * TWO, HALF), BF16),
            vmem((256, HALF), BF16),
            vmem((256, HALF), BF16),
            vmem((128, HALF), BF16),
            vmem((128, HALF), BF16),
            pltpu.SMEM((1, 4), jnp.int32),
            vmem((1, 64), jnp.int32),
            vmem((2 * ROWS, 384), F32),
            vmem((2, 8, FAR), F32),
            vmem((2, 2 * ROWS, 768), F32),
            vmem((2, 768, 2 * ROWS), BF16),
            vmem((2 * ROWS, HALF), F32),
            vmem((8, 8, ROWS), F32),
            vmem((2 * ROWS, HALF), F32),
            vmem((2 * ROWS, HALF), BF16),
            vmem((2 * ROWS, HALF), BF16),
            vmem((2, 2 * ROWS, HALF), BF16),
            vmem((4, POOLED, HALF), BF16),
            vmem((2, 9, 2 * TWO, HALF), BF16),
            vmem((2 * ROWS, HALF), BF16),
            vmem((2, 5, 2 * TWO, HALF), BF16),
            vmem((2, 2, 2 * TWO, HALF), BF16),
            vmem((2, 2 * ROWS, HALF), BF16),
            vmem((2, 2, POOLED, HALF), BF16),
            vmem((2, 2, 2 * TWO, HALF), BF16),
            vmem((2 * ROWS, HALF), BF16),
            vmem((ROWS, width), BF16),
            vmem((ROWS, width), BF16),
            dma((14,)),
            dma((64,)),
            dma((5,)),
            dma((2,)),
            dma((4,)),
            dma((2, 9)),
            dma((8,)),
            dma((2, 4)),
            dma((2,)),
            dma((2, 2)),
            dma((2, 2)),
            dma((3,)),
        ],
        compiler_params=pltpu.CompilerParams(collective_id=0, has_side_effects=True, vmem_limit_bytes=limit),
        cost_estimate=pl.CostEstimate(flops=700_000_000, bytes_accessed=1_100_000, transcendentals=400_000),
    )(*[pltpu.with_memory_space_constraint(array, pltpu.HBM) for array in arrays])
    return pl.pallas_call(
        write_out,
        out_shape=(out, out, out, out),
        in_specs=[pl.BlockSpec(memory_space=pl.ANY)] * 4,
        out_specs=(pl.BlockSpec(memory_space=pl.ANY),) * 4,
        scratch_shapes=[dma((8,))],
        compiler_params=pltpu.CompilerParams(vmem_limit_bytes=limit),
        cost_estimate=pl.CostEstimate(flops=0, bytes_accessed=1_100_000, transcendentals=0),
    )(*results)


def solution(mesh):
    in_specs = (
        P("seq", "head"),
        P("seq", "head"),
        P("seq", "head"),
        P("seq", "head"),
        P("seq", None),
        P(),
    )
    out_specs = (P("seq", "head"), P("seq", "head"), P("seq", "head"), P("seq", "head"))
    return jax.shard_map(body, mesh=mesh, in_specs=in_specs, out_specs=out_specs, check_vma=False)
```

```python
import math

import jax
import jax.numpy as jnp
from jax import lax
from jax.experimental import pallas as pl
from jax.experimental.pallas import tpu as pltpu
from jax.sharding import PartitionSpec as P

HEADS = 16
HEAD_DIM = 128
POOL1 = 4
POOL2 = 16
REACH1 = 3
REACH2 = 11
MATCHED_FRAME_ADD = 1.0
NORM_EPSILON = 1e-06

MESH = pl.DeviceIdType.MESH
F32 = jnp.float32
BF16 = jnp.bfloat16
LOG2E = math.log2(math.e)
MASKED = -1e30

ROWS = 128
HALF = 256
ONE = ROWS // POOL1
TWO = ROWS // POOL2
POOLED = 2 * (ONE + TWO)
NEAR = 3 * ROWS
FAR = 384

STEPS_ONE = (2, -1)


def direction(b):
    return 2 * b - 1


REL_ONE = [-2 * steps * direction(b) + b for b in (0, 1) for steps in STEPS_ONE] + [-1, 2]


def relative_two(side):
    sigma = direction(side)
    spots = [(2, 1 - side), (3, 1 - side), (3, side), (4, 1 - side), (4, side), (5, 1 - side), (5, side), (6, side)]
    return [-2 * k * sigma + b for k, b in spots]


REL_TWO = [relative_two(0), relative_two(1)]
REL_MIDDLE = REL_ONE + [REL_TWO[0][0], REL_TWO[1][0]]
REL_LAST = REL_TWO[0][1:] + REL_TWO[1][1:]
OWN, SIDE, MIDDLE, LAST = slice(0, 256), slice(256, 384), slice(384, 640), slice(640, 768)


def dot_nt(a, b):
    return lax.dot_general(a, b, (((1,), (1,)), ((), ())), preferred_element_type=F32)


def dot_tn(a, b):
    return lax.dot_general(a, b, (((0,), (0,)), ((), ())), preferred_element_type=F32)


def dot(a, b):
    return jnp.dot(a, b, preferred_element_type=F32)


def pool_matrix():
    r = lax.broadcasted_iota(jnp.int32, (ONE + TWO, ROWS), 0)
    t = lax.broadcasted_iota(jnp.int32, (ONE + TWO, ROWS), 1)
    one = jnp.where((t >> 2) == r, 1.0 / POOL1, 0.0)
    two = jnp.where((t >> 4) == r - ONE, 1.0 / POOL2, 0.0)
    return jnp.where(r < ONE, one, two).astype(BF16)


def spread_matrix():
    t = lax.broadcasted_iota(jnp.int32, (ROWS, ONE + TWO), 0)
    r = lax.broadcasted_iota(jnp.int32, (ROWS, ONE + TWO), 1)
    one = jnp.where((t >> 2) == r, 1.0 / POOL1, 0.0)
    two = jnp.where((t >> 4) == r - ONE, 1.0 / POOL2, 0.0)
    return jnp.where(r < ONE, one, two).astype(BF16)


def column_of(row):
    i = lax.broadcasted_iota(jnp.int32, (ROWS, ROWS), 0)
    j = lax.broadcasted_iota(jnp.int32, (ROWS, ROWS), 1)
    return jnp.sum(jnp.where(i == j, row, 0.0), axis=1, keepdims=True)


def row_of(column):
    i = lax.broadcasted_iota(jnp.int32, (ROWS, ROWS), 0)
    j = lax.broadcasted_iota(jnp.int32, (ROWS, ROWS), 1)
    return jnp.sum(jnp.where(i == j, column, 0.0), axis=0, keepdims=True)


def kernel(
    q_hbm, k_hbm, v_hbm, g_hbm, level_hbm, frame_hbm,
    att_hbm, dq_hbm, dk_hbm, dv_hbm,
    kv_own, q_two, g_two, kv_near, pooled, one_in, two_in, k_middle, v_middle, k_last, v_last,
    level_s, frame_v, near_bias, far_bias, weight, turned, mixed, stats,
    mixed_grad, att, dq, near_out, pool_out, two_out, sib_out,
    pass_in, near_back, one_back, two_back, sib_back, dk, dv,
    local_sem, send_sem, sib_recv, near_recv, one_recv, two_recv, stat_recv, pass_recv,
    back_near_recv, back_one_recv, back_two_recv, out_recv,
):
    blocks = lax.axis_size("seq")
    chips = blocks // 2
    heads = lax.axis_size("head")
    me = lax.axis_index("seq")
    lane = lax.axis_index("head")
    chip = me // 2
    core = me % 2
    other = 1 - core
    d = direction(core)

    def at(steps, c):
        return {"seq": ((chip + steps + chips) % chips) * 2 + c}

    sibling = {"seq": chip * 2 + other}

    def half(h):
        return pl.ds(pl.multiple_of(h * HALF, HALF), HALF)

    def remote(src, dst, send, recv, device):
        return pltpu.make_async_remote_copy(
            src_ref=src, dst_ref=dst, send_sem=send, recv_sem=recv, device_id=device, device_id_type=MESH
        )

    def inside(*steps, sided=()):
        away = [s for s in steps] + [s * d for s in sided]
        known = True
        for s in away:
            known = known & (chip + s >= 0) & (chip + s < chips)
        return (steps, sided), known

    def only(when, act):
        if when is None:
            act()
        else:
            pl.when(when[1])(act)

    sent = 0
    started = []

    def send(src, dst, recv, device, when=None):
        nonlocal sent
        copy = remote(src, dst, send_sem.at[sent], recv, device)
        sent += 1
        only(when, copy.start)
        started.append((copy, when))

    def flush(keep=0):
        groups = {}
        done = len(started) - keep
        for copy, when in started[:done]:
            groups.setdefault(when and when[0], (when, []))[1].append(copy)
        del started[:done]
        for when, copies in groups.values():

            def wait_all(copies=copies):
                for copy in copies:
                    copy.wait_send()

            only(when, wait_all)

    def arrived(ref, sem, when=None):
        only(when, remote(ref, ref, sem, sem, sibling).wait_recv)

    @pl.when((chip < 6) | (chip >= chips - 6))
    def _():
        for ref in (one_in, two_in, pass_in, near_back, one_back, two_back):
            ref[...] = jnp.zeros(ref.shape, ref.dtype)
        for s in (0, 3):
            kv_near[s] = jnp.zeros(kv_near.shape[1:], BF16)

    mine = pl.ds(pl.multiple_of(core * ROWS, ROWS), ROWS)
    theirs = pl.ds(pl.multiple_of(other * ROWS, ROWS), ROWS)
    k_rows, v_rows = pl.ds(0, ROWS), pl.ds(ROWS, ROWS)
    locals_in = [
        pltpu.make_async_copy(k_hbm, kv_own.at[k_rows], local_sem.at[0]),
        pltpu.make_async_copy(v_hbm, kv_own.at[v_rows], local_sem.at[1]),
        pltpu.make_async_copy(level_hbm, level_s, local_sem.at[2]),
        pltpu.make_async_copy(frame_hbm, frame_v, local_sem.at[3]),
        pltpu.make_async_copy(k_hbm.at[:, half(core)], kv_near.at[1 + core, k_rows], local_sem.at[4]),
        pltpu.make_async_copy(v_hbm.at[:, half(core)], kv_near.at[1 + core, v_rows], local_sem.at[5]),
        pltpu.make_async_copy(q_hbm.at[:, half(core)], q_two.at[mine], local_sem.at[6]),
        pltpu.make_async_copy(g_hbm.at[:, half(core)], g_two.at[mine], local_sem.at[7]),
    ]
    for copy in locals_in[:2]:
        copy.start()

    barrier = pltpu.get_barrier_semaphore()
    partners = [sibling]
    for k in range(1, heads):
        for c in (0, 1):
            partners.append({"seq": chip * 2 + c, "head": (lane + k) % heads})
    expected = len(partners)

    def greet(devices):
        for device in devices:
            pl.semaphore_signal(barrier, inc=1, device_id=device, device_id_type=MESH)

    for steps in (4, -4, 2, -2, 1, -1):
        when = inside(steps)
        only(when, lambda: greet([at(steps, 0), at(steps, 1)]))
        expected = expected + jnp.where(when[1], 2, 0)
    greet(partners)
    for copy in locals_in[2:]:
        copy.start()

    locals_in[0].wait()
    locals_in[1].wait()
    pool = pool_matrix()
    k_pool = dot(pool, kv_own[:ROWS])
    v_pool = dot(pool, kv_own[ROWS:])
    pooled[0 : 2 * ONE, :] = jnp.concatenate([k_pool[:ONE], v_pool[:ONE]], axis=0).astype(BF16)
    pooled[2 * ONE :, :] = jnp.concatenate([k_pool[ONE:], v_pool[ONE:]], axis=0).astype(BF16)

    pl.semaphore_wait(barrier, expected)

    def send_two(steps, side, spot):
        for h in (0, 1):
            send(
                pooled.at[pl.ds(2 * ONE, 2 * TWO), half(h)], two_in.at[side, spot],
                two_recv.at[side, spot], at(steps * d, h), inside(sided=(steps,)),
            )

    send_two(4, core, 5)
    send_two(-4, other, 4)
    send_two(2, core, 1)
    send_two(-2, other, 0)
    send(kv_own.at[:, half(other)], kv_near.at[1 + core], sib_recv.at[0], sibling)
    send(q_hbm.at[:, half(other)], q_two.at[mine], sib_recv.at[2], sibling)
    for h in (0, 1):
        send(kv_own.at[:, half(h)], kv_near.at[3 - 3 * core], near_recv.at[core], at(d, h), inside(sided=(1,)))
    for h in (0, 1):
        send(
            pooled.at[:, half(h)], one_in.at[core * 2 + 1],
            one_recv.at[core * 2 + 1], at(-d, h), inside(sided=(-1,)),
        )
    ones_only = pl.ds(0, 2 * ONE)
    for h in (0, 1):
        send(
            pooled.at[ones_only, half(h)], one_in.at[core * 2, ones_only],
            one_recv.at[core * 2], at(2 * d, h), inside(sided=(2,)),
        )

    locals_in[2].wait()
    locals_in[3].wait()
    table = [level_s[0, i] for i in range(4)]
    spot = lax.broadcasted_iota(jnp.int32, (8, FAR), 1)
    row = jnp.full((8, FAR), MASKED, F32)

    def level_at(offset):
        choice = jnp.where(offset == -3, table[0], table[1])
        choice = jnp.where(offset == 2, table[2], choice)
        return jnp.where(offset == 3, table[3], choice)

    def slot_bias(rel, wanted, most, bias):
        offset = rel - core
        distance = jnp.abs(offset)
        block = 2 * chip + rel
        inside = (distance >= 2) & (distance <= most) & (block >= 0) & (block < blocks)
        chosen = (distance > REACH1) | (level_at(offset) == wanted)
        return jnp.where(inside & chosen, bias * LOG2E, MASKED)

    for s, rel in enumerate(REL_ONE):
        value = slot_bias(rel, 1, REACH1, math.log(POOL1))
        row = jnp.where((spot >= s * ONE) & (spot < (s + 1) * ONE), value, row)
    for s, rel in enumerate(REL_MIDDLE + REL_LAST):
        low = len(REL_ONE) * ONE + s * TWO
        value = slot_bias(rel, 2, REACH2, math.log(POOL2))
        row = jnp.where((spot >= low) & (spot < low + TWO), value, row)
    far_bias[core] = row
    send(far_bias.at[core], far_bias.at[core], sib_recv.at[4], sibling)

    lengths = frame_v[...].astype(F32)
    count = lengths.shape[1]
    i = lax.broadcasted_iota(jnp.int32, (count, count), 0)
    j = lax.broadcasted_iota(jnp.int32, (count, count), 1)
    ends_column = jnp.sum(jnp.where(j <= i, lengths, 0.0), axis=1, keepdims=True)
    ends_row = jnp.sum(jnp.where(i == j, ends_column, 0.0), axis=0, keepdims=True)
    start = (2 * chip - 1) * ROWS
    key_place = start + lax.broadcasted_iota(jnp.int32, (1, 4 * ROWS), 1)
    key_frame = jnp.sum(jnp.where(key_place.astype(F32) >= ends_column, 1.0, 0.0), axis=0, keepdims=True)
    key_inside = (key_place >= 0) & (key_place < blocks * ROWS)
    for b in (0, 1):
        place = start + (b + 1) * ROWS + lax.broadcasted_iota(jnp.int32, (ROWS, 1), 0)
        frame = jnp.sum(jnp.where(place.astype(F32) >= ends_row, 1.0, 0.0), axis=1, keepdims=True)
        matched = jnp.where(frame == key_frame, MATCHED_FRAME_ADD * LOG2E, 0.0)
        matched = jnp.where(key_inside, matched, MASKED)
        rows = slice(b * ROWS, (b + 1) * ROWS)
        near_bias[rows, OWN] = matched[:, ROWS : 3 * ROWS]
        near_bias[rows, SIDE] = matched[:, 3 * b * ROWS : (3 * b + 1) * ROWS]

    scale = LOG2E / math.sqrt(HEAD_DIM)
    columns = [slice(h * HEAD_DIM, (h + 1) * HEAD_DIM) for h in (0, 1)]
    first, second = slice(0, ROWS), slice(ROWS, 2 * ROWS)
    highs, totals, accs = [[], []], [None, None], [None, None]

    def far_of(part):
        low, high = part.start - MIDDLE.start, part.stop - MIDDLE.start
        shape = (ROWS, high - low)
        return jnp.concatenate([jnp.broadcast_to(far_bias[b, 0:1, low:high], shape) for b in (0, 1)], axis=0)

    def attend(h, part, scores, product):
        top = jnp.max(scores, axis=1, keepdims=True)
        if highs[h]:
            top = jnp.maximum(highs[h][-1], top)
        e = jnp.exp2(scores - top)
        weight[h, :, part] = e
        total = jnp.sum(e, axis=1, keepdims=True)
        rounded = e.astype(BF16)
        acc = product(rounded)
        if part in (OWN, SIDE):
            turned[h, part, :] = rounded.T
        if highs[h]:
            alpha = jnp.exp2(highs[h][-1] - top)
            total = totals[h] * alpha + total
            acc = accs[h] * alpha + acc
        highs[h].append(top)
        totals[h], accs[h] = total, acc

    rows_of = (first, second)

    def own_of(kind, h):
        return kv_near[1:3, rows_of[kind], columns[h]].reshape(2 * ROWS, HEAD_DIM)

    for side in (0, 1):
        sigma = direction(side)
        four, two = -4 * sigma, -2 * sigma
        for s in (4, 5):
            arrived(two_in.at[side, s], two_recv.at[side, s], inside(four))
        send(two_in.at[side, 5], two_in.at[side, 8], two_recv.at[side, 8], at(2 * sigma, core), inside(four, 2 * sigma))
        send(
            two_in.at[side, pl.ds(4, 2)], two_in.at[side, pl.ds(6, 2)],
            two_recv.at[side, 6], at(sigma, core), inside(four, sigma),
        )
        for s in (0, 1):
            arrived(two_in.at[side, s], two_recv.at[side, s], inside(two))
        send(
            two_in.at[side, pl.ds(0, 2)], two_in.at[side, pl.ds(2, 2)],
            two_recv.at[side, 2], at(sigma, core), inside(two, sigma),
        )

    send(g_hbm.at[:, half(other)], g_two.at[mine], sib_recv.at[3], sibling)

    locals_in[4].wait()
    locals_in[6].wait()
    locals_in[5].wait()
    arrived(kv_near.at[1 + other], sib_recv.at[0])
    arrived(q_two.at[theirs], sib_recv.at[2])
    for h in (0, 1):
        scores = dot_nt(q_two[:, columns[h]], own_of(0, h)) * scale + near_bias[:, OWN]
        attend(h, OWN, scores, lambda e: dot(e, own_of(1, h)))

    arrived(kv_near.at[3], near_recv.at[0], inside(1))
    arrived(kv_near.at[0], near_recv.at[1], inside(-1))
    for h in (0, 1):
        query = q_two[:, columns[h]]
        scores = jnp.concatenate(
            [dot_nt(query[first], kv_near[0, first, columns[h]]), dot_nt(query[second], kv_near[3, first, columns[h]])], axis=0
        )
        attend(
            h, SIDE, scores * scale + near_bias[:, SIDE],
            lambda e: jnp.concatenate(
                [dot(e[first], kv_near[0, second, columns[h]]), dot(e[second], kv_near[3, second, columns[h]])], axis=0
            ),
        )

    near_pools = [(dot(pool, kv_near[s, first]), dot(pool, kv_near[s, second])) for s in (0, 3)]
    for side in (0, 1):
        sigma = direction(side)
        arrived(one_in.at[side * 2, ones_only], one_recv.at[side * 2], inside(-2 * sigma))
        arrived(one_in.at[side * 2 + 1], one_recv.at[side * 2 + 1], inside(sigma))
    arrived(far_bias.at[other], sib_recv.at[4])
    nearest = [two_in[0, 1], one_in[1, 2 * ONE :], two_in[1, 1], one_in[3, 2 * ONE :]]
    nearest = [x.astype(F32) for x in nearest]
    for kind, middle in ((0, k_middle), (1, v_middle)):
        ones = slice(kind * ONE, (kind + 1) * ONE)
        rows = slice(kind * TWO, (kind + 1) * TWO)
        for s in range(4):
            middle[s * ONE : (s + 1) * ONE] = one_in[s, ones]
        middle[4 * ONE : 6 * ONE] = jnp.concatenate([p[kind][:ONE] for p in near_pools], axis=0).astype(BF16)
        parts = [x[rows] for x in nearest] + [p[kind][ONE:] for p in near_pools]
        parts += [two_in[side, 0].astype(F32)[rows] for side in (0, 1)]
        middle[6 * ONE :] = jnp.concatenate(parts, axis=0).astype(BF16)
    for h in (0, 1):
        scores = dot_nt(q_two[:, columns[h]], k_middle[:, columns[h]]) * scale + far_of(MIDDLE)
        attend(h, MIDDLE, scores, lambda e: dot(e, v_middle[:, columns[h]]))

    for side in (0, 1):
        sigma = direction(side)
        for s, steps in ((2, 3), (6, 5)):
            arrived(two_in.at[side, pl.ds(s, 2)], two_recv.at[side, s], inside(-steps * sigma))
        arrived(two_in.at[side, 8], two_recv.at[side, 8], inside(-6 * sigma))
    twos = [two_in[side, 2:].astype(F32) for side in (0, 1)]
    for kind, last in ((0, k_last), (1, v_last)):
        rows = slice(kind * TWO, (kind + 1) * TWO)
        parts = [t[:, rows].reshape(7 * TWO, HALF) for t in twos] + [jnp.zeros((2 * TWO, HALF), F32)]
        last[...] = jnp.concatenate(parts, axis=0).astype(BF16)
    for h in (0, 1):
        scores = dot_nt(q_two[:, columns[h]], k_last[:, columns[h]]) * scale + far_of(LAST)
        attend(h, LAST, scores, lambda e: dot(e, v_last[:, columns[h]]))
    inverse_totals = [1.0 / totals[h] for h in (0, 1)]
    for h in (0, 1):
        mixed[:, columns[h]] = accs[h] * inverse_totals[h]

    locals_in[7].wait()
    arrived(g_two.at[theirs], sib_recv.at[3])
    mates = 2 * heads
    place = lane * 2 + core
    value = mixed[...]
    energy = jnp.sum(value * value, axis=1, keepdims=True)
    product = jnp.sum(value * g_two[...].astype(F32), axis=1, keepdims=True)
    stats[place] = jnp.concatenate(
        [row_of(energy[:ROWS]), row_of(energy[ROWS:]), row_of(product[:ROWS]), row_of(product[ROWS:]), jnp.zeros((4, ROWS), F32)],
        axis=0,
    )
    for k in range(1, mates):
        to = (place + k) % mates
        send(stats.at[place], stats.at[place], stat_recv.at[place], {"seq": chip * 2 + to % 2, "head": to // 2})
    factors = [[], []]
    for h in (0, 1):
        for index, part in enumerate((OWN, SIDE, MIDDLE, LAST)):
            factors[h].append(jnp.exp2(highs[h][index] - highs[h][-1]) * inverse_totals[h])
            if part in (MIDDLE, LAST):
                turned[h, part, :] = weight[h, :, part].astype(BF16).T
    flush(keep=mates - 1)
    for k in range(1, mates):
        source = (place + k) % mates
        arrived(stats.at[source], stat_recv.at[source])
    summed = stats[0]
    for k in range(1, mates):
        summed = summed + stats[k]
    width = HEADS * HEAD_DIM
    deltas = [[], []]
    for b, rows in ((0, first), (1, second)):
        inverse = lax.rsqrt(column_of(summed[b : b + 1]) / width + NORM_EPSILON)
        agreement = column_of(summed[2 + b : 3 + b]) * inverse
        normed = mixed[rows] * inverse
        att[rows] = normed.astype(BF16)
        grad = inverse * (g_two[rows].astype(F32) - normed * (agreement / width))
        mixed_grad[rows] = grad
        both = grad.astype(BF16).astype(F32) * mixed[rows]
        for h in (0, 1):
            deltas[h].append(jnp.sum(both[:, columns[h]], axis=1, keepdims=True))
    deltas = [jnp.concatenate(deltas[h], axis=0) for h in (0, 1)]

    out_att = pltpu.make_async_copy(att.at[mine], att_hbm.at[:, half(core)], local_sem.at[8])
    out_att.start()
    send(att.at[theirs], att_hbm.at[:, half(core)], out_recv.at[0], sibling)

    unscale = 1.0 / math.sqrt(HEAD_DIM)
    query_grads = [None, None]

    def scaled(h, part):
        factor = factors[h][(OWN, SIDE, MIDDLE, LAST).index(part)]
        return (mixed_grad[:, columns[h]] * factor).astype(BF16), deltas[h] * factor

    def slopes_of(h, part, products, delta):
        return (weight[h, :, part] * (products - delta)).astype(BF16)

    def plain_backward(part, k_ref, v_ref):
        k_parts, v_parts = [], []
        for h in (0, 1):
            grad, delta = scaled(h, part)
            slopes = slopes_of(h, part, dot_nt(grad, v_ref(h)), delta)
            change = dot(slopes, k_ref(h))
            query_grads[h] = change if query_grads[h] is None else query_grads[h] + change
            k_parts.append(dot_tn(slopes, q_two[:, columns[h]]) * unscale)
            v_parts.append(dot(turned[h, part, :], grad))
        return jnp.concatenate(k_parts, axis=1), jnp.concatenate(v_parts, axis=1)

    def two_rows(pair, low):
        return jnp.concatenate([g[low : low + TWO] for g in pair], axis=0)

    last = plain_backward(LAST, lambda h: k_last[:, columns[h]], lambda h: v_last[:, columns[h]])
    for side in (0, 1):
        sigma = direction(side)
        for s in (1, 2, 5, 6, 7):
            two_out[side, s] = two_rows(last, (side * 7 + s - 1) * TWO).astype(BF16)
        send(
            two_out.at[side, pl.ds(5, 2)], pass_in.at[side, pl.ds(0, 2)],
            pass_recv.at[side, 0], at(-sigma, core), inside(-5 * sigma),
        )
        send(two_out.at[side, 7], pass_in.at[side, 4], pass_recv.at[side, 2], at(-2 * sigma, core), inside(-6 * sigma))
        send(
            two_out.at[side, pl.ds(1, 2)], pass_in.at[side, pl.ds(2, 2)],
            pass_recv.at[side, 1], at(-sigma, core), inside(-3 * sigma),
        )

    middle = plain_backward(MIDDLE, lambda h: k_middle[:, columns[h]], lambda h: v_middle[:, columns[h]])
    for s in range(4):
        for kind in (0, 1):
            pool_out[s, kind * ONE : (kind + 1) * ONE] = middle[kind][s * ONE : (s + 1) * ONE].astype(BF16)
    for b in (0, 1):
        s = 2 * b + 1
        pool_out[s, 2 * ONE :] = two_rows(middle, 6 * ONE + s * TWO).astype(BF16)
        send(pool_out.at[s], one_back.at[core, 1], back_one_recv.at[core, 1], at(direction(b), b), inside(direction(b)))
    for side in (0, 1):
        sigma = direction(side)
        send(
            pool_out.at[2 * side, ones_only], one_back.at[core, 0, ones_only],
            back_one_recv.at[core, 0], at(-2 * sigma, side), inside(-2 * sigma),
        )

    spread = spread_matrix()
    k_sides, v_sides = [[], []], [[], []]
    for h in (0, 1):
        grad, delta = scaled(h, SIDE)
        query = q_two[:, columns[h]]
        products = jnp.concatenate(
            [dot_nt(grad[first], kv_near[0, second, columns[h]]), dot_nt(grad[second], kv_near[3, second, columns[h]])], axis=0
        )
        slopes = slopes_of(h, SIDE, products, delta)
        query_grads[h] = query_grads[h] + jnp.concatenate(
            [dot(slopes[first], kv_near[0, first, columns[h]]), dot(slopes[second], kv_near[3, first, columns[h]])], axis=0
        )
        for b, rows in ((0, second), (1, first)):
            k_sides[b].append(dot_tn(slopes[rows], query[rows]) * unscale)
            v_sides[b].append(dot(turned[h, SIDE, rows], grad[rows]))
    for side in (0, 1):
        sigma = direction(side)
        four, two = -4 * sigma, -2 * sigma
        arrived(pass_in.at[side, pl.ds(0, 2)], pass_recv.at[side, 0], inside(sigma, four))
        arrived(pass_in.at[side, 4], pass_recv.at[side, 2], inside(2 * sigma, four))
        arrived(pass_in.at[side, pl.ds(2, 2)], pass_recv.at[side, 1], inside(sigma, two))
        passed = pass_in[side].astype(F32)
        two_out[side, 3] = (two_rows(last, (side * 7 + 2) * TWO) + passed[0]).astype(BF16)
        two_out[side, 4] = (two_rows(last, (side * 7 + 3) * TWO) + passed[1] + passed[4]).astype(BF16)
        two_out[side, 0] = (two_rows(middle, 6 * ONE + (6 + side) * TWO) + passed[2]).astype(BF16)
        two_out[side, 8] = (two_rows(middle, 6 * ONE + 2 * side * TWO) + passed[3]).astype(BF16)
        for s, spot, owner, steps in ((3, 2, 1 - side, four), (4, 3, side, four), (0, 0, 1 - side, two), (8, 1, side, two)):
            send(
                two_out.at[side, s], two_back.at[core, spot],
                back_two_recv.at[core, spot], at(steps, owner), inside(steps),
            )

    for b in (0, 1):
        p = 5 - b
        for kind, sides in ((0, k_sides), (1, v_sides)):
            pools = middle[kind]
            small = jnp.concatenate(
                [pools[p * ONE : (p + 1) * ONE], pools[6 * ONE + p * TWO : 6 * ONE + (p + 1) * TWO]], axis=0
            )
            near_out[b, kind * ROWS : (kind + 1) * ROWS] = (
                jnp.concatenate(sides[b], axis=1) + dot(spread, small.astype(BF16))
            ).astype(BF16)
        send(near_out.at[b], near_back.at[core], back_near_recv.at[core], at(-direction(b), b), inside(-direction(b)))

    own = plain_backward(OWN, lambda h: own_of(0, h), lambda h: own_of(1, h))
    for kind in (0, 1):
        sib_out[kind * ROWS : (kind + 1) * ROWS] = jnp.where(core == 0, own[kind][second], own[kind][first]).astype(BF16)
    send(sib_out, sib_back, out_recv.at[1], sibling)
    for h in (0, 1):
        dq[:, columns[h]] = (query_grads[h] * unscale).astype(BF16)
    out_dq = pltpu.make_async_copy(dq.at[mine], dq_hbm.at[:, half(core)], local_sem.at[9])
    out_dq.start()
    send(dq.at[theirs], dq_hbm.at[:, half(core)], out_recv.at[2], sibling)

    flush(keep=4)
    outs = [out_att, out_dq]

    def finish(h, sem, rest):
        arrived(one_back.at[h, 0, ones_only], back_one_recv.at[h, 0], inside(sided=(2,)))
        arrived(one_back.at[h, 1], back_one_recv.at[h, 1], inside(sided=(-1,)))
        arrived(near_back.at[h], back_near_recv.at[h], inside(sided=(1,)))
        for j, steps in enumerate((-2, 2, -4, 4)):
            arrived(two_back.at[h, j], back_two_recv.at[h, j], inside(sided=(steps,)))
        ones = one_back[h, 1].astype(F32)
        twos = ones[2 * ONE :]
        for j in range(4):
            twos = twos + two_back[h, j].astype(F32)
        ones = ones[: 2 * ONE] + one_back[h, 0, : 2 * ONE].astype(F32)
        sums = []
        for kind, rows in ((0, first), (1, second)):
            small = jnp.concatenate([ones[kind * ONE : (kind + 1) * ONE], twos[kind * TWO : (kind + 1) * TWO]], axis=0)
            sums.append(near_back[h, rows].astype(F32) + dot(spread, small.astype(BF16)))
        rest = rest()
        for kind, out, out_hbm in ((0, dk, dk_hbm), (1, dv, dv_hbm)):
            out[:, half(h)] = (sums[kind] + rest[kind]).astype(BF16)
            outs.append(pltpu.make_async_copy(out.at[:, half(h)], out_hbm.at[:, half(h)], local_sem.at[sem + kind]))
            outs[-1].start()

    def from_sibling():
        arrived(sib_back, out_recv.at[1])
        return [sib_back[rows].astype(F32) for rows in (first, second)]

    finish(core, 10, lambda: [jnp.where(core == 0, own[kind][first], own[kind][second]) for kind in (0, 1)])
    finish(other, 12, from_sibling)
    arrived(att_hbm.at[:, half(other)], out_recv.at[0])
    arrived(dq_hbm.at[:, half(other)], out_recv.at[2])
    flush()
    for copy in outs:
        copy.wait()


def write_out(*refs):
    *arrays, sems = refs
    copies = [pltpu.make_async_copy(arrays[i], arrays[4 + i], sems.at[i]) for i in range(4)]
    for copy in copies:
        copy.start()
    for copy in copies:
        copy.wait()


def body(queries, keys, values, out_grad, level_choice, frame_lengths):
    rows, width = queries.shape
    vmem = pltpu.VMEM
    dma = pltpu.SemaphoreType.DMA
    out = jax.ShapeDtypeStruct((rows, width), BF16)
    limit = 40 * 1024 * 1024
    arrays = (queries, keys, values, out_grad, level_choice, frame_lengths.reshape(1, -1))
    results = pl.pallas_call(
        kernel,
        out_shape=(out, out, out, out),
        in_specs=[pl.BlockSpec(memory_space=pl.ANY)] * 6,
        out_specs=(pl.BlockSpec(memory_space=pl.ANY),) * 4,
        scratch_shapes=[
            vmem((2 * ROWS, width), BF16),
            vmem((2 * ROWS, HALF), BF16),
            vmem((2 * ROWS, HALF), BF16),
            vmem((4, 2 * ROWS, HALF), BF16),
            vmem((POOLED, width), BF16),
            vmem((4, POOLED, HALF), BF16),
            vmem((2, 9, 2 * TWO, HALF), BF16),
            vmem((256, HALF), BF16),
            vmem((256, HALF), BF16),
            vmem((128, HALF), BF16),
            vmem((128, HALF), BF16),
            pltpu.SMEM((1, 4), jnp.int32),
            vmem((1, 64), jnp.int32),
            vmem((2 * ROWS, 384), F32),
            vmem((2, 8, FAR), F32),
            vmem((2, 2 * ROWS, 768), F32),
            vmem((2, 768, 2 * ROWS), BF16),
            vmem((2 * ROWS, HALF), F32),
            vmem((8, 8, ROWS), F32),
            vmem((2 * ROWS, HALF), F32),
            vmem((2 * ROWS, HALF), BF16),
            vmem((2 * ROWS, HALF), BF16),
            vmem((2, 2 * ROWS, HALF), BF16),
            vmem((4, POOLED, HALF), BF16),
            vmem((2, 9, 2 * TWO, HALF), BF16),
            vmem((2 * ROWS, HALF), BF16),
            vmem((2, 5, 2 * TWO, HALF), BF16),
            vmem((2, 2 * ROWS, HALF), BF16),
            vmem((2, 2, POOLED, HALF), BF16),
            vmem((2, 4, 2 * TWO, HALF), BF16),
            vmem((2 * ROWS, HALF), BF16),
            vmem((ROWS, width), BF16),
            vmem((ROWS, width), BF16),
            dma((14,)),
            dma((64,)),
            dma((5,)),
            dma((2,)),
            dma((4,)),
            dma((2, 9)),
            dma((8,)),
            dma((2, 3)),
            dma((2,)),
            dma((2, 2)),
            dma((2, 4)),
            dma((3,)),
        ],
        compiler_params=pltpu.CompilerParams(collective_id=0, has_side_effects=True, vmem_limit_bytes=limit),
        cost_estimate=pl.CostEstimate(flops=700_000_000, bytes_accessed=1_100_000, transcendentals=400_000),
    )(*[pltpu.with_memory_space_constraint(array, pltpu.HBM) for array in arrays])
    return pl.pallas_call(
        write_out,
        out_shape=(out, out, out, out),
        in_specs=[pl.BlockSpec(memory_space=pl.ANY)] * 4,
        out_specs=(pl.BlockSpec(memory_space=pl.ANY),) * 4,
        scratch_shapes=[dma((4,))],
        compiler_params=pltpu.CompilerParams(vmem_limit_bytes=limit),
        cost_estimate=pl.CostEstimate(flops=0, bytes_accessed=1_100_000, transcendentals=0),
    )(*results)


def solution(mesh):
    in_specs = (
        P("seq", "head"),
        P("seq", "head"),
        P("seq", "head"),
        P("seq", "head"),
        P("seq", None),
        P(),
    )
    out_specs = (P("seq", "head"), P("seq", "head"), P("seq", "head"), P("seq", "head"))
    return jax.shard_map(body, mesh=mesh, in_specs=in_specs, out_specs=out_specs, check_vma=False)
```

```python
import math

import jax
import jax.numpy as jnp
from jax import lax
from jax.experimental import pallas as pl
from jax.experimental.pallas import tpu as pltpu
from jax.sharding import PartitionSpec as P

HEADS = 16
HEAD_DIM = 128
POOL1 = 4
POOL2 = 16
REACH1 = 3
REACH2 = 11
MATCHED_FRAME_ADD = 1.0
NORM_EPSILON = 1e-06

MESH = pl.DeviceIdType.MESH
F32 = jnp.float32
BF16 = jnp.bfloat16
LOG2E = math.log2(math.e)
MASKED = -1e30

ROWS = 128
HALF = 256
ONE = ROWS // POOL1
TWO = ROWS // POOL2
POOLED = 2 * (ONE + TWO)
NEAR = 3 * ROWS
FAR = 384

STEPS_ONE = (2, -1)


def direction(b):
    return 2 * b - 1


REL_ONE = [-2 * steps * direction(b) + b for b in (0, 1) for steps in STEPS_ONE] + [-1, 2]


def relative_two(side):
    sigma = direction(side)
    spots = [(2, 1 - side), (3, 1 - side), (3, side), (4, 1 - side), (4, side), (5, 1 - side), (5, side), (6, side)]
    return [-2 * k * sigma + b for k, b in spots]


REL_TWO = [relative_two(0), relative_two(1)]
REL_MIDDLE = REL_ONE + [REL_TWO[0][0], REL_TWO[1][0]]
REL_LAST = REL_TWO[0][1:] + REL_TWO[1][1:]
OWN, SIDE, MIDDLE, LAST = slice(0, 256), slice(256, 384), slice(384, 640), slice(640, 768)


def dot_nt(a, b):
    return lax.dot_general(a, b, (((1,), (1,)), ((), ())), preferred_element_type=F32)


def dot_tn(a, b):
    return lax.dot_general(a, b, (((0,), (0,)), ((), ())), preferred_element_type=F32)


def dot(a, b):
    return jnp.dot(a, b, preferred_element_type=F32)


def pool_matrix():
    r = lax.broadcasted_iota(jnp.int32, (ONE + TWO, ROWS), 0)
    t = lax.broadcasted_iota(jnp.int32, (ONE + TWO, ROWS), 1)
    one = jnp.where((t >> 2) == r, 1.0 / POOL1, 0.0)
    two = jnp.where((t >> 4) == r - ONE, 1.0 / POOL2, 0.0)
    return jnp.where(r < ONE, one, two).astype(BF16)


def spread_matrix():
    t = lax.broadcasted_iota(jnp.int32, (ROWS, ONE + TWO), 0)
    r = lax.broadcasted_iota(jnp.int32, (ROWS, ONE + TWO), 1)
    one = jnp.where((t >> 2) == r, 1.0 / POOL1, 0.0)
    two = jnp.where((t >> 4) == r - ONE, 1.0 / POOL2, 0.0)
    return jnp.where(r < ONE, one, two).astype(BF16)


def column_of(row):
    i = lax.broadcasted_iota(jnp.int32, (ROWS, ROWS), 0)
    j = lax.broadcasted_iota(jnp.int32, (ROWS, ROWS), 1)
    return jnp.sum(jnp.where(i == j, row, 0.0), axis=1, keepdims=True)


def row_of(column):
    i = lax.broadcasted_iota(jnp.int32, (ROWS, ROWS), 0)
    j = lax.broadcasted_iota(jnp.int32, (ROWS, ROWS), 1)
    return jnp.sum(jnp.where(i == j, column, 0.0), axis=0, keepdims=True)


def kernel(
    q_hbm, k_hbm, v_hbm, g_hbm, level_hbm, frame_hbm,
    att_hbm, dq_hbm, dk_hbm, dv_hbm,
    kv_own, q_two, g_two, kv_near, pooled, one_in, two_in, k_middle, v_middle, k_last, v_last,
    level_s, frame_v, near_bias, far_bias, weight, turned, mixed, stats,
    mixed_grad, att, dq, near_out, pool_out, two_out, sib_out,
    pass_in, near_back, one_back, two_back, sib_back, dk, dv,
    local_sem, send_sem, sib_recv, near_recv, one_recv, two_recv, stat_recv, pass_recv,
    back_near_recv, back_one_recv, back_two_recv, out_recv,
):
    blocks = lax.axis_size("seq")
    chips = blocks // 2
    heads = lax.axis_size("head")
    me = lax.axis_index("seq")
    lane = lax.axis_index("head")
    chip = me // 2
    core = me % 2
    other = 1 - core
    d = direction(core)

    def at(steps, c):
        return {"seq": ((chip + steps + chips) % chips) * 2 + c}

    sibling = {"seq": chip * 2 + other}

    def half(h):
        return pl.ds(pl.multiple_of(h * HALF, HALF), HALF)

    def remote(src, dst, send, recv, device):
        return pltpu.make_async_remote_copy(
            src_ref=src, dst_ref=dst, send_sem=send, recv_sem=recv, device_id=device, device_id_type=MESH
        )

    def inside(*steps, sided=()):
        away = [s for s in steps] + [s * d for s in sided]
        known = True
        for s in away:
            known = known & (chip + s >= 0) & (chip + s < chips)
        return (steps, sided), known

    def only(when, act):
        if when is None:
            act()
        else:
            pl.when(when[1])(act)

    sent = 0
    started = []

    def send(src, dst, recv, device, when=None):
        nonlocal sent
        copy = remote(src, dst, send_sem.at[sent], recv, device)
        sent += 1
        only(when, copy.start)
        started.append((copy, when))

    def flush(keep=0):
        groups = {}
        done = len(started) - keep
        for copy, when in started[:done]:
            groups.setdefault(when and when[0], (when, []))[1].append(copy)
        del started[:done]
        for when, copies in groups.values():

            def wait_all(copies=copies):
                for copy in copies:
                    copy.wait_send()

            only(when, wait_all)

    def arrived(ref, sem, when=None):
        only(when, remote(ref, ref, sem, sem, sibling).wait_recv)

    @pl.when((chip < 6) | (chip >= chips - 6))
    def _():
        for ref in (one_in, two_in, pass_in, near_back, one_back, two_back):
            ref[...] = jnp.zeros(ref.shape, ref.dtype)
        for s in (0, 3):
            kv_near[s] = jnp.zeros(kv_near.shape[1:], BF16)

    mine = pl.ds(pl.multiple_of(core * ROWS, ROWS), ROWS)
    theirs = pl.ds(pl.multiple_of(other * ROWS, ROWS), ROWS)
    k_rows, v_rows = pl.ds(0, ROWS), pl.ds(ROWS, ROWS)
    locals_in = [
        pltpu.make_async_copy(k_hbm, kv_own.at[k_rows], local_sem.at[0]),
        pltpu.make_async_copy(v_hbm, kv_own.at[v_rows], local_sem.at[1]),
        pltpu.make_async_copy(level_hbm, level_s, local_sem.at[2]),
        pltpu.make_async_copy(frame_hbm, frame_v, local_sem.at[3]),
        pltpu.make_async_copy(k_hbm.at[:, half(core)], kv_near.at[1 + core, k_rows], local_sem.at[4]),
        pltpu.make_async_copy(v_hbm.at[:, half(core)], kv_near.at[1 + core, v_rows], local_sem.at[5]),
        pltpu.make_async_copy(q_hbm.at[:, half(core)], q_two.at[mine], local_sem.at[6]),
        pltpu.make_async_copy(g_hbm.at[:, half(core)], g_two.at[mine], local_sem.at[7]),
    ]
    for copy in locals_in[:2]:
        copy.start()

    barrier = pltpu.get_barrier_semaphore()
    partners = [sibling]
    for k in range(1, heads):
        for c in (0, 1):
            partners.append({"seq": chip * 2 + c, "head": (lane + k) % heads})
    expected = len(partners)

    def greet(devices):
        for device in devices:
            pl.semaphore_signal(barrier, inc=1, device_id=device, device_id_type=MESH)

    for steps in (4, -4, 2, -2, 1, -1):
        when = inside(steps)
        only(when, lambda: greet([at(steps, 0), at(steps, 1)]))
        expected = expected + jnp.where(when[1], 2, 0)
    greet(partners)
    for copy in locals_in[2:]:
        copy.start()

    locals_in[0].wait()
    locals_in[1].wait()
    pool = pool_matrix()
    k_pool = dot(pool, kv_own[:ROWS])
    v_pool = dot(pool, kv_own[ROWS:])
    pooled[0 : 2 * ONE, :] = jnp.concatenate([k_pool[:ONE], v_pool[:ONE]], axis=0).astype(BF16)
    pooled[2 * ONE :, :] = jnp.concatenate([k_pool[ONE:], v_pool[ONE:]], axis=0).astype(BF16)

    pl.semaphore_wait(barrier, expected)

    def send_two(steps, side, spot):
        for h in (0, 1):
            send(
                pooled.at[pl.ds(2 * ONE, 2 * TWO), half(h)], two_in.at[side, spot],
                two_recv.at[side, spot], at(steps * d, h), inside(sided=(steps,)),
            )

    send_two(4, core, 5)
    send_two(-4, other, 4)
    send_two(2, core, 1)
    send_two(-2, other, 0)
    send(kv_own.at[:, half(other)], kv_near.at[1 + core], sib_recv.at[0], sibling)
    send(q_hbm.at[:, half(other)], q_two.at[mine], sib_recv.at[2], sibling)
    for h in (0, 1):
        send(kv_own.at[:, half(h)], kv_near.at[3 - 3 * core], near_recv.at[core], at(d, h), inside(sided=(1,)))
    for h in (0, 1):
        send(
            pooled.at[:, half(h)], one_in.at[core * 2 + 1],
            one_recv.at[core * 2 + 1], at(-d, h), inside(sided=(-1,)),
        )
    ones_only = pl.ds(0, 2 * ONE)
    for h in (0, 1):
        send(
            pooled.at[ones_only, half(h)], one_in.at[core * 2, ones_only],
            one_recv.at[core * 2], at(2 * d, h), inside(sided=(2,)),
        )

    locals_in[2].wait()
    locals_in[3].wait()
    table = [level_s[0, i] for i in range(4)]
    spot = lax.broadcasted_iota(jnp.int32, (8, FAR), 1)
    row = jnp.full((8, FAR), MASKED, F32)

    def level_at(offset):
        choice = jnp.where(offset == -3, table[0], table[1])
        choice = jnp.where(offset == 2, table[2], choice)
        return jnp.where(offset == 3, table[3], choice)

    def slot_bias(rel, wanted, most, bias):
        offset = rel - core
        distance = jnp.abs(offset)
        block = 2 * chip + rel
        inside = (distance >= 2) & (distance <= most) & (block >= 0) & (block < blocks)
        chosen = (distance > REACH1) | (level_at(offset) == wanted)
        return jnp.where(inside & chosen, bias * LOG2E, MASKED)

    for s, rel in enumerate(REL_ONE):
        value = slot_bias(rel, 1, REACH1, math.log(POOL1))
        row = jnp.where((spot >= s * ONE) & (spot < (s + 1) * ONE), value, row)
    for s, rel in enumerate(REL_MIDDLE + REL_LAST):
        low = len(REL_ONE) * ONE + s * TWO
        value = slot_bias(rel, 2, REACH2, math.log(POOL2))
        row = jnp.where((spot >= low) & (spot < low + TWO), value, row)
    far_bias[core] = row
    send(far_bias.at[core], far_bias.at[core], sib_recv.at[4], sibling)

    lengths = frame_v[...].astype(F32)
    count = lengths.shape[1]
    i = lax.broadcasted_iota(jnp.int32, (count, count), 0)
    j = lax.broadcasted_iota(jnp.int32, (count, count), 1)
    ends_column = jnp.sum(jnp.where(j <= i, lengths, 0.0), axis=1, keepdims=True)
    ends_row = jnp.sum(jnp.where(i == j, ends_column, 0.0), axis=0, keepdims=True)
    start = (2 * chip - 1) * ROWS
    key_place = start + lax.broadcasted_iota(jnp.int32, (1, 4 * ROWS), 1)
    key_frame = jnp.sum(jnp.where(key_place.astype(F32) >= ends_column, 1.0, 0.0), axis=0, keepdims=True)
    key_inside = (key_place >= 0) & (key_place < blocks * ROWS)
    for b in (0, 1):
        place = start + (b + 1) * ROWS + lax.broadcasted_iota(jnp.int32, (ROWS, 1), 0)
        frame = jnp.sum(jnp.where(place.astype(F32) >= ends_row, 1.0, 0.0), axis=1, keepdims=True)
        matched = jnp.where(frame == key_frame, MATCHED_FRAME_ADD * LOG2E, 0.0)
        matched = jnp.where(key_inside, matched, MASKED)
        rows = slice(b * ROWS, (b + 1) * ROWS)
        near_bias[rows, OWN] = matched[:, ROWS : 3 * ROWS]
        near_bias[rows, SIDE] = matched[:, 3 * b * ROWS : (3 * b + 1) * ROWS]

    scale = LOG2E / math.sqrt(HEAD_DIM)
    columns = [slice(h * HEAD_DIM, (h + 1) * HEAD_DIM) for h in (0, 1)]
    first, second = slice(0, ROWS), slice(ROWS, 2 * ROWS)
    highs, totals, accs = [[], []], [None, None], [None, None]

    def far_of(part):
        low, high = part.start - MIDDLE.start, part.stop - MIDDLE.start
        shape = (ROWS, high - low)
        return jnp.concatenate([jnp.broadcast_to(far_bias[b, 0:1, low:high], shape) for b in (0, 1)], axis=0)

    def attend(h, part, scores, product):
        top = jnp.max(scores, axis=1, keepdims=True)
        if highs[h]:
            top = jnp.maximum(highs[h][-1], top)
        e = jnp.exp2(scores - top)
        weight[h, :, part] = e
        total = jnp.sum(e, axis=1, keepdims=True)
        rounded = e.astype(BF16)
        acc = product(rounded)
        if part in (OWN, SIDE):
            turned[h, part, :] = rounded.T
        if highs[h]:
            alpha = jnp.exp2(highs[h][-1] - top)
            total = totals[h] * alpha + total
            acc = accs[h] * alpha + acc
        highs[h].append(top)
        totals[h], accs[h] = total, acc

    rows_of = (first, second)

    def own_of(kind, h):
        return kv_near[1:3, rows_of[kind], columns[h]].reshape(2 * ROWS, HEAD_DIM)

    for side in (0, 1):
        sigma = direction(side)
        four, two = -4 * sigma, -2 * sigma
        for s in (4, 5):
            arrived(two_in.at[side, s], two_recv.at[side, s], inside(four))
        send(two_in.at[side, 5], two_in.at[side, 8], two_recv.at[side, 8], at(2 * sigma, core), inside(four, 2 * sigma))
        send(
            two_in.at[side, pl.ds(4, 2)], two_in.at[side, pl.ds(6, 2)],
            two_recv.at[side, 6], at(sigma, core), inside(four, sigma),
        )
        for s in (0, 1):
            arrived(two_in.at[side, s], two_recv.at[side, s], inside(two))
        send(
            two_in.at[side, pl.ds(0, 2)], two_in.at[side, pl.ds(2, 2)],
            two_recv.at[side, 2], at(sigma, core), inside(two, sigma),
        )

    send(g_hbm.at[:, half(other)], g_two.at[mine], sib_recv.at[3], sibling)

    locals_in[4].wait()
    locals_in[6].wait()
    locals_in[5].wait()
    arrived(kv_near.at[1 + other], sib_recv.at[0])
    arrived(q_two.at[theirs], sib_recv.at[2])
    for h in (0, 1):
        scores = dot_nt(q_two[:, columns[h]], own_of(0, h)) * scale + near_bias[:, OWN]
        attend(h, OWN, scores, lambda e: dot(e, own_of(1, h)))

    arrived(kv_near.at[3], near_recv.at[0], inside(1))
    arrived(kv_near.at[0], near_recv.at[1], inside(-1))
    for h in (0, 1):
        query = q_two[:, columns[h]]
        scores = jnp.concatenate(
            [dot_nt(query[first], kv_near[0, first, columns[h]]), dot_nt(query[second], kv_near[3, first, columns[h]])], axis=0
        )
        attend(
            h, SIDE, scores * scale + near_bias[:, SIDE],
            lambda e: jnp.concatenate(
                [dot(e[first], kv_near[0, second, columns[h]]), dot(e[second], kv_near[3, second, columns[h]])], axis=0
            ),
        )

    near_pools = [(dot(pool, kv_near[s, first]), dot(pool, kv_near[s, second])) for s in (0, 3)]
    for side in (0, 1):
        sigma = direction(side)
        arrived(one_in.at[side * 2, ones_only], one_recv.at[side * 2], inside(-2 * sigma))
        arrived(one_in.at[side * 2 + 1], one_recv.at[side * 2 + 1], inside(sigma))
    arrived(far_bias.at[other], sib_recv.at[4])
    nearest = [two_in[0, 1], one_in[1, 2 * ONE :], two_in[1, 1], one_in[3, 2 * ONE :]]
    nearest = [x.astype(F32) for x in nearest]
    for kind, middle in ((0, k_middle), (1, v_middle)):
        ones = slice(kind * ONE, (kind + 1) * ONE)
        rows = slice(kind * TWO, (kind + 1) * TWO)
        for s in range(4):
            middle[s * ONE : (s + 1) * ONE] = one_in[s, ones]
        middle[4 * ONE : 6 * ONE] = jnp.concatenate([p[kind][:ONE] for p in near_pools], axis=0).astype(BF16)
        parts = [x[rows] for x in nearest] + [p[kind][ONE:] for p in near_pools]
        parts += [two_in[side, 0].astype(F32)[rows] for side in (0, 1)]
        middle[6 * ONE :] = jnp.concatenate(parts, axis=0).astype(BF16)
    for h in (0, 1):
        scores = dot_nt(q_two[:, columns[h]], k_middle[:, columns[h]]) * scale + far_of(MIDDLE)
        attend(h, MIDDLE, scores, lambda e: dot(e, v_middle[:, columns[h]]))

    for side in (0, 1):
        sigma = direction(side)
        for s, steps in ((2, 3), (6, 5)):
            arrived(two_in.at[side, pl.ds(s, 2)], two_recv.at[side, s], inside(-steps * sigma))
        arrived(two_in.at[side, 8], two_recv.at[side, 8], inside(-6 * sigma))
    twos = [two_in[side, 2:].astype(F32) for side in (0, 1)]
    for kind, last in ((0, k_last), (1, v_last)):
        rows = slice(kind * TWO, (kind + 1) * TWO)
        parts = [t[:, rows].reshape(7 * TWO, HALF) for t in twos] + [jnp.zeros((2 * TWO, HALF), F32)]
        last[...] = jnp.concatenate(parts, axis=0).astype(BF16)
    for h in (0, 1):
        scores = dot_nt(q_two[:, columns[h]], k_last[:, columns[h]]) * scale + far_of(LAST)
        attend(h, LAST, scores, lambda e: dot(e, v_last[:, columns[h]]))
    inverse_totals = [1.0 / totals[h] for h in (0, 1)]
    for h in (0, 1):
        mixed[:, columns[h]] = accs[h] * inverse_totals[h]

    locals_in[7].wait()
    arrived(g_two.at[theirs], sib_recv.at[3])
    mates = 2 * heads
    place = lane * 2 + core
    value = mixed[...]
    energy = jnp.sum(value * value, axis=1, keepdims=True)
    product = jnp.sum(value * g_two[...].astype(F32), axis=1, keepdims=True)
    stats[place] = jnp.concatenate(
        [row_of(energy[:ROWS]), row_of(energy[ROWS:]), row_of(product[:ROWS]), row_of(product[ROWS:]), jnp.zeros((4, ROWS), F32)],
        axis=0,
    )
    for k in range(1, mates):
        to = (place + k) % mates
        send(stats.at[place], stats.at[place], stat_recv.at[place], {"seq": chip * 2 + to % 2, "head": to // 2})
    factors = [[], []]
    for h in (0, 1):
        for index, part in enumerate((OWN, SIDE, MIDDLE, LAST)):
            factors[h].append(jnp.exp2(highs[h][index] - highs[h][-1]) * inverse_totals[h])
            if part in (MIDDLE, LAST):
                turned[h, part, :] = weight[h, :, part].astype(BF16).T
    flush(keep=mates - 1)
    for k in range(1, mates):
        source = (place + k) % mates
        arrived(stats.at[source], stat_recv.at[source])
    summed = stats[0]
    for k in range(1, mates):
        summed = summed + stats[k]
    width = HEADS * HEAD_DIM
    deltas = [[], []]
    for b, rows in ((0, first), (1, second)):
        inverse = lax.rsqrt(column_of(summed[b : b + 1]) / width + NORM_EPSILON)
        agreement = column_of(summed[2 + b : 3 + b]) * inverse
        normed = mixed[rows] * inverse
        att[rows] = normed.astype(BF16)
        grad = inverse * (g_two[rows].astype(F32) - normed * (agreement / width))
        mixed_grad[rows] = grad
        both = grad.astype(BF16).astype(F32) * mixed[rows]
        for h in (0, 1):
            deltas[h].append(jnp.sum(both[:, columns[h]], axis=1, keepdims=True))
    deltas = [jnp.concatenate(deltas[h], axis=0) for h in (0, 1)]

    out_att = pltpu.make_async_copy(att.at[mine], att_hbm.at[:, half(core)], local_sem.at[8])
    out_att.start()
    send(att.at[theirs], att_hbm.at[:, half(core)], out_recv.at[0], sibling)

    unscale = 1.0 / math.sqrt(HEAD_DIM)
    query_grads = [None, None]

    def scaled(h, part):
        factor = factors[h][(OWN, SIDE, MIDDLE, LAST).index(part)]
        return (mixed_grad[:, columns[h]] * factor).astype(BF16), deltas[h] * factor

    def slopes_of(h, part, products, delta):
        return (weight[h, :, part] * (products - delta)).astype(BF16)

    def plain_backward(part, k_ref, v_ref):
        k_parts, v_parts = [], []
        for h in (0, 1):
            grad, delta = scaled(h, part)
            slopes = slopes_of(h, part, dot_nt(grad, v_ref(h)), delta)
            change = dot(slopes, k_ref(h))
            query_grads[h] = change if query_grads[h] is None else query_grads[h] + change
            k_parts.append(dot_tn(slopes, q_two[:, columns[h]]) * unscale)
            v_parts.append(dot(turned[h, part, :], grad))
        return jnp.concatenate(k_parts, axis=1), jnp.concatenate(v_parts, axis=1)

    def two_rows(pair, low):
        return jnp.concatenate([g[low : low + TWO] for g in pair], axis=0)

    last = plain_backward(LAST, lambda h: k_last[:, columns[h]], lambda h: v_last[:, columns[h]])
    for side in (0, 1):
        sigma = direction(side)
        for s in (1, 2, 5, 6, 7):
            two_out[side, s] = two_rows(last, (side * 7 + s - 1) * TWO).astype(BF16)
        send(
            two_out.at[side, pl.ds(5, 2)], pass_in.at[side, pl.ds(0, 2)],
            pass_recv.at[side, 0], at(-sigma, core), inside(-5 * sigma),
        )
        send(two_out.at[side, 7], pass_in.at[side, 4], pass_recv.at[side, 2], at(-2 * sigma, core), inside(-6 * sigma))
        send(
            two_out.at[side, pl.ds(1, 2)], pass_in.at[side, pl.ds(2, 2)],
            pass_recv.at[side, 1], at(-sigma, core), inside(-3 * sigma),
        )

    middle = plain_backward(MIDDLE, lambda h: k_middle[:, columns[h]], lambda h: v_middle[:, columns[h]])
    for s in range(4):
        for kind in (0, 1):
            pool_out[s, kind * ONE : (kind + 1) * ONE] = middle[kind][s * ONE : (s + 1) * ONE].astype(BF16)
    for b in (0, 1):
        s = 2 * b + 1
        pool_out[s, 2 * ONE :] = two_rows(middle, 6 * ONE + s * TWO).astype(BF16)
        send(pool_out.at[s], one_back.at[core, 1], back_one_recv.at[core, 1], at(direction(b), b), inside(direction(b)))
    for side in (0, 1):
        sigma = direction(side)
        send(
            pool_out.at[2 * side, ones_only], one_back.at[core, 0, ones_only],
            back_one_recv.at[core, 0], at(-2 * sigma, side), inside(-2 * sigma),
        )

    spread = spread_matrix()
    k_sides, v_sides = [[], []], [[], []]
    for h in (0, 1):
        grad, delta = scaled(h, SIDE)
        query = q_two[:, columns[h]]
        products = jnp.concatenate(
            [dot_nt(grad[first], kv_near[0, second, columns[h]]), dot_nt(grad[second], kv_near[3, second, columns[h]])], axis=0
        )
        slopes = slopes_of(h, SIDE, products, delta)
        query_grads[h] = query_grads[h] + jnp.concatenate(
            [dot(slopes[first], kv_near[0, first, columns[h]]), dot(slopes[second], kv_near[3, first, columns[h]])], axis=0
        )
        for b, rows in ((0, second), (1, first)):
            k_sides[b].append(dot_tn(slopes[rows], query[rows]) * unscale)
            v_sides[b].append(dot(turned[h, SIDE, rows], grad[rows]))
    for b in (0, 1):
        p = 5 - b
        for kind, sides in ((0, k_sides), (1, v_sides)):
            pools = middle[kind]
            small = jnp.concatenate(
                [pools[p * ONE : (p + 1) * ONE], pools[6 * ONE + p * TWO : 6 * ONE + (p + 1) * TWO]], axis=0
            )
            near_out[b, kind * ROWS : (kind + 1) * ROWS] = (
                jnp.concatenate(sides[b], axis=1) + dot(spread, small.astype(BF16))
            ).astype(BF16)
        send(near_out.at[b], near_back.at[core], back_near_recv.at[core], at(-direction(b), b), inside(-direction(b)))

    for side in (0, 1):
        sigma = direction(side)
        four, two = -4 * sigma, -2 * sigma
        arrived(pass_in.at[side, pl.ds(0, 2)], pass_recv.at[side, 0], inside(sigma, four))
        arrived(pass_in.at[side, 4], pass_recv.at[side, 2], inside(2 * sigma, four))
        arrived(pass_in.at[side, pl.ds(2, 2)], pass_recv.at[side, 1], inside(sigma, two))
        passed = pass_in[side].astype(F32)
        two_out[side, 3] = (two_rows(last, (side * 7 + 2) * TWO) + passed[0]).astype(BF16)
        two_out[side, 4] = (two_rows(last, (side * 7 + 3) * TWO) + passed[1] + passed[4]).astype(BF16)
        two_out[side, 0] = (two_rows(middle, 6 * ONE + (6 + side) * TWO) + passed[2]).astype(BF16)
        two_out[side, 8] = (two_rows(middle, 6 * ONE + 2 * side * TWO) + passed[3]).astype(BF16)
        for s, spot, owner, steps in ((3, 2, 1 - side, four), (4, 3, side, four), (0, 0, 1 - side, two), (8, 1, side, two)):
            send(
                two_out.at[side, s], two_back.at[core, spot],
                back_two_recv.at[core, spot], at(steps, owner), inside(steps),
            )

    own = plain_backward(OWN, lambda h: own_of(0, h), lambda h: own_of(1, h))
    for kind in (0, 1):
        sib_out[kind * ROWS : (kind + 1) * ROWS] = jnp.where(core == 0, own[kind][second], own[kind][first]).astype(BF16)
    send(sib_out, sib_back, out_recv.at[1], sibling)
    for h in (0, 1):
        dq[:, columns[h]] = (query_grads[h] * unscale).astype(BF16)
    out_dq = pltpu.make_async_copy(dq.at[mine], dq_hbm.at[:, half(core)], local_sem.at[9])
    out_dq.start()
    send(dq.at[theirs], dq_hbm.at[:, half(core)], out_recv.at[2], sibling)

    flush(keep=4)
    outs = [out_att, out_dq]

    def finish(h, sem, rest):
        arrived(one_back.at[h, 0, ones_only], back_one_recv.at[h, 0], inside(sided=(2,)))
        arrived(one_back.at[h, 1], back_one_recv.at[h, 1], inside(sided=(-1,)))
        arrived(near_back.at[h], back_near_recv.at[h], inside(sided=(1,)))
        for j, steps in enumerate((-2, 2, -4, 4)):
            arrived(two_back.at[h, j], back_two_recv.at[h, j], inside(sided=(steps,)))
        ones = one_back[h, 1].astype(F32)
        twos = ones[2 * ONE :]
        for j in range(4):
            twos = twos + two_back[h, j].astype(F32)
        ones = ones[: 2 * ONE] + one_back[h, 0, : 2 * ONE].astype(F32)
        sums = []
        for kind, rows in ((0, first), (1, second)):
            small = jnp.concatenate([ones[kind * ONE : (kind + 1) * ONE], twos[kind * TWO : (kind + 1) * TWO]], axis=0)
            sums.append(near_back[h, rows].astype(F32) + dot(spread, small.astype(BF16)))
        rest = rest()
        for kind, out, out_hbm in ((0, dk, dk_hbm), (1, dv, dv_hbm)):
            out[:, half(h)] = (sums[kind] + rest[kind]).astype(BF16)
            outs.append(pltpu.make_async_copy(out.at[:, half(h)], out_hbm.at[:, half(h)], local_sem.at[sem + kind]))
            outs[-1].start()

    def from_sibling():
        arrived(sib_back, out_recv.at[1])
        return [sib_back[rows].astype(F32) for rows in (first, second)]

    finish(core, 10, lambda: [jnp.where(core == 0, own[kind][first], own[kind][second]) for kind in (0, 1)])
    finish(other, 12, from_sibling)
    arrived(att_hbm.at[:, half(other)], out_recv.at[0])
    arrived(dq_hbm.at[:, half(other)], out_recv.at[2])
    flush()
    for copy in outs:
        copy.wait()


def write_out(*refs):
    *arrays, sems = refs
    copies = [pltpu.make_async_copy(arrays[i], arrays[4 + i], sems.at[i]) for i in range(4)]
    for copy in copies:
        copy.start()
    for copy in copies:
        copy.wait()


def body(queries, keys, values, out_grad, level_choice, frame_lengths):
    rows, width = queries.shape
    vmem = pltpu.VMEM
    dma = pltpu.SemaphoreType.DMA
    out = jax.ShapeDtypeStruct((rows, width), BF16)
    limit = 40 * 1024 * 1024
    arrays = (queries, keys, values, out_grad, level_choice, frame_lengths.reshape(1, -1))
    results = pl.pallas_call(
        kernel,
        out_shape=(out, out, out, out),
        in_specs=[pl.BlockSpec(memory_space=pl.ANY)] * 6,
        out_specs=(pl.BlockSpec(memory_space=pl.ANY),) * 4,
        scratch_shapes=[
            vmem((2 * ROWS, width), BF16),
            vmem((2 * ROWS, HALF), BF16),
            vmem((2 * ROWS, HALF), BF16),
            vmem((4, 2 * ROWS, HALF), BF16),
            vmem((POOLED, width), BF16),
            vmem((4, POOLED, HALF), BF16),
            vmem((2, 9, 2 * TWO, HALF), BF16),
            vmem((256, HALF), BF16),
            vmem((256, HALF), BF16),
            vmem((128, HALF), BF16),
            vmem((128, HALF), BF16),
            pltpu.SMEM((1, 4), jnp.int32),
            vmem((1, 64), jnp.int32),
            vmem((2 * ROWS, 384), F32),
            vmem((2, 8, FAR), F32),
            vmem((2, 2 * ROWS, 768), F32),
            vmem((2, 768, 2 * ROWS), BF16),
            vmem((2 * ROWS, HALF), F32),
            vmem((8, 8, ROWS), F32),
            vmem((2 * ROWS, HALF), F32),
            vmem((2 * ROWS, HALF), BF16),
            vmem((2 * ROWS, HALF), BF16),
            vmem((2, 2 * ROWS, HALF), BF16),
            vmem((4, POOLED, HALF), BF16),
            vmem((2, 9, 2 * TWO, HALF), BF16),
            vmem((2 * ROWS, HALF), BF16),
            vmem((2, 5, 2 * TWO, HALF), BF16),
            vmem((2, 2 * ROWS, HALF), BF16),
            vmem((2, 2, POOLED, HALF), BF16),
            vmem((2, 4, 2 * TWO, HALF), BF16),
            vmem((2 * ROWS, HALF), BF16),
            vmem((ROWS, width), BF16),
            vmem((ROWS, width), BF16),
            dma((14,)),
            dma((64,)),
            dma((5,)),
            dma((2,)),
            dma((4,)),
            dma((2, 9)),
            dma((8,)),
            dma((2, 3)),
            dma((2,)),
            dma((2, 2)),
            dma((2, 4)),
            dma((3,)),
        ],
        compiler_params=pltpu.CompilerParams(collective_id=0, has_side_effects=True, vmem_limit_bytes=limit),
        cost_estimate=pl.CostEstimate(flops=700_000_000, bytes_accessed=1_100_000, transcendentals=400_000),
    )(*[pltpu.with_memory_space_constraint(array, pltpu.HBM) for array in arrays])
    return pl.pallas_call(
        write_out,
        out_shape=(out, out, out, out),
        in_specs=[pl.BlockSpec(memory_space=pl.ANY)] * 4,
        out_specs=(pl.BlockSpec(memory_space=pl.ANY),) * 4,
        scratch_shapes=[dma((4,))],
        compiler_params=pltpu.CompilerParams(vmem_limit_bytes=limit),
        cost_estimate=pl.CostEstimate(flops=0, bytes_accessed=1_100_000, transcendentals=0),
    )(*results)


def solution(mesh):
    in_specs = (
        P("seq", "head"),
        P("seq", "head"),
        P("seq", "head"),
        P("seq", "head"),
        P("seq", None),
        P(),
    )
    out_specs = (P("seq", "head"), P("seq", "head"), P("seq", "head"), P("seq", "head"))
    return jax.shard_map(body, mesh=mesh, in_specs=in_specs, out_specs=out_specs, check_vma=False)
```

```python
import math

import jax
import jax.numpy as jnp
from jax import lax
from jax.experimental import pallas as pl
from jax.experimental.pallas import tpu as pltpu
from jax.sharding import PartitionSpec as P

HEADS = 16
HEAD_DIM = 128
POOL1 = 4
POOL2 = 16
REACH1 = 3
REACH2 = 11
MATCHED_FRAME_ADD = 1.0
NORM_EPSILON = 1e-06

MESH = pl.DeviceIdType.MESH
F32 = jnp.float32
BF16 = jnp.bfloat16
LOG2E = math.log2(math.e)
MASKED = -1e30

ROWS = 128
HALF = 256
ONE = ROWS // POOL1
TWO = ROWS // POOL2
POOLED = 2 * (ONE + TWO)
NEAR = 3 * ROWS
FAR = 384

STEPS_ONE = (2, -1)


def direction(b):
    return 2 * b - 1


REL_ONE = [-2 * steps * direction(b) + b for b in (0, 1) for steps in STEPS_ONE] + [-1, 2]


def relative_two(side):
    sigma = direction(side)
    spots = [(2, 1 - side), (3, 1 - side), (3, side), (4, 1 - side), (4, side), (5, 1 - side), (5, side), (6, side)]
    return [-2 * k * sigma + b for k, b in spots]


REL_TWO = [relative_two(0), relative_two(1)]
REL_MIDDLE = REL_ONE + [REL_TWO[0][0], REL_TWO[1][0]]
REL_LAST = REL_TWO[0][1:] + REL_TWO[1][1:]
OWN, SIDE, MIDDLE, LAST = slice(0, 256), slice(256, 384), slice(384, 640), slice(640, 768)


def dot_nt(a, b):
    return lax.dot_general(a, b, (((1,), (1,)), ((), ())), preferred_element_type=F32)


def dot_tn(a, b):
    return lax.dot_general(a, b, (((0,), (0,)), ((), ())), preferred_element_type=F32)


def dot(a, b):
    return jnp.dot(a, b, preferred_element_type=F32)


def pool_matrix():
    r = lax.broadcasted_iota(jnp.int32, (ONE + TWO, ROWS), 0)
    t = lax.broadcasted_iota(jnp.int32, (ONE + TWO, ROWS), 1)
    one = jnp.where((t >> 2) == r, 1.0 / POOL1, 0.0)
    two = jnp.where((t >> 4) == r - ONE, 1.0 / POOL2, 0.0)
    return jnp.where(r < ONE, one, two).astype(BF16)


def spread_matrix():
    t = lax.broadcasted_iota(jnp.int32, (ROWS, ONE + TWO), 0)
    r = lax.broadcasted_iota(jnp.int32, (ROWS, ONE + TWO), 1)
    one = jnp.where((t >> 2) == r, 1.0 / POOL1, 0.0)
    two = jnp.where((t >> 4) == r - ONE, 1.0 / POOL2, 0.0)
    return jnp.where(r < ONE, one, two).astype(BF16)


def column_of(row):
    i = lax.broadcasted_iota(jnp.int32, (ROWS, ROWS), 0)
    j = lax.broadcasted_iota(jnp.int32, (ROWS, ROWS), 1)
    return jnp.sum(jnp.where(i == j, row, 0.0), axis=1, keepdims=True)


def row_of(column):
    i = lax.broadcasted_iota(jnp.int32, (ROWS, ROWS), 0)
    j = lax.broadcasted_iota(jnp.int32, (ROWS, ROWS), 1)
    return jnp.sum(jnp.where(i == j, column, 0.0), axis=0, keepdims=True)


def kernel(
    q_hbm, k_hbm, v_hbm, g_hbm, level_hbm, frame_hbm,
    att_hbm, dq_hbm, dk_hbm, dv_hbm,
    kv_own, q_two, g_two, kv_near, pooled, one_in, two_in, k_middle, v_middle, k_last, v_last,
    level_s, frame_v, near_bias, far_bias, weight, turned, mixed, stats,
    mixed_grad, att, dq, near_out, pool_out, two_out, sib_out,
    pass_in, near_back, one_back, two_back, sib_back, dk, dv,
    local_sem, send_sem, sib_recv, near_recv, one_recv, two_recv, stat_recv, pass_recv,
    back_near_recv, back_one_recv, back_two_recv, out_recv,
):
    blocks = lax.axis_size("seq")
    chips = blocks // 2
    heads = lax.axis_size("head")
    me = lax.axis_index("seq")
    lane = lax.axis_index("head")
    chip = me // 2
    core = me % 2
    other = 1 - core
    d = direction(core)

    def at(steps, c):
        return {"seq": ((chip + steps + chips) % chips) * 2 + c}

    sibling = {"seq": chip * 2 + other}

    def half(h):
        return pl.ds(pl.multiple_of(h * HALF, HALF), HALF)

    def remote(src, dst, send, recv, device):
        return pltpu.make_async_remote_copy(
            src_ref=src, dst_ref=dst, send_sem=send, recv_sem=recv, device_id=device, device_id_type=MESH
        )

    def inside(*steps, sided=()):
        away = [s for s in steps] + [s * d for s in sided]
        known = True
        for s in away:
            known = known & (chip + s >= 0) & (chip + s < chips)
        return (steps, sided), known

    def only(when, act):
        if when is None:
            act()
        else:
            pl.when(when[1])(act)

    sent = 0
    started = []

    def send(src, dst, recv, device, when=None):
        nonlocal sent
        copy = remote(src, dst, send_sem.at[sent], recv, device)
        sent += 1
        only(when, copy.start)
        started.append((copy, when))

    def flush(keep=0):
        groups = {}
        done = len(started) - keep
        for copy, when in started[:done]:
            groups.setdefault(when and when[0], (when, []))[1].append(copy)
        del started[:done]
        for when, copies in groups.values():

            def wait_all(copies=copies):
                for copy in copies:
                    copy.wait_send()

            only(when, wait_all)

    def arrived(ref, sem, when=None):
        only(when, remote(ref, ref, sem, sem, sibling).wait_recv)

    @pl.when((chip < 6) | (chip >= chips - 6))
    def _():
        for ref in (one_in, two_in, pass_in, near_back, one_back, two_back):
            ref[...] = jnp.zeros(ref.shape, ref.dtype)
        for s in (0, 3):
            kv_near[s] = jnp.zeros(kv_near.shape[1:], BF16)

    mine = pl.ds(pl.multiple_of(core * ROWS, ROWS), ROWS)
    theirs = pl.ds(pl.multiple_of(other * ROWS, ROWS), ROWS)
    k_rows, v_rows = pl.ds(0, ROWS), pl.ds(ROWS, ROWS)
    locals_in = [
        pltpu.make_async_copy(k_hbm, kv_own.at[k_rows], local_sem.at[0]),
        pltpu.make_async_copy(v_hbm, kv_own.at[v_rows], local_sem.at[1]),
        pltpu.make_async_copy(level_hbm, level_s, local_sem.at[2]),
        pltpu.make_async_copy(frame_hbm, frame_v, local_sem.at[3]),
        pltpu.make_async_copy(k_hbm.at[:, half(core)], kv_near.at[1 + core, k_rows], local_sem.at[4]),
        pltpu.make_async_copy(v_hbm.at[:, half(core)], kv_near.at[1 + core, v_rows], local_sem.at[5]),
        pltpu.make_async_copy(q_hbm.at[:, half(core)], q_two.at[mine], local_sem.at[6]),
        pltpu.make_async_copy(g_hbm.at[:, half(core)], g_two.at[mine], local_sem.at[7]),
    ]
    for copy in locals_in[:2]:
        copy.start()

    barrier = pltpu.get_barrier_semaphore()
    partners = [sibling]
    for k in range(1, heads):
        for c in (0, 1):
            partners.append({"seq": chip * 2 + c, "head": (lane + k) % heads})
    expected = len(partners)

    def greet(devices):
        for device in devices:
            pl.semaphore_signal(barrier, inc=1, device_id=device, device_id_type=MESH)

    for steps in (4, -4, 2, -2, 1, -1):
        when = inside(steps)
        only(when, lambda: greet([at(steps, 0), at(steps, 1)]))
        expected = expected + jnp.where(when[1], 2, 0)
    greet(partners)
    for copy in locals_in[2:]:
        copy.start()

    locals_in[0].wait()
    locals_in[1].wait()
    pool = pool_matrix()
    k_pool = dot(pool, kv_own[:ROWS])
    v_pool = dot(pool, kv_own[ROWS:])
    pooled[0 : 2 * ONE, :] = jnp.concatenate([k_pool[:ONE], v_pool[:ONE]], axis=0).astype(BF16)
    pooled[2 * ONE :, :] = jnp.concatenate([k_pool[ONE:], v_pool[ONE:]], axis=0).astype(BF16)

    pl.semaphore_wait(barrier, expected)

    def send_two(steps, side, spot):
        for h in (0, 1):
            send(
                pooled.at[pl.ds(2 * ONE, 2 * TWO), half(h)], two_in.at[side, spot],
                two_recv.at[side, spot], at(steps * d, h), inside(sided=(steps,)),
            )

    send_two(4, core, 5)
    send_two(-4, other, 4)
    send_two(2, core, 1)
    send_two(-2, other, 0)
    send(kv_own.at[:, half(other)], kv_near.at[1 + core], sib_recv.at[0], sibling)
    send(q_hbm.at[:, half(other)], q_two.at[mine], sib_recv.at[2], sibling)
    for h in (0, 1):
        send(kv_own.at[:, half(h)], kv_near.at[3 - 3 * core], near_recv.at[core], at(d, h), inside(sided=(1,)))
    send(g_hbm.at[:, half(other)], g_two.at[mine], sib_recv.at[3], sibling)
    for h in (0, 1):
        send(
            pooled.at[:, half(h)], one_in.at[core * 2 + 1],
            one_recv.at[core * 2 + 1], at(-d, h), inside(sided=(-1,)),
        )
    ones_only = pl.ds(0, 2 * ONE)
    for h in (0, 1):
        send(
            pooled.at[ones_only, half(h)], one_in.at[core * 2, ones_only],
            one_recv.at[core * 2], at(2 * d, h), inside(sided=(2,)),
        )

    locals_in[2].wait()
    locals_in[3].wait()
    table = [level_s[0, i] for i in range(4)]
    spot = lax.broadcasted_iota(jnp.int32, (8, FAR), 1)
    row = jnp.full((8, FAR), MASKED, F32)

    def level_at(offset):
        choice = jnp.where(offset == -3, table[0], table[1])
        choice = jnp.where(offset == 2, table[2], choice)
        return jnp.where(offset == 3, table[3], choice)

    def slot_bias(rel, wanted, most, bias):
        offset = rel - core
        distance = jnp.abs(offset)
        block = 2 * chip + rel
        inside = (distance >= 2) & (distance <= most) & (block >= 0) & (block < blocks)
        chosen = (distance > REACH1) | (level_at(offset) == wanted)
        return jnp.where(inside & chosen, bias * LOG2E, MASKED)

    for s, rel in enumerate(REL_ONE):
        value = slot_bias(rel, 1, REACH1, math.log(POOL1))
        row = jnp.where((spot >= s * ONE) & (spot < (s + 1) * ONE), value, row)
    for s, rel in enumerate(REL_MIDDLE + REL_LAST):
        low = len(REL_ONE) * ONE + s * TWO
        value = slot_bias(rel, 2, REACH2, math.log(POOL2))
        row = jnp.where((spot >= low) & (spot < low + TWO), value, row)
    far_bias[core] = row
    send(far_bias.at[core], far_bias.at[core], sib_recv.at[4], sibling)

    lengths = frame_v[...].astype(F32)
    count = lengths.shape[1]
    i = lax.broadcasted_iota(jnp.int32, (count, count), 0)
    j = lax.broadcasted_iota(jnp.int32, (count, count), 1)
    ends_column = jnp.sum(jnp.where(j <= i, lengths, 0.0), axis=1, keepdims=True)
    ends_row = jnp.sum(jnp.where(i == j, ends_column, 0.0), axis=0, keepdims=True)
    start = (2 * chip - 1) * ROWS
    key_place = start + lax.broadcasted_iota(jnp.int32, (1, 4 * ROWS), 1)
    key_frame = jnp.sum(jnp.where(key_place.astype(F32) >= ends_column, 1.0, 0.0), axis=0, keepdims=True)
    key_inside = (key_place >= 0) & (key_place < blocks * ROWS)
    for b in (0, 1):
        place = start + (b + 1) * ROWS + lax.broadcasted_iota(jnp.int32, (ROWS, 1), 0)
        frame = jnp.sum(jnp.where(place.astype(F32) >= ends_row, 1.0, 0.0), axis=1, keepdims=True)
        matched = jnp.where(frame == key_frame, MATCHED_FRAME_ADD * LOG2E, 0.0)
        matched = jnp.where(key_inside, matched, MASKED)
        rows = slice(b * ROWS, (b + 1) * ROWS)
        near_bias[rows, OWN] = matched[:, ROWS : 3 * ROWS]
        near_bias[rows, SIDE] = matched[:, 3 * b * ROWS : (3 * b + 1) * ROWS]

    scale = LOG2E / math.sqrt(HEAD_DIM)
    columns = [slice(h * HEAD_DIM, (h + 1) * HEAD_DIM) for h in (0, 1)]
    first, second = slice(0, ROWS), slice(ROWS, 2 * ROWS)
    highs, totals, accs = [[], []], [None, None], [None, None]

    def far_of(part):
        low, high = part.start - MIDDLE.start, part.stop - MIDDLE.start
        shape = (ROWS, high - low)
        return jnp.concatenate([jnp.broadcast_to(far_bias[b, 0:1, low:high], shape) for b in (0, 1)], axis=0)

    def attend(h, part, scores, product):
        top = jnp.max(scores, axis=1, keepdims=True)
        if highs[h]:
            top = jnp.maximum(highs[h][-1], top)
        e = jnp.exp2(scores - top)
        weight[h, :, part] = e
        total = jnp.sum(e, axis=1, keepdims=True)
        rounded = e.astype(BF16)
        acc = product(rounded)
        if part in (OWN, SIDE):
            turned[h, part, :] = rounded.T
        if highs[h]:
            alpha = jnp.exp2(highs[h][-1] - top)
            total = totals[h] * alpha + total
            acc = accs[h] * alpha + acc
        highs[h].append(top)
        totals[h], accs[h] = total, acc

    rows_of = (first, second)

    def own_of(kind, h):
        return kv_near[1:3, rows_of[kind], columns[h]].reshape(2 * ROWS, HEAD_DIM)

    for side in (0, 1):
        sigma = direction(side)
        four, two = -4 * sigma, -2 * sigma
        for s in (4, 5):
            arrived(two_in.at[side, s], two_recv.at[side, s], inside(four))
        send(two_in.at[side, 5], two_in.at[side, 8], two_recv.at[side, 8], at(2 * sigma, core), inside(four, 2 * sigma))
        send(
            two_in.at[side, pl.ds(4, 2)], two_in.at[side, pl.ds(6, 2)],
            two_recv.at[side, 6], at(sigma, core), inside(four, sigma),
        )
        for s in (0, 1):
            arrived(two_in.at[side, s], two_recv.at[side, s], inside(two))
        send(
            two_in.at[side, pl.ds(0, 2)], two_in.at[side, pl.ds(2, 2)],
            two_recv.at[side, 2], at(sigma, core), inside(two, sigma),
        )

    locals_in[4].wait()
    locals_in[6].wait()
    locals_in[5].wait()
    arrived(kv_near.at[1 + other], sib_recv.at[0])
    arrived(q_two.at[theirs], sib_recv.at[2])
    for h in (0, 1):
        scores = dot_nt(q_two[:, columns[h]], own_of(0, h)) * scale + near_bias[:, OWN]
        attend(h, OWN, scores, lambda e: dot(e, own_of(1, h)))

    arrived(kv_near.at[3], near_recv.at[0], inside(1))
    arrived(kv_near.at[0], near_recv.at[1], inside(-1))
    for h in (0, 1):
        query = q_two[:, columns[h]]
        scores = jnp.concatenate(
            [dot_nt(query[first], kv_near[0, first, columns[h]]), dot_nt(query[second], kv_near[3, first, columns[h]])], axis=0
        )
        attend(
            h, SIDE, scores * scale + near_bias[:, SIDE],
            lambda e: jnp.concatenate(
                [dot(e[first], kv_near[0, second, columns[h]]), dot(e[second], kv_near[3, second, columns[h]])], axis=0
            ),
        )

    near_pools = [(dot(pool, kv_near[s, first]), dot(pool, kv_near[s, second])) for s in (0, 3)]
    for side in (0, 1):
        sigma = direction(side)
        arrived(one_in.at[side * 2, ones_only], one_recv.at[side * 2], inside(-2 * sigma))
        arrived(one_in.at[side * 2 + 1], one_recv.at[side * 2 + 1], inside(sigma))
    arrived(far_bias.at[other], sib_recv.at[4])
    nearest = [two_in[0, 1], one_in[1, 2 * ONE :], two_in[1, 1], one_in[3, 2 * ONE :]]
    nearest = [x.astype(F32) for x in nearest]
    for kind, middle in ((0, k_middle), (1, v_middle)):
        ones = slice(kind * ONE, (kind + 1) * ONE)
        rows = slice(kind * TWO, (kind + 1) * TWO)
        for s in range(4):
            middle[s * ONE : (s + 1) * ONE] = one_in[s, ones]
        middle[4 * ONE : 6 * ONE] = jnp.concatenate([p[kind][:ONE] for p in near_pools], axis=0).astype(BF16)
        parts = [x[rows] for x in nearest] + [p[kind][ONE:] for p in near_pools]
        parts += [two_in[side, 0].astype(F32)[rows] for side in (0, 1)]
        middle[6 * ONE :] = jnp.concatenate(parts, axis=0).astype(BF16)
    for h in (0, 1):
        scores = dot_nt(q_two[:, columns[h]], k_middle[:, columns[h]]) * scale + far_of(MIDDLE)
        attend(h, MIDDLE, scores, lambda e: dot(e, v_middle[:, columns[h]]))

    for side in (0, 1):
        sigma = direction(side)
        for s, steps in ((2, 3), (6, 5)):
            arrived(two_in.at[side, pl.ds(s, 2)], two_recv.at[side, s], inside(-steps * sigma))
        arrived(two_in.at[side, 8], two_recv.at[side, 8], inside(-6 * sigma))
    twos = [two_in[side, 2:].astype(F32) for side in (0, 1)]
    for kind, last in ((0, k_last), (1, v_last)):
        rows = slice(kind * TWO, (kind + 1) * TWO)
        parts = [t[:, rows].reshape(7 * TWO, HALF) for t in twos] + [jnp.zeros((2 * TWO, HALF), F32)]
        last[...] = jnp.concatenate(parts, axis=0).astype(BF16)
    for h in (0, 1):
        scores = dot_nt(q_two[:, columns[h]], k_last[:, columns[h]]) * scale + far_of(LAST)
        attend(h, LAST, scores, lambda e: dot(e, v_last[:, columns[h]]))
    inverse_totals = [1.0 / totals[h] for h in (0, 1)]
    for h in (0, 1):
        mixed[:, columns[h]] = accs[h] * inverse_totals[h]

    locals_in[7].wait()
    arrived(g_two.at[theirs], sib_recv.at[3])
    mates = 2 * heads
    place = lane * 2 + core
    value = mixed[...]
    energy = jnp.sum(value * value, axis=1, keepdims=True)
    product = jnp.sum(value * g_two[...].astype(F32), axis=1, keepdims=True)
    stats[place] = jnp.concatenate(
        [row_of(energy[:ROWS]), row_of(energy[ROWS:]), row_of(product[:ROWS]), row_of(product[ROWS:]), jnp.zeros((4, ROWS), F32)],
        axis=0,
    )
    for k in range(1, mates):
        to = (place + k) % mates
        send(stats.at[place], stats.at[place], stat_recv.at[place], {"seq": chip * 2 + to % 2, "head": to // 2})
    factors = [[], []]
    for h in (0, 1):
        for index, part in enumerate((OWN, SIDE, MIDDLE, LAST)):
            factors[h].append(jnp.exp2(highs[h][index] - highs[h][-1]) * inverse_totals[h])
            if part in (MIDDLE, LAST):
                turned[h, part, :] = weight[h, :, part].astype(BF16).T
    flush(keep=mates - 1)
    for k in range(1, mates):
        source = (place + k) % mates
        arrived(stats.at[source], stat_recv.at[source])
    summed = stats[0]
    for k in range(1, mates):
        summed = summed + stats[k]
    width = HEADS * HEAD_DIM
    deltas = [[], []]
    for b, rows in ((0, first), (1, second)):
        inverse = lax.rsqrt(column_of(summed[b : b + 1]) / width + NORM_EPSILON)
        agreement = column_of(summed[2 + b : 3 + b]) * inverse
        normed = mixed[rows] * inverse
        att[rows] = normed.astype(BF16)
        grad = inverse * (g_two[rows].astype(F32) - normed * (agreement / width))
        mixed_grad[rows] = grad
        both = grad.astype(BF16).astype(F32) * mixed[rows]
        for h in (0, 1):
            deltas[h].append(jnp.sum(both[:, columns[h]], axis=1, keepdims=True))
    deltas = [jnp.concatenate(deltas[h], axis=0) for h in (0, 1)]

    out_att = pltpu.make_async_copy(att.at[mine], att_hbm.at[:, half(core)], local_sem.at[8])
    out_att.start()
    send(att.at[theirs], att_hbm.at[:, half(core)], out_recv.at[0], sibling)

    unscale = 1.0 / math.sqrt(HEAD_DIM)
    query_grads = [None, None]

    def scaled(h, part):
        factor = factors[h][(OWN, SIDE, MIDDLE, LAST).index(part)]
        return (mixed_grad[:, columns[h]] * factor).astype(BF16), deltas[h] * factor

    def slopes_of(h, part, products, delta):
        return (weight[h, :, part] * (products - delta)).astype(BF16)

    def plain_backward(part, k_ref, v_ref):
        k_parts, v_parts = [], []
        for h in (0, 1):
            grad, delta = scaled(h, part)
            slopes = slopes_of(h, part, dot_nt(grad, v_ref(h)), delta)
            change = dot(slopes, k_ref(h))
            query_grads[h] = change if query_grads[h] is None else query_grads[h] + change
            k_parts.append(dot_tn(slopes, q_two[:, columns[h]]) * unscale)
            v_parts.append(dot(turned[h, part, :], grad))
        return jnp.concatenate(k_parts, axis=1), jnp.concatenate(v_parts, axis=1)

    def two_rows(pair, low):
        return jnp.concatenate([g[low : low + TWO] for g in pair], axis=0)

    last = plain_backward(LAST, lambda h: k_last[:, columns[h]], lambda h: v_last[:, columns[h]])
    for side in (0, 1):
        sigma = direction(side)
        for s in (1, 2, 5, 6, 7):
            two_out[side, s] = two_rows(last, (side * 7 + s - 1) * TWO).astype(BF16)
        send(
            two_out.at[side, pl.ds(5, 2)], pass_in.at[side, pl.ds(0, 2)],
            pass_recv.at[side, 0], at(-sigma, core), inside(-5 * sigma),
        )
        send(two_out.at[side, 7], pass_in.at[side, 4], pass_recv.at[side, 2], at(-2 * sigma, core), inside(-6 * sigma))
        send(
            two_out.at[side, pl.ds(1, 2)], pass_in.at[side, pl.ds(2, 2)],
            pass_recv.at[side, 1], at(-sigma, core), inside(-3 * sigma),
        )

    middle = plain_backward(MIDDLE, lambda h: k_middle[:, columns[h]], lambda h: v_middle[:, columns[h]])
    for s in range(4):
        for kind in (0, 1):
            pool_out[s, kind * ONE : (kind + 1) * ONE] = middle[kind][s * ONE : (s + 1) * ONE].astype(BF16)
    for b in (0, 1):
        s = 2 * b + 1
        pool_out[s, 2 * ONE :] = two_rows(middle, 6 * ONE + s * TWO).astype(BF16)
        send(pool_out.at[s], one_back.at[core, 1], back_one_recv.at[core, 1], at(direction(b), b), inside(direction(b)))
    for side in (0, 1):
        sigma = direction(side)
        send(
            pool_out.at[2 * side, ones_only], one_back.at[core, 0, ones_only],
            back_one_recv.at[core, 0], at(-2 * sigma, side), inside(-2 * sigma),
        )

    spread = spread_matrix()
    k_sides, v_sides = [[], []], [[], []]
    for h in (0, 1):
        grad, delta = scaled(h, SIDE)
        query = q_two[:, columns[h]]
        products = jnp.concatenate(
            [dot_nt(grad[first], kv_near[0, second, columns[h]]), dot_nt(grad[second], kv_near[3, second, columns[h]])], axis=0
        )
        slopes = slopes_of(h, SIDE, products, delta)
        query_grads[h] = query_grads[h] + jnp.concatenate(
            [dot(slopes[first], kv_near[0, first, columns[h]]), dot(slopes[second], kv_near[3, first, columns[h]])], axis=0
        )
        for b, rows in ((0, second), (1, first)):
            k_sides[b].append(dot_tn(slopes[rows], query[rows]) * unscale)
            v_sides[b].append(dot(turned[h, SIDE, rows], grad[rows]))
    for side in (0, 1):
        sigma = direction(side)
        four, two = -4 * sigma, -2 * sigma
        arrived(pass_in.at[side, pl.ds(0, 2)], pass_recv.at[side, 0], inside(sigma, four))
        arrived(pass_in.at[side, 4], pass_recv.at[side, 2], inside(2 * sigma, four))
        arrived(pass_in.at[side, pl.ds(2, 2)], pass_recv.at[side, 1], inside(sigma, two))
        passed = pass_in[side].astype(F32)
        two_out[side, 3] = (two_rows(last, (side * 7 + 2) * TWO) + passed[0]).astype(BF16)
        two_out[side, 4] = (two_rows(last, (side * 7 + 3) * TWO) + passed[1] + passed[4]).astype(BF16)
        two_out[side, 0] = (two_rows(middle, 6 * ONE + (6 + side) * TWO) + passed[2]).astype(BF16)
        two_out[side, 8] = (two_rows(middle, 6 * ONE + 2 * side * TWO) + passed[3]).astype(BF16)
        for s, spot, owner, steps in ((3, 2, 1 - side, four), (4, 3, side, four), (0, 0, 1 - side, two), (8, 1, side, two)):
            send(
                two_out.at[side, s], two_back.at[core, spot],
                back_two_recv.at[core, spot], at(steps, owner), inside(steps),
            )

    for b in (0, 1):
        p = 5 - b
        for kind, sides in ((0, k_sides), (1, v_sides)):
            pools = middle[kind]
            small = jnp.concatenate(
                [pools[p * ONE : (p + 1) * ONE], pools[6 * ONE + p * TWO : 6 * ONE + (p + 1) * TWO]], axis=0
            )
            near_out[b, kind * ROWS : (kind + 1) * ROWS] = (
                jnp.concatenate(sides[b], axis=1) + dot(spread, small.astype(BF16))
            ).astype(BF16)
        send(near_out.at[b], near_back.at[core], back_near_recv.at[core], at(-direction(b), b), inside(-direction(b)))

    own = plain_backward(OWN, lambda h: own_of(0, h), lambda h: own_of(1, h))
    for kind in (0, 1):
        sib_out[kind * ROWS : (kind + 1) * ROWS] = jnp.where(core == 0, own[kind][second], own[kind][first]).astype(BF16)
    send(sib_out, sib_back, out_recv.at[1], sibling)
    for h in (0, 1):
        dq[:, columns[h]] = (query_grads[h] * unscale).astype(BF16)
    out_dq = pltpu.make_async_copy(dq.at[mine], dq_hbm.at[:, half(core)], local_sem.at[9])
    out_dq.start()
    send(dq.at[theirs], dq_hbm.at[:, half(core)], out_recv.at[2], sibling)

    flush(keep=4)
    outs = [out_att, out_dq]

    def finish(h, sem, rest):
        arrived(one_back.at[h, 0, ones_only], back_one_recv.at[h, 0], inside(sided=(2,)))
        arrived(one_back.at[h, 1], back_one_recv.at[h, 1], inside(sided=(-1,)))
        arrived(near_back.at[h], back_near_recv.at[h], inside(sided=(1,)))
        for j, steps in enumerate((-2, 2, -4, 4)):
            arrived(two_back.at[h, j], back_two_recv.at[h, j], inside(sided=(steps,)))
        ones = one_back[h, 1].astype(F32)
        twos = ones[2 * ONE :]
        for j in range(4):
            twos = twos + two_back[h, j].astype(F32)
        ones = ones[: 2 * ONE] + one_back[h, 0, : 2 * ONE].astype(F32)
        sums = []
        for kind, rows in ((0, first), (1, second)):
            small = jnp.concatenate([ones[kind * ONE : (kind + 1) * ONE], twos[kind * TWO : (kind + 1) * TWO]], axis=0)
            sums.append(near_back[h, rows].astype(F32) + dot(spread, small.astype(BF16)))
        rest = rest()
        for kind, out, out_hbm in ((0, dk, dk_hbm), (1, dv, dv_hbm)):
            out[:, half(h)] = (sums[kind] + rest[kind]).astype(BF16)
            outs.append(pltpu.make_async_copy(out.at[:, half(h)], out_hbm.at[:, half(h)], local_sem.at[sem + kind]))
            outs[-1].start()

    def from_sibling():
        arrived(sib_back, out_recv.at[1])
        return [sib_back[rows].astype(F32) for rows in (first, second)]

    finish(core, 10, lambda: [jnp.where(core == 0, own[kind][first], own[kind][second]) for kind in (0, 1)])
    finish(other, 12, from_sibling)
    arrived(att_hbm.at[:, half(other)], out_recv.at[0])
    arrived(dq_hbm.at[:, half(other)], out_recv.at[2])
    flush()
    for copy in outs:
        copy.wait()


def write_out(*refs):
    *arrays, sems = refs
    copies = [pltpu.make_async_copy(arrays[i], arrays[4 + i], sems.at[i]) for i in range(4)]
    for copy in copies:
        copy.start()
    for copy in copies:
        copy.wait()


def body(queries, keys, values, out_grad, level_choice, frame_lengths):
    rows, width = queries.shape
    vmem = pltpu.VMEM
    dma = pltpu.SemaphoreType.DMA
    out = jax.ShapeDtypeStruct((rows, width), BF16)
    limit = 40 * 1024 * 1024
    arrays = (queries, keys, values, out_grad, level_choice, frame_lengths.reshape(1, -1))
    results = pl.pallas_call(
        kernel,
        out_shape=(out, out, out, out),
        in_specs=[pl.BlockSpec(memory_space=pl.ANY)] * 6,
        out_specs=(pl.BlockSpec(memory_space=pl.ANY),) * 4,
        scratch_shapes=[
            vmem((2 * ROWS, width), BF16),
            vmem((2 * ROWS, HALF), BF16),
            vmem((2 * ROWS, HALF), BF16),
            vmem((4, 2 * ROWS, HALF), BF16),
            vmem((POOLED, width), BF16),
            vmem((4, POOLED, HALF), BF16),
            vmem((2, 9, 2 * TWO, HALF), BF16),
            vmem((256, HALF), BF16),
            vmem((256, HALF), BF16),
            vmem((128, HALF), BF16),
            vmem((128, HALF), BF16),
            pltpu.SMEM((1, 4), jnp.int32),
            vmem((1, 64), jnp.int32),
            vmem((2 * ROWS, 384), F32),
            vmem((2, 8, FAR), F32),
            vmem((2, 2 * ROWS, 768), F32),
            vmem((2, 768, 2 * ROWS), BF16),
            vmem((2 * ROWS, HALF), F32),
            vmem((8, 8, ROWS), F32),
            vmem((2 * ROWS, HALF), F32),
            vmem((2 * ROWS, HALF), BF16),
            vmem((2 * ROWS, HALF), BF16),
            vmem((2, 2 * ROWS, HALF), BF16),
            vmem((4, POOLED, HALF), BF16),
            vmem((2, 9, 2 * TWO, HALF), BF16),
            vmem((2 * ROWS, HALF), BF16),
            vmem((2, 5, 2 * TWO, HALF), BF16),
            vmem((2, 2 * ROWS, HALF), BF16),
            vmem((2, 2, POOLED, HALF), BF16),
            vmem((2, 4, 2 * TWO, HALF), BF16),
            vmem((2 * ROWS, HALF), BF16),
            vmem((ROWS, width), BF16),
            vmem((ROWS, width), BF16),
            dma((14,)),
            dma((64,)),
            dma((5,)),
            dma((2,)),
            dma((4,)),
            dma((2, 9)),
            dma((8,)),
            dma((2, 3)),
            dma((2,)),
            dma((2, 2)),
            dma((2, 4)),
            dma((3,)),
        ],
        compiler_params=pltpu.CompilerParams(collective_id=0, has_side_effects=True, vmem_limit_bytes=limit),
        cost_estimate=pl.CostEstimate(flops=700_000_000, bytes_accessed=1_100_000, transcendentals=400_000),
    )(*[pltpu.with_memory_space_constraint(array, pltpu.HBM) for array in arrays])
    return pl.pallas_call(
        write_out,
        out_shape=(out, out, out, out),
        in_specs=[pl.BlockSpec(memory_space=pl.ANY)] * 4,
        out_specs=(pl.BlockSpec(memory_space=pl.ANY),) * 4,
        scratch_shapes=[dma((4,))],
        compiler_params=pltpu.CompilerParams(vmem_limit_bytes=limit),
        cost_estimate=pl.CostEstimate(flops=0, bytes_accessed=1_100_000, transcendentals=0),
    )(*results)


def solution(mesh):
    in_specs = (
        P("seq", "head"),
        P("seq", "head"),
        P("seq", "head"),
        P("seq", "head"),
        P("seq", None),
        P(),
    )
    out_specs = (P("seq", "head"), P("seq", "head"), P("seq", "head"), P("seq", "head"))
    return jax.shard_map(body, mesh=mesh, in_specs=in_specs, out_specs=out_specs, check_vma=False)
```

```python
import math

import jax
import jax.numpy as jnp
from jax import lax
from jax.experimental import pallas as pl
from jax.experimental.pallas import tpu as pltpu
from jax.sharding import PartitionSpec as P

HEADS = 16
HEAD_DIM = 128
POOL1 = 4
POOL2 = 16
REACH1 = 3
REACH2 = 11
MATCHED_FRAME_ADD = 1.0
NORM_EPSILON = 1e-06

MESH = pl.DeviceIdType.MESH
F32 = jnp.float32
BF16 = jnp.bfloat16
LOG2E = math.log2(math.e)
MASKED = -1e30

ROWS = 128
HALF = 256
ONE = ROWS // POOL1
TWO = ROWS // POOL2
POOLED = 2 * (ONE + TWO)
NEAR = 3 * ROWS
FAR = 384

STEPS_ONE = (2, -1)


def direction(b):
    return 2 * b - 1


REL_ONE = [-2 * steps * direction(b) + b for b in (0, 1) for steps in STEPS_ONE] + [-1, 2]


def relative_two(side):
    sigma = direction(side)
    spots = [(2, 1 - side), (3, 1 - side), (3, side), (4, 1 - side), (4, side), (5, 1 - side), (5, side), (6, side)]
    return [-2 * k * sigma + b for k, b in spots]


REL_TWO = [relative_two(0), relative_two(1)]
REL_MIDDLE = REL_ONE + [REL_TWO[0][0], REL_TWO[1][0]]
REL_LAST = REL_TWO[0][1:] + REL_TWO[1][1:]
OWN, SIDE, MIDDLE, LAST = slice(0, 256), slice(256, 384), slice(384, 640), slice(640, 768)


def dot_nt(a, b):
    return lax.dot_general(a, b, (((1,), (1,)), ((), ())), preferred_element_type=F32)


def dot_tn(a, b):
    return lax.dot_general(a, b, (((0,), (0,)), ((), ())), preferred_element_type=F32)


def dot(a, b):
    return jnp.dot(a, b, preferred_element_type=F32)


def pool_matrix():
    r = lax.broadcasted_iota(jnp.int32, (ONE + TWO, ROWS), 0)
    t = lax.broadcasted_iota(jnp.int32, (ONE + TWO, ROWS), 1)
    one = jnp.where((t >> 2) == r, 1.0 / POOL1, 0.0)
    two = jnp.where((t >> 4) == r - ONE, 1.0 / POOL2, 0.0)
    return jnp.where(r < ONE, one, two).astype(BF16)


def spread_matrix():
    t = lax.broadcasted_iota(jnp.int32, (ROWS, ONE + TWO), 0)
    r = lax.broadcasted_iota(jnp.int32, (ROWS, ONE + TWO), 1)
    one = jnp.where((t >> 2) == r, 1.0 / POOL1, 0.0)
    two = jnp.where((t >> 4) == r - ONE, 1.0 / POOL2, 0.0)
    return jnp.where(r < ONE, one, two).astype(BF16)


def column_of(row):
    i = lax.broadcasted_iota(jnp.int32, (ROWS, ROWS), 0)
    j = lax.broadcasted_iota(jnp.int32, (ROWS, ROWS), 1)
    return jnp.sum(jnp.where(i == j, row, 0.0), axis=1, keepdims=True)


def row_of(column):
    i = lax.broadcasted_iota(jnp.int32, (ROWS, ROWS), 0)
    j = lax.broadcasted_iota(jnp.int32, (ROWS, ROWS), 1)
    return jnp.sum(jnp.where(i == j, column, 0.0), axis=0, keepdims=True)


def kernel(
    q_hbm, k_hbm, v_hbm, g_hbm, level_hbm, frame_hbm,
    att_hbm, dq_hbm, dk_hbm, dv_hbm,
    kv_own, q_two, g_two, kv_near, pooled, one_in, two_in, k_middle, v_middle, k_last, v_last,
    level_s, frame_v, near_bias, far_bias, weight, turned, mixed, stats,
    mixed_grad, att, dq, near_out, pool_out, two_out, sib_out,
    pass_in, near_back, one_back, two_back, sib_back, dk, dv,
    local_sem, send_sem, sib_recv, near_recv, one_recv, two_recv, stat_recv, pass_recv,
    back_near_recv, back_one_recv, back_two_recv, out_recv,
):
    blocks = lax.axis_size("seq")
    chips = blocks // 2
    heads = lax.axis_size("head")
    me = lax.axis_index("seq")
    lane = lax.axis_index("head")
    chip = me // 2
    core = me % 2
    other = 1 - core
    d = direction(core)

    def at(steps, c):
        return {"seq": ((chip + steps + chips) % chips) * 2 + c}

    sibling = {"seq": chip * 2 + other}

    def half(h):
        return pl.ds(pl.multiple_of(h * HALF, HALF), HALF)

    def remote(src, dst, send, recv, device):
        return pltpu.make_async_remote_copy(
            src_ref=src, dst_ref=dst, send_sem=send, recv_sem=recv, device_id=device, device_id_type=MESH
        )

    def inside(*steps, sided=()):
        away = [s for s in steps] + [s * d for s in sided]
        known = True
        for s in away:
            known = known & (chip + s >= 0) & (chip + s < chips)
        return (steps, sided), known

    def only(when, act):
        if when is None:
            act()
        else:
            pl.when(when[1])(act)

    sent = 0
    started = []

    def send(src, dst, recv, device, when=None):
        nonlocal sent
        copy = remote(src, dst, send_sem.at[sent], recv, device)
        sent += 1
        only(when, copy.start)
        started.append((copy, when))

    def flush(keep=0):
        groups = {}
        done = len(started) - keep
        for copy, when in started[:done]:
            groups.setdefault(when and when[0], (when, []))[1].append(copy)
        del started[:done]
        for when, copies in groups.values():

            def wait_all(copies=copies):
                for copy in copies:
                    copy.wait_send()

            only(when, wait_all)

    def arrived(ref, sem, when=None):
        only(when, remote(ref, ref, sem, sem, sibling).wait_recv)

    @pl.when((chip < 6) | (chip >= chips - 6))
    def _():
        for ref in (one_in, two_in, pass_in, near_back, one_back, two_back):
            ref[...] = jnp.zeros(ref.shape, ref.dtype)
        for s in (0, 3):
            kv_near[s] = jnp.zeros(kv_near.shape[1:], BF16)

    mine = pl.ds(pl.multiple_of(core * ROWS, ROWS), ROWS)
    theirs = pl.ds(pl.multiple_of(other * ROWS, ROWS), ROWS)
    k_rows, v_rows = pl.ds(0, ROWS), pl.ds(ROWS, ROWS)
    locals_in = [
        pltpu.make_async_copy(k_hbm, kv_own.at[k_rows], local_sem.at[0]),
        pltpu.make_async_copy(v_hbm, kv_own.at[v_rows], local_sem.at[1]),
        pltpu.make_async_copy(level_hbm, level_s, local_sem.at[2]),
        pltpu.make_async_copy(frame_hbm, frame_v, local_sem.at[3]),
        pltpu.make_async_copy(k_hbm.at[:, half(core)], kv_near.at[1 + core, k_rows], local_sem.at[4]),
        pltpu.make_async_copy(v_hbm.at[:, half(core)], kv_near.at[1 + core, v_rows], local_sem.at[5]),
        pltpu.make_async_copy(q_hbm.at[:, half(core)], q_two.at[mine], local_sem.at[6]),
        pltpu.make_async_copy(g_hbm.at[:, half(core)], g_two.at[mine], local_sem.at[7]),
    ]
    for copy in locals_in[:2]:
        copy.start()

    barrier = pltpu.get_barrier_semaphore()
    partners = [sibling]
    for k in range(1, heads):
        for c in (0, 1):
            partners.append({"seq": chip * 2 + c, "head": (lane + k) % heads})
    expected = len(partners)

    def greet(devices):
        for device in devices:
            pl.semaphore_signal(barrier, inc=1, device_id=device, device_id_type=MESH)

    for steps in (4, -4, 2, -2, 1, -1):
        when = inside(steps)
        only(when, lambda: greet([at(steps, 0), at(steps, 1)]))
        expected = expected + jnp.where(when[1], 2, 0)
    greet(partners)
    for copy in locals_in[2:]:
        copy.start()

    locals_in[0].wait()
    locals_in[1].wait()
    pool = pool_matrix()
    k_pool = dot(pool, kv_own[:ROWS])
    v_pool = dot(pool, kv_own[ROWS:])
    pooled[0 : 2 * ONE, :] = jnp.concatenate([k_pool[:ONE], v_pool[:ONE]], axis=0).astype(BF16)
    pooled[2 * ONE :, :] = jnp.concatenate([k_pool[ONE:], v_pool[ONE:]], axis=0).astype(BF16)

    pl.semaphore_wait(barrier, expected)

    def send_two(steps, side, spot):
        for h in (0, 1):
            send(
                pooled.at[pl.ds(2 * ONE, 2 * TWO), half(h)], two_in.at[side, spot],
                two_recv.at[side, spot], at(steps * d, h), inside(sided=(steps,)),
            )

    send_two(4, core, 5)
    send_two(-4, other, 4)
    send_two(2, core, 1)
    send_two(-2, other, 0)
    send(kv_own.at[:, half(other)], kv_near.at[1 + core], sib_recv.at[0], sibling)
    send(q_hbm.at[:, half(other)], q_two.at[mine], sib_recv.at[2], sibling)
    for h in (0, 1):
        send(kv_own.at[:, half(h)], kv_near.at[3 - 3 * core], near_recv.at[core], at(d, h), inside(sided=(1,)))
    send(g_hbm.at[:, half(other)], g_two.at[mine], sib_recv.at[3], sibling)
    for h in (0, 1):
        send(
            pooled.at[:, half(h)], one_in.at[core * 2 + 1],
            one_recv.at[core * 2 + 1], at(-d, h), inside(sided=(-1,)),
        )
    ones_only = pl.ds(0, 2 * ONE)
    for h in (0, 1):
        send(
            pooled.at[ones_only, half(h)], one_in.at[core * 2, ones_only],
            one_recv.at[core * 2], at(2 * d, h), inside(sided=(2,)),
        )

    locals_in[2].wait()
    locals_in[3].wait()
    table = [level_s[0, i] for i in range(4)]
    spot = lax.broadcasted_iota(jnp.int32, (8, FAR), 1)
    row = jnp.full((8, FAR), MASKED, F32)

    def level_at(offset):
        choice = jnp.where(offset == -3, table[0], table[1])
        choice = jnp.where(offset == 2, table[2], choice)
        return jnp.where(offset == 3, table[3], choice)

    def slot_bias(rel, wanted, most, bias):
        offset = rel - core
        distance = jnp.abs(offset)
        block = 2 * chip + rel
        inside = (distance >= 2) & (distance <= most) & (block >= 0) & (block < blocks)
        chosen = (distance > REACH1) | (level_at(offset) == wanted)
        return jnp.where(inside & chosen, bias * LOG2E, MASKED)

    for s, rel in enumerate(REL_ONE):
        value = slot_bias(rel, 1, REACH1, math.log(POOL1))
        row = jnp.where((spot >= s * ONE) & (spot < (s + 1) * ONE), value, row)
    for s, rel in enumerate(REL_MIDDLE + REL_LAST):
        low = len(REL_ONE) * ONE + s * TWO
        value = slot_bias(rel, 2, REACH2, math.log(POOL2))
        row = jnp.where((spot >= low) & (spot < low + TWO), value, row)
    far_bias[core] = row
    send(far_bias.at[core], far_bias.at[core], sib_recv.at[4], sibling)

    lengths = frame_v[...].astype(F32)
    count = lengths.shape[1]
    i = lax.broadcasted_iota(jnp.int32, (count, count), 0)
    j = lax.broadcasted_iota(jnp.int32, (count, count), 1)
    ends_column = jnp.sum(jnp.where(j <= i, lengths, 0.0), axis=1, keepdims=True)
    ends_row = jnp.sum(jnp.where(i == j, ends_column, 0.0), axis=0, keepdims=True)
    start = (2 * chip - 1) * ROWS
    key_place = start + lax.broadcasted_iota(jnp.int32, (1, 4 * ROWS), 1)
    key_frame = jnp.sum(jnp.where(key_place.astype(F32) >= ends_column, 1.0, 0.0), axis=0, keepdims=True)
    key_inside = (key_place >= 0) & (key_place < blocks * ROWS)
    for b in (0, 1):
        place = start + (b + 1) * ROWS + lax.broadcasted_iota(jnp.int32, (ROWS, 1), 0)
        frame = jnp.sum(jnp.where(place.astype(F32) >= ends_row, 1.0, 0.0), axis=1, keepdims=True)
        matched = jnp.where(frame == key_frame, MATCHED_FRAME_ADD * LOG2E, 0.0)
        matched = jnp.where(key_inside, matched, MASKED)
        rows = slice(b * ROWS, (b + 1) * ROWS)
        near_bias[rows, OWN] = matched[:, ROWS : 3 * ROWS]
        near_bias[rows, SIDE] = matched[:, 3 * b * ROWS : (3 * b + 1) * ROWS]

    scale = LOG2E / math.sqrt(HEAD_DIM)
    columns = [slice(h * HEAD_DIM, (h + 1) * HEAD_DIM) for h in (0, 1)]
    first, second = slice(0, ROWS), slice(ROWS, 2 * ROWS)
    highs, totals, accs = [[], []], [None, None], [None, None]

    def far_of(part):
        low, high = part.start - MIDDLE.start, part.stop - MIDDLE.start
        shape = (ROWS, high - low)
        return jnp.concatenate([jnp.broadcast_to(far_bias[b, 0:1, low:high], shape) for b in (0, 1)], axis=0)

    def attend(h, part, scores, product):
        top = jnp.max(scores, axis=1, keepdims=True)
        if highs[h]:
            top = jnp.maximum(highs[h][-1], top)
        e = jnp.exp2(scores - top)
        weight[h, :, part] = e
        total = jnp.sum(e, axis=1, keepdims=True)
        rounded = e.astype(BF16)
        acc = product(rounded)
        if part in (OWN, SIDE):
            turned[h, part, :] = rounded.T
        if highs[h]:
            alpha = jnp.exp2(highs[h][-1] - top)
            total = totals[h] * alpha + total
            acc = accs[h] * alpha + acc
        highs[h].append(top)
        totals[h], accs[h] = total, acc

    rows_of = (first, second)

    def own_of(kind, h):
        return kv_near[1:3, rows_of[kind], columns[h]].reshape(2 * ROWS, HEAD_DIM)

    for side in (0, 1):
        sigma = direction(side)
        four, two = -4 * sigma, -2 * sigma
        for s in (4, 5):
            arrived(two_in.at[side, s], two_recv.at[side, s], inside(four))
        send(two_in.at[side, 5], two_in.at[side, 8], two_recv.at[side, 8], at(2 * sigma, core), inside(four, 2 * sigma))
        send(
            two_in.at[side, pl.ds(4, 2)], two_in.at[side, pl.ds(6, 2)],
            two_recv.at[side, 6], at(sigma, core), inside(four, sigma),
        )
        for s in (0, 1):
            arrived(two_in.at[side, s], two_recv.at[side, s], inside(two))
        send(
            two_in.at[side, pl.ds(0, 2)], two_in.at[side, pl.ds(2, 2)],
            two_recv.at[side, 2], at(sigma, core), inside(two, sigma),
        )

    locals_in[4].wait()
    locals_in[6].wait()
    locals_in[5].wait()
    arrived(kv_near.at[1 + other], sib_recv.at[0])
    arrived(q_two.at[theirs], sib_recv.at[2])
    for h in (0, 1):
        scores = dot_nt(q_two[:, columns[h]], own_of(0, h)) * scale + near_bias[:, OWN]
        attend(h, OWN, scores, lambda e: dot(e, own_of(1, h)))

    arrived(kv_near.at[3], near_recv.at[0], inside(1))
    arrived(kv_near.at[0], near_recv.at[1], inside(-1))
    for h in (0, 1):
        query = q_two[:, columns[h]]
        scores = jnp.concatenate(
            [dot_nt(query[first], kv_near[0, first, columns[h]]), dot_nt(query[second], kv_near[3, first, columns[h]])], axis=0
        )
        attend(
            h, SIDE, scores * scale + near_bias[:, SIDE],
            lambda e: jnp.concatenate(
                [dot(e[first], kv_near[0, second, columns[h]]), dot(e[second], kv_near[3, second, columns[h]])], axis=0
            ),
        )

    near_pools = [(dot(pool, kv_near[s, first]), dot(pool, kv_near[s, second])) for s in (0, 3)]
    for side in (0, 1):
        sigma = direction(side)
        arrived(one_in.at[side * 2, ones_only], one_recv.at[side * 2], inside(-2 * sigma))
        arrived(one_in.at[side * 2 + 1], one_recv.at[side * 2 + 1], inside(sigma))
    arrived(far_bias.at[other], sib_recv.at[4])
    nearest = [two_in[0, 1], one_in[1, 2 * ONE :], two_in[1, 1], one_in[3, 2 * ONE :]]
    nearest = [x.astype(F32) for x in nearest]
    for kind, middle in ((0, k_middle), (1, v_middle)):
        ones = slice(kind * ONE, (kind + 1) * ONE)
        rows = slice(kind * TWO, (kind + 1) * TWO)
        for s in range(4):
            middle[s * ONE : (s + 1) * ONE] = one_in[s, ones]
        middle[4 * ONE : 6 * ONE] = jnp.concatenate([p[kind][:ONE] for p in near_pools], axis=0).astype(BF16)
        parts = [x[rows] for x in nearest] + [p[kind][ONE:] for p in near_pools]
        parts += [two_in[side, 0].astype(F32)[rows] for side in (0, 1)]
        middle[6 * ONE :] = jnp.concatenate(parts, axis=0).astype(BF16)
    for h in (0, 1):
        scores = dot_nt(q_two[:, columns[h]], k_middle[:, columns[h]]) * scale + far_of(MIDDLE)
        attend(h, MIDDLE, scores, lambda e: dot(e, v_middle[:, columns[h]]))

    for side in (0, 1):
        sigma = direction(side)
        for s, steps in ((2, 3), (6, 5)):
            arrived(two_in.at[side, pl.ds(s, 2)], two_recv.at[side, s], inside(-steps * sigma))
        arrived(two_in.at[side, 8], two_recv.at[side, 8], inside(-6 * sigma))
    twos = [two_in[side, 2:].astype(F32) for side in (0, 1)]
    for kind, last in ((0, k_last), (1, v_last)):
        rows = slice(kind * TWO, (kind + 1) * TWO)
        parts = [t[:, rows].reshape(7 * TWO, HALF) for t in twos] + [jnp.zeros((2 * TWO, HALF), F32)]
        last[...] = jnp.concatenate(parts, axis=0).astype(BF16)
    for h in (0, 1):
        scores = dot_nt(q_two[:, columns[h]], k_last[:, columns[h]]) * scale + far_of(LAST)
        attend(h, LAST, scores, lambda e: dot(e, v_last[:, columns[h]]))
    inverse_totals = [1.0 / totals[h] for h in (0, 1)]
    for h in (0, 1):
        mixed[:, columns[h]] = accs[h] * inverse_totals[h]

    locals_in[7].wait()
    arrived(g_two.at[theirs], sib_recv.at[3])
    mates = 2 * heads
    place = lane * 2 + core
    value = mixed[...]
    energy = jnp.sum(value * value, axis=1, keepdims=True)
    product = jnp.sum(value * g_two[...].astype(F32), axis=1, keepdims=True)
    stats[place] = jnp.concatenate(
        [row_of(energy[:ROWS]), row_of(energy[ROWS:]), row_of(product[:ROWS]), row_of(product[ROWS:]), jnp.zeros((4, ROWS), F32)],
        axis=0,
    )
    for k in range(1, mates):
        to = (place + k) % mates
        send(stats.at[place], stats.at[place], stat_recv.at[place], {"seq": chip * 2 + to % 2, "head": to // 2})
    factors = [[], []]
    for h in (0, 1):
        for index, part in enumerate((OWN, SIDE, MIDDLE, LAST)):
            factors[h].append(jnp.exp2(highs[h][index] - highs[h][-1]) * inverse_totals[h])
            if part in (MIDDLE, LAST):
                turned[h, part, :] = weight[h, :, part].astype(BF16).T
    forward_sends = len(started)
    for k in range(1, mates):
        source = (place + k) % mates
        arrived(stats.at[source], stat_recv.at[source])
    summed = stats[0]
    for k in range(1, mates):
        summed = summed + stats[k]
    width = HEADS * HEAD_DIM
    deltas = [[], []]
    for b, rows in ((0, first), (1, second)):
        inverse = lax.rsqrt(column_of(summed[b : b + 1]) / width + NORM_EPSILON)
        agreement = column_of(summed[2 + b : 3 + b]) * inverse
        normed = mixed[rows] * inverse
        att[rows] = normed.astype(BF16)
        grad = inverse * (g_two[rows].astype(F32) - normed * (agreement / width))
        mixed_grad[rows] = grad
        both = grad.astype(BF16).astype(F32) * mixed[rows]
        for h in (0, 1):
            deltas[h].append(jnp.sum(both[:, columns[h]], axis=1, keepdims=True))
    deltas = [jnp.concatenate(deltas[h], axis=0) for h in (0, 1)]

    out_att = pltpu.make_async_copy(att.at[mine], att_hbm.at[:, half(core)], local_sem.at[8])
    out_att.start()
    send(att.at[theirs], att_hbm.at[:, half(core)], out_recv.at[0], sibling)

    unscale = 1.0 / math.sqrt(HEAD_DIM)
    query_grads = [None, None]

    def scaled(h, part):
        factor = factors[h][(OWN, SIDE, MIDDLE, LAST).index(part)]
        return (mixed_grad[:, columns[h]] * factor).astype(BF16), deltas[h] * factor

    def slopes_of(h, part, products, delta):
        return (weight[h, :, part] * (products - delta)).astype(BF16)

    def plain_backward(part, k_ref, v_ref):
        k_parts, v_parts = [], []
        for h in (0, 1):
            grad, delta = scaled(h, part)
            slopes = slopes_of(h, part, dot_nt(grad, v_ref(h)), delta)
            change = dot(slopes, k_ref(h))
            query_grads[h] = change if query_grads[h] is None else query_grads[h] + change
            k_parts.append(dot_tn(slopes, q_two[:, columns[h]]) * unscale)
            v_parts.append(dot(turned[h, part, :], grad))
        return jnp.concatenate(k_parts, axis=1), jnp.concatenate(v_parts, axis=1)

    def two_rows(pair, low):
        return jnp.concatenate([g[low : low + TWO] for g in pair], axis=0)

    last = plain_backward(LAST, lambda h: k_last[:, columns[h]], lambda h: v_last[:, columns[h]])
    for side in (0, 1):
        sigma = direction(side)
        for s in (1, 2, 5, 6, 7):
            two_out[side, s] = two_rows(last, (side * 7 + s - 1) * TWO).astype(BF16)
        send(
            two_out.at[side, pl.ds(5, 2)], pass_in.at[side, pl.ds(0, 2)],
            pass_recv.at[side, 0], at(-sigma, core), inside(-5 * sigma),
        )
        send(two_out.at[side, 7], pass_in.at[side, 4], pass_recv.at[side, 2], at(-2 * sigma, core), inside(-6 * sigma))
        send(
            two_out.at[side, pl.ds(1, 2)], pass_in.at[side, pl.ds(2, 2)],
            pass_recv.at[side, 1], at(-sigma, core), inside(-3 * sigma),
        )

    middle = plain_backward(MIDDLE, lambda h: k_middle[:, columns[h]], lambda h: v_middle[:, columns[h]])
    for s in range(4):
        for kind in (0, 1):
            pool_out[s, kind * ONE : (kind + 1) * ONE] = middle[kind][s * ONE : (s + 1) * ONE].astype(BF16)
    for b in (0, 1):
        s = 2 * b + 1
        pool_out[s, 2 * ONE :] = two_rows(middle, 6 * ONE + s * TWO).astype(BF16)
        send(pool_out.at[s], one_back.at[core, 1], back_one_recv.at[core, 1], at(direction(b), b), inside(direction(b)))
    for side in (0, 1):
        sigma = direction(side)
        send(
            pool_out.at[2 * side, ones_only], one_back.at[core, 0, ones_only],
            back_one_recv.at[core, 0], at(-2 * sigma, side), inside(-2 * sigma),
        )

    spread = spread_matrix()
    k_sides, v_sides = [[], []], [[], []]
    for h in (0, 1):
        grad, delta = scaled(h, SIDE)
        query = q_two[:, columns[h]]
        products = jnp.concatenate(
            [dot_nt(grad[first], kv_near[0, second, columns[h]]), dot_nt(grad[second], kv_near[3, second, columns[h]])], axis=0
        )
        slopes = slopes_of(h, SIDE, products, delta)
        query_grads[h] = query_grads[h] + jnp.concatenate(
            [dot(slopes[first], kv_near[0, first, columns[h]]), dot(slopes[second], kv_near[3, first, columns[h]])], axis=0
        )
        for b, rows in ((0, second), (1, first)):
            k_sides[b].append(dot_tn(slopes[rows], query[rows]) * unscale)
            v_sides[b].append(dot(turned[h, SIDE, rows], grad[rows]))
    for side in (0, 1):
        sigma = direction(side)
        four, two = -4 * sigma, -2 * sigma
        arrived(pass_in.at[side, pl.ds(0, 2)], pass_recv.at[side, 0], inside(sigma, four))
        arrived(pass_in.at[side, 4], pass_recv.at[side, 2], inside(2 * sigma, four))
        arrived(pass_in.at[side, pl.ds(2, 2)], pass_recv.at[side, 1], inside(sigma, two))
        passed = pass_in[side].astype(F32)
        two_out[side, 3] = (two_rows(last, (side * 7 + 2) * TWO) + passed[0]).astype(BF16)
        two_out[side, 4] = (two_rows(last, (side * 7 + 3) * TWO) + passed[1] + passed[4]).astype(BF16)
        two_out[side, 0] = (two_rows(middle, 6 * ONE + (6 + side) * TWO) + passed[2]).astype(BF16)
        two_out[side, 8] = (two_rows(middle, 6 * ONE + 2 * side * TWO) + passed[3]).astype(BF16)
        for s, spot, owner, steps in ((3, 2, 1 - side, four), (4, 3, side, four), (0, 0, 1 - side, two), (8, 1, side, two)):
            send(
                two_out.at[side, s], two_back.at[core, spot],
                back_two_recv.at[core, spot], at(steps, owner), inside(steps),
            )

    for b in (0, 1):
        p = 5 - b
        for kind, sides in ((0, k_sides), (1, v_sides)):
            pools = middle[kind]
            small = jnp.concatenate(
                [pools[p * ONE : (p + 1) * ONE], pools[6 * ONE + p * TWO : 6 * ONE + (p + 1) * TWO]], axis=0
            )
            near_out[b, kind * ROWS : (kind + 1) * ROWS] = (
                jnp.concatenate(sides[b], axis=1) + dot(spread, small.astype(BF16))
            ).astype(BF16)
        send(near_out.at[b], near_back.at[core], back_near_recv.at[core], at(-direction(b), b), inside(-direction(b)))

    flush(keep=len(started) - forward_sends)
    own = plain_backward(OWN, lambda h: own_of(0, h), lambda h: own_of(1, h))
    for kind in (0, 1):
        sib_out[kind * ROWS : (kind + 1) * ROWS] = jnp.where(core == 0, own[kind][second], own[kind][first]).astype(BF16)
    send(sib_out, sib_back, out_recv.at[1], sibling)
    for h in (0, 1):
        dq[:, columns[h]] = (query_grads[h] * unscale).astype(BF16)
    out_dq = pltpu.make_async_copy(dq.at[mine], dq_hbm.at[:, half(core)], local_sem.at[9])
    out_dq.start()
    send(dq.at[theirs], dq_hbm.at[:, half(core)], out_recv.at[2], sibling)

    flush(keep=4)
    outs = [out_att, out_dq]

    def finish(h, sem, rest):
        arrived(one_back.at[h, 0, ones_only], back_one_recv.at[h, 0], inside(sided=(2,)))
        arrived(one_back.at[h, 1], back_one_recv.at[h, 1], inside(sided=(-1,)))
        arrived(near_back.at[h], back_near_recv.at[h], inside(sided=(1,)))
        for j, steps in enumerate((-2, 2, -4, 4)):
            arrived(two_back.at[h, j], back_two_recv.at[h, j], inside(sided=(steps,)))
        ones = one_back[h, 1].astype(F32)
        twos = ones[2 * ONE :]
        for j in range(4):
            twos = twos + two_back[h, j].astype(F32)
        ones = ones[: 2 * ONE] + one_back[h, 0, : 2 * ONE].astype(F32)
        sums = []
        for kind, rows in ((0, first), (1, second)):
            small = jnp.concatenate([ones[kind * ONE : (kind + 1) * ONE], twos[kind * TWO : (kind + 1) * TWO]], axis=0)
            sums.append(near_back[h, rows].astype(F32) + dot(spread, small.astype(BF16)))
        rest = rest()
        for kind, out, out_hbm in ((0, dk, dk_hbm), (1, dv, dv_hbm)):
            out[:, half(h)] = (sums[kind] + rest[kind]).astype(BF16)
            outs.append(pltpu.make_async_copy(out.at[:, half(h)], out_hbm.at[:, half(h)], local_sem.at[sem + kind]))
            outs[-1].start()

    def from_sibling():
        arrived(sib_back, out_recv.at[1])
        return [sib_back[rows].astype(F32) for rows in (first, second)]

    finish(core, 10, lambda: [jnp.where(core == 0, own[kind][first], own[kind][second]) for kind in (0, 1)])
    finish(other, 12, from_sibling)
    arrived(att_hbm.at[:, half(other)], out_recv.at[0])
    arrived(dq_hbm.at[:, half(other)], out_recv.at[2])
    flush()
    for copy in outs:
        copy.wait()


def write_out(*refs):
    *arrays, sems = refs
    copies = [pltpu.make_async_copy(arrays[i], arrays[4 + i], sems.at[i]) for i in range(4)]
    for copy in copies:
        copy.start()
    for copy in copies:
        copy.wait()


def body(queries, keys, values, out_grad, level_choice, frame_lengths):
    rows, width = queries.shape
    vmem = pltpu.VMEM
    dma = pltpu.SemaphoreType.DMA
    out = jax.ShapeDtypeStruct((rows, width), BF16)
    limit = 40 * 1024 * 1024
    arrays = (queries, keys, values, out_grad, level_choice, frame_lengths.reshape(1, -1))
    results = pl.pallas_call(
        kernel,
        out_shape=(out, out, out, out),
        in_specs=[pl.BlockSpec(memory_space=pl.ANY)] * 6,
        out_specs=(pl.BlockSpec(memory_space=pl.ANY),) * 4,
        scratch_shapes=[
            vmem((2 * ROWS, width), BF16),
            vmem((2 * ROWS, HALF), BF16),
            vmem((2 * ROWS, HALF), BF16),
            vmem((4, 2 * ROWS, HALF), BF16),
            vmem((POOLED, width), BF16),
            vmem((4, POOLED, HALF), BF16),
            vmem((2, 9, 2 * TWO, HALF), BF16),
            vmem((256, HALF), BF16),
            vmem((256, HALF), BF16),
            vmem((128, HALF), BF16),
            vmem((128, HALF), BF16),
            pltpu.SMEM((1, 4), jnp.int32),
            vmem((1, 64), jnp.int32),
            vmem((2 * ROWS, 384), F32),
            vmem((2, 8, FAR), F32),
            vmem((2, 2 * ROWS, 768), F32),
            vmem((2, 768, 2 * ROWS), BF16),
            vmem((2 * ROWS, HALF), F32),
            vmem((8, 8, ROWS), F32),
            vmem((2 * ROWS, HALF), F32),
            vmem((2 * ROWS, HALF), BF16),
            vmem((2 * ROWS, HALF), BF16),
            vmem((2, 2 * ROWS, HALF), BF16),
            vmem((4, POOLED, HALF), BF16),
            vmem((2, 9, 2 * TWO, HALF), BF16),
            vmem((2 * ROWS, HALF), BF16),
            vmem((2, 5, 2 * TWO, HALF), BF16),
            vmem((2, 2 * ROWS, HALF), BF16),
            vmem((2, 2, POOLED, HALF), BF16),
            vmem((2, 4, 2 * TWO, HALF), BF16),
            vmem((2 * ROWS, HALF), BF16),
            vmem((ROWS, width), BF16),
            vmem((ROWS, width), BF16),
            dma((14,)),
            dma((64,)),
            dma((5,)),
            dma((2,)),
            dma((4,)),
            dma((2, 9)),
            dma((8,)),
            dma((2, 3)),
            dma((2,)),
            dma((2, 2)),
            dma((2, 4)),
            dma((3,)),
        ],
        compiler_params=pltpu.CompilerParams(collective_id=0, has_side_effects=True, vmem_limit_bytes=limit),
        cost_estimate=pl.CostEstimate(flops=700_000_000, bytes_accessed=1_100_000, transcendentals=400_000),
    )(*[pltpu.with_memory_space_constraint(array, pltpu.HBM) for array in arrays])
    return pl.pallas_call(
        write_out,
        out_shape=(out, out, out, out),
        in_specs=[pl.BlockSpec(memory_space=pl.ANY)] * 4,
        out_specs=(pl.BlockSpec(memory_space=pl.ANY),) * 4,
        scratch_shapes=[dma((4,))],
        compiler_params=pltpu.CompilerParams(vmem_limit_bytes=limit),
        cost_estimate=pl.CostEstimate(flops=0, bytes_accessed=1_100_000, transcendentals=0),
    )(*results)


def solution(mesh):
    in_specs = (
        P("seq", "head"),
        P("seq", "head"),
        P("seq", "head"),
        P("seq", "head"),
        P("seq", None),
        P(),
    )
    out_specs = (P("seq", "head"), P("seq", "head"), P("seq", "head"), P("seq", "head"))
    return jax.shard_map(body, mesh=mesh, in_specs=in_specs, out_specs=out_specs, check_vma=False)
```
